32 devices in a mesh: idx: 16 (over z, y, x), enc: 2 (over core).
Axes of the slice: x: 2, y: 2, z: 4, core: 2. Of those that a mesh axis runs over, the one named last changes fastest.
Arguments:
- queries: bfloat16 [65536, 1024], P(('idx', 'enc')), may hold values from -12 to 12
- positives: bfloat16 [65536, 1024], P(('idx', 'enc')), may hold values from -6 to 6
- passages: bfloat16 [32768, 1024], P('idx'), may hold values from -12 to 12
- negatives: int32 [32, 2048], P(('idx', 'enc')), may hold values from -1 to 32767, as said below
Outputs:
- query_loss: float32 [65536], P(('idx', 'enc'))
- grad_queries: bfloat16 [65536, 1024], P(('idx', 'enc'))
- grad_passages: bfloat16 [32768, 1024], P('idx')
The draws below stay inside these ranges and needn't reach their ends.
Inputs may be any that keep to these rules, and one draw needn't show every extreme that they name: `negatives`: -1 marks a padding slot. Of the 2048 slots of one device (its 1 row), at most 128 name passages of one index shard (ids 2048 * k to 2048 * k + 2047), and in every draw some shard is named exactly 128 times by every device.
All inputs are finite; a program needn't handle non-finite values.
Results may differ from the reference program's by a relative error of at most 0.0055.
Values may be sent and summed in bfloat16 or wider, within the bound.
No kernel may reach another device: no remote copies, remote signals or barrier semaphores. Data moves between devices by JAX's collectives and lax.ppermute only.
A program may use at most 128 MiB of HBM per device.

```python
import math
import jax
import jax.numpy as jnp
from jax import lax

D = 1024
GQ = 2048
ROWS_SHARD = 2048
LSCALE = 32
NEG = 2048
LIST_DEV = 2048
CAP = 128
TRAINERS = 32
GROUPS = 32
QTOT = 65536
PASSAGES = 32768
N_IDX = 16


def draw_queries(key, part):
    key = jax.random.fold_in(key, 11)
    values = jax.random.truncated_normal(key, -6.0, 6.0, (QTOT, D), jnp.float32)
    return values.astype(jnp.bfloat16)


def draw_passages(key, part):
    key = jax.random.fold_in(key, 23)
    values = jax.random.truncated_normal(key, -6.0, 6.0, (PASSAGES, D), jnp.float32)
    return values.astype(jnp.bfloat16)


def draw_negatives(key, part):
    key = jax.random.fold_in(key, 37)
    key_hot, key_first, key_count, key_row, key_perm = jax.random.split(key, 5)
    owners = jnp.arange(N_IDX, dtype=jnp.int32)
    first_hot = jax.random.randint(key_first, (), 0, N_IDX, dtype=jnp.int32)
    hot_owner = (jax.random.randint(key_hot, (N_IDX,), 0, 4, dtype=jnp.int32) == 0) | (owners == first_hot)
    light = jax.random.randint(key_count, (TRAINERS, N_IDX), CAP // 4, CAP // 2 + 1, dtype=jnp.int32)
    counts = jnp.where(hot_owner[None, :], CAP, light)
    bounds = jnp.cumsum(counts, axis=1)
    slot_index = jnp.arange(LIST_DEV, dtype=jnp.int32)
    owner_of = jnp.sum((slot_index[None, :, None] >= bounds[:, None, :]).astype(jnp.int32), axis=2)
    is_live = owner_of < N_IDX
    local_row = jax.random.randint(key_row, (TRAINERS, LIST_DEV), 0, ROWS_SHARD, dtype=jnp.int32)
    slot_ids = jnp.where(is_live, owner_of * ROWS_SHARD + local_row, -1)
    perm_keys = jax.random.split(key_perm, TRAINERS)
    shuffled = jax.vmap(lambda one_key, one_row: jax.random.permutation(one_key, one_row))(perm_keys, slot_ids)
    return shuffled.reshape(GROUPS, NEG).astype(jnp.int32)


def level_of(own_key, dims, cuts, low, high):
    def one(axis_at, shards_of):
        heights = jax.random.uniform(jax.random.fold_in(jax.random.fold_in(own_key, 6), axis_at), (shards_of,), jnp.float32, low / len(cuts), high / len(cuts))
        return jnp.repeat(jnp.exp(heights), dims[axis_at] // shards_of).reshape((-1,) + (1,) * (len(dims) - axis_at - 1))

    factor_of = one(*cuts[0])
    for cut in cuts[1:]:
        factor_of = factor_of * one(*cut)
    return factor_of


def gaussian(own_key, dims, width, most, cuts=(), held_as=jnp.bfloat16):
    loudness = level_of(own_key, dims, cuts, -0.22, 0.18) if cuts else 1.0
    values = jax.random.normal(own_key, dims, jnp.float32) * width * loudness
    return jnp.minimum(jnp.maximum(values, -most), most).astype(held_as)


def setup_inputs(seed: int = 0) -> dict:
    streams_of = jax.random.split(jax.random.key(seed), 5)
    queries = draw_queries(jax.random.fold_in(streams_of[4], 71), 0)
    positives = gaussian(streams_of[1], (QTOT, D), 1.0, 6.0, ((0, 32),))
    passages = draw_passages(jax.random.fold_in(streams_of[4], 71), 0)
    negatives = draw_negatives(jax.random.fold_in(streams_of[4], 71), 0)
    return {"queries": queries, "positives": positives, "passages": passages, "negatives": negatives}


masked_value = -1e+30

def group_terms(query_block, positive_block, neg_rows, is_live, loss_scale):
    feature_dim = query_block.shape[1]
    logit_scale = 3.0 / math.sqrt(feature_dim)
    pos_logit = logit_scale * lax.optimization_barrier(jnp.sum(query_block.astype(jnp.float32) * positive_block.astype(jnp.float32), axis=1))
    neg_logit = logit_scale * lax.dot_general(query_block, neg_rows, (((1,), (1,)), ((), ())), preferred_element_type=jnp.float32)
    masked = jnp.where(is_live[None, :], neg_logit, masked_value)
    top_logit = jnp.maximum(lax.optimization_barrier(jnp.max(masked, axis=1)), pos_logit)
    neg_exp = jnp.where(is_live[None, :], jnp.exp(masked - top_logit[:, None]), 0.0)
    pos_exp = jnp.exp(pos_logit - top_logit)
    norm_total = pos_exp + lax.optimization_barrier(jnp.sum(neg_exp, axis=1))
    query_loss = top_logit + jnp.log(norm_total) - pos_logit
    factor = loss_scale * logit_scale
    weights = (factor * neg_exp / norm_total[:, None]).astype(jnp.bfloat16)
    grad_query = jnp.dot(weights, neg_rows, preferred_element_type=jnp.float32)
    grad_query = grad_query + (factor * (pos_exp / norm_total - 1.0))[:, None] * positive_block.astype(jnp.float32)
    row_grad = lax.dot_general(weights, query_block, (((0,), (0,)), ((), ())), preferred_element_type=jnp.float32).astype(jnp.bfloat16)
    return (query_loss, grad_query.astype(jnp.bfloat16), row_grad)

def reference(queries, positives, passages, negatives):
    feature_dim = queries.shape[1]
    group_count = negatives.shape[0]
    query_groups = queries.reshape(group_count, GQ, feature_dim)
    positive_groups = positives.reshape(group_count, GQ, feature_dim)

    def one_group(grad_sum, group_inputs):
        query_block, positive_block, group_ids = group_inputs
        is_live = group_ids >= 0
        neg_rows = jnp.take(passages, jnp.maximum(group_ids, 0).astype(jnp.int32), axis=0)
        query_loss, grad_query, row_grad = group_terms(query_block, positive_block, neg_rows, is_live, LSCALE)
        target = jnp.where(is_live, group_ids, PASSAGES).astype(jnp.int32)
        grad_sum = grad_sum.at[target].add(row_grad.astype(jnp.float32), mode='drop')
        return (grad_sum, (query_loss, grad_query))
    grad_sum, (losses, grads) = lax.scan(one_group, jnp.zeros((PASSAGES, feature_dim), jnp.float32), (query_groups, positive_groups, negatives))
    return (losses.reshape(QTOT), grads.reshape(QTOT, feature_dim), grad_sum.astype(jnp.bfloat16))
```

```python
import functools
import math

import jax
import jax.numpy as jnp
from jax import lax
from jax.experimental import pallas as pl
from jax.experimental.pallas import tpu as pltpu
from jax.sharding import PartitionSpec as P

LSCALE = 32
DEAD = -1e30
LANES = 128
MIB = 1 << 20
FETCH_CHUNKS = 4
RETURN_CHUNKS = 4


def params(vmem_mib):
    return pltpu.CompilerParams(vmem_limit_bytes=vmem_mib * MIB)


def cost(flops, bytes_accessed, transcendentals=0):
    return pl.CostEstimate(
        flops=int(flops), bytes_accessed=int(bytes_accessed), transcendentals=int(transcendentals)
    )


def whole(shape):
    return pl.BlockSpec(shape, lambda *_: (0,) * len(shape))


def request_kernel(shard_rows, ids_ref, out_ref):
    shards, capacity = out_ref.shape
    count = ids_ref.shape[1]
    ids = ids_ref[...]
    base = lax.broadcasted_iota(jnp.int32, (shards, 1), 0) * shard_rows
    row = ids - base
    mine = (row >= 0) & (row < shard_rows)
    one = jnp.where(mine, 1.0, 0.0)
    high = jnp.where(mine, row // 128, 0).astype(jnp.float32)
    low = jnp.where(mine, row % 128, 0).astype(jnp.float32)
    before = (
        lax.broadcasted_iota(jnp.int32, (LANES, LANES), 0)
        < lax.broadcasted_iota(jnp.int32, (LANES, LANES), 1)
    ).astype(jnp.bfloat16)
    carry = jnp.zeros((shards, 1), jnp.float32)
    places = []
    for start in range(0, count, LANES):
        part = one[:, start : start + LANES]
        inside = jnp.dot(part.astype(jnp.bfloat16), before, preferred_element_type=jnp.float32)
        rank = jnp.sum(part * (inside + carry), axis=0, keepdims=True)
        carry = carry + jnp.sum(part, axis=1, keepdims=True)
        slot = lax.broadcasted_iota(jnp.int32, (capacity, LANES), 0).astype(jnp.float32)
        places.append(jnp.where(slot == rank, 1.0, 0.0))
    place = jnp.concatenate(places, axis=1).astype(jnp.bfloat16)
    parts = jnp.concatenate([one, high, low], axis=0).astype(jnp.bfloat16)
    packed = lax.dot_general(
        parts, place, (((1,), (1,)), ((), ())), preferred_element_type=jnp.float32
    )
    filled = packed[:shards] > 0.5
    rows = packed[shards : 2 * shards] * 128.0 + packed[2 * shards :]
    out_ref[...] = jnp.where(filled, rows.astype(jnp.int32), -1)


def build_request(ids, shards, shard_rows):
    count = ids.shape[1]
    capacity = count // shards
    return pl.pallas_call(
        functools.partial(request_kernel, shard_rows),
        out_shape=jax.ShapeDtypeStruct((shards, capacity), jnp.int32),
        compiler_params=params(16),
        cost_estimate=cost(2 * 3 * shards * count * capacity, 16384),
        name="build_request",
    )(ids)


def as_columns(table, first, size):
    parts, capacity = table.shape
    blocks = []
    for part in range(parts):
        line = jnp.broadcast_to(table[part : part + 1, :], (LANES, capacity))
        blocks.append(line.T[first : first + size])
    return jnp.concatenate(blocks, axis=0)


def pick_kernel(first, wanted_ref, passages_ref, out_ref):
    parts, size, width = out_ref.shape
    rows = passages_ref.shape[0]
    wanted = as_columns(wanted_ref[...].astype(jnp.float32), first, size)
    lane = lax.broadcasted_iota(jnp.int32, wanted.shape, 1)
    hot = jnp.concatenate(
        [
            jnp.where(wanted == (lane + start).astype(jnp.float32), 1.0, 0.0).astype(jnp.bfloat16)
            for start in range(0, rows, LANES)
        ],
        axis=1,
    )
    picked = jnp.dot(hot, passages_ref[...], preferred_element_type=jnp.float32)
    out_ref[...] = picked.astype(jnp.bfloat16).reshape(parts, size, width)


def pick(wanted, passages, chunk, chunks):
    shards, capacity = wanted.shape
    rows, width = passages.shape
    size = capacity // chunks
    parts = max(8, 256 // size)
    return pl.pallas_call(
        functools.partial(pick_kernel, chunk * size),
        out_shape=jax.ShapeDtypeStruct((shards, size, width), jnp.bfloat16),
        grid=(shards // parts,),
        in_specs=[
            pl.BlockSpec((parts, capacity), lambda t: (t, 0)),
            whole((rows, width)),
        ],
        out_specs=pl.BlockSpec((parts, size, width), lambda t: (t, 0, 0)),
        compiler_params=params(32),
        cost_estimate=cost(2 * shards * size * rows * width, 2 * rows * width),
        name="pick_rows",
    )(wanted, passages)


def masked_logits(first, size, scale, request, fetched, queries):
    live = as_columns(request.astype(jnp.float32), first, size) >= 0.0
    logits = scale * lax.dot_general(
        fetched, queries, (((1,), (1,)), ((), ())), preferred_element_type=jnp.float32
    )
    lanes = logits.shape[1]
    return jnp.concatenate(
        [
            jnp.where(live, logits[:, start : start + LANES], DEAD)
            for start in range(0, lanes, LANES)
        ],
        axis=1,
    )


def logits_kernel(first, size, scale, request_ref, fetched_ref, queries_ref, out_ref):
    out_ref[...] = masked_logits(
        first, size, scale, request_ref[...], fetched_ref[...], queries_ref[...]
    )


def chunk_logits(request, fetched, queries, chunk, chunks, scale):
    shards, capacity = request.shape
    slots, width = fetched.shape
    count = queries.shape[0]
    tile = min(256, count)
    size = capacity // chunks
    return pl.pallas_call(
        functools.partial(logits_kernel, chunk * size, size, scale),
        out_shape=jax.ShapeDtypeStruct((slots, count), jnp.float32),
        grid=(count // tile,),
        in_specs=[
            whole((shards, capacity)),
            whole((slots, width)),
            pl.BlockSpec((tile, width), lambda t: (t, 0)),
        ],
        out_specs=pl.BlockSpec((slots, tile), lambda t: (0, t)),
        compiler_params=params(32),
        cost_estimate=cost(
            2 * slots * width * count, 2 * (slots + count) * width + 4 * slots * count
        ),
        name="chunk_logits",
    )(request, fetched, queries)


def weights_kernel(chunks, size, scale, *refs):
    request_ref, pos_ref, fetched_ref, queries_ref, first_ref = refs[:5]
    earlier_refs = refs[5 : 4 + chunks]
    weights_ref, loss_ref, coef_ref, grad_ref, total_ref = refs[4 + chunks :]
    step = pl.program_id(0)
    slots = fetched_ref.shape[0]
    factor = LSCALE * scale
    last = masked_logits(
        (chunks - 1) * size, size, scale, request_ref[...], fetched_ref[...], queries_ref[...]
    )
    pos = pos_ref[...]
    top = jnp.maximum(jnp.max(last, axis=0, keepdims=True), pos)
    for ref in earlier_refs:
        top = jnp.maximum(top, jnp.max(ref[...], axis=0, keepdims=True))
    pos_exp = jnp.exp(pos - top)
    total = pos_exp
    exps = []
    for ref in earlier_refs:
        exps.append(jnp.exp(ref[...] - top))
    exps.append(jnp.exp(last - top))
    for value in exps:
        total = total + jnp.sum(value, axis=0, keepdims=True)
    loss_ref[...] = top + jnp.log(total) - pos
    coef_ref[...] = factor * (pos_exp / total - 1.0)
    share = factor / total

    @pl.when(step == 0)
    def _():
        total_ref[...] = jnp.zeros_like(total_ref)

    for chunk, value in enumerate(exps):
        weights = (value * share).astype(jnp.bfloat16)
        weights_ref[chunk * slots : (chunk + 1) * slots, :] = weights
        total_ref[chunk * slots : (chunk + 1) * slots, :] += jnp.dot(
            weights, first_ref[...], preferred_element_type=jnp.float32
        )

    @pl.when(step == pl.num_programs(0) - 1)
    def _():
        shards = grad_ref.shape[0]
        for chunk in range(chunks):
            part = total_ref[chunk * slots : (chunk + 1) * slots, :].astype(jnp.bfloat16)
            grad_ref[:, chunk] = part.reshape(shards, size, part.shape[1])


def softmax_weights(request, pos_logit, earlier, fetched, queries, scale, features):
    shards, capacity = request.shape
    slots, width = fetched.shape
    count = queries.shape[0]
    chunks = len(earlier) + 1
    size = capacity // chunks
    tile = min(256, count)
    line = pl.BlockSpec((1, tile), lambda t: (0, t))
    return pl.pallas_call(
        functools.partial(weights_kernel, chunks, size, scale),
        out_shape=(
            jax.ShapeDtypeStruct((chunks * slots, count), jnp.bfloat16),
            jax.ShapeDtypeStruct((1, count), jnp.float32),
            jax.ShapeDtypeStruct((1, count), jnp.float32),
            jax.ShapeDtypeStruct((shards, chunks, size, features), jnp.bfloat16),
        ),
        grid=(count // tile,),
        in_specs=[
            whole((shards, capacity)),
            line,
            whole((slots, width)),
            pl.BlockSpec((tile, width), lambda t: (t, 0)),
            pl.BlockSpec((tile, features), lambda t: (t, 0)),
        ]
        + [pl.BlockSpec((slots, tile), lambda t: (0, t))] * (chunks - 1),
        out_specs=(
            pl.BlockSpec((chunks * slots, tile), lambda t: (0, t)),
            line,
            line,
            whole((shards, chunks, size, features)),
        ),
        scratch_shapes=[pltpu.VMEM((chunks * slots, features), jnp.float32)],
        compiler_params=params(48),
        cost_estimate=cost(
            2 * slots * width * count + 2 * chunks * slots * count * features,
            6 * chunks * slots * count,
            chunks * slots * count,
        ),
        name="softmax_weights",
    )(request, pos_logit, fetched, queries, queries, *earlier)


def row_grad_kernel(weights_ref, queries_ref, out_ref):
    shards, _, size, features = out_ref.shape
    value = jnp.dot(weights_ref[...], queries_ref[...], preferred_element_type=jnp.float32)
    out_ref[...] = value.astype(jnp.bfloat16).reshape(shards, 1, size, features)


def row_grad(weights, queries, shards, chunks, features, index):
    slots, count = weights.shape
    size = slots // shards // chunks
    return pl.pallas_call(
        row_grad_kernel,
        out_shape=jax.ShapeDtypeStruct((shards, chunks, size, features), jnp.bfloat16),
        grid=(chunks,),
        in_specs=[
            pl.BlockSpec((slots // chunks, count), lambda t: (t, 0)),
            pl.BlockSpec((count, features), lambda t: (0, index)),
        ],
        out_specs=pl.BlockSpec((shards, 1, size, features), lambda t: (0, t, 0, 0)),
        compiler_params=params(32),
        cost_estimate=cost(2 * slots * count * features, 2 * (slots + features) * count),
        name="row_grad",
    )(weights, queries)


def scatter_kernel(wanted_ref, returned_ref, out_ref):
    rows = out_ref.shape[0]
    lines = wanted_ref.shape[0]
    row = pl.program_id(0) * rows + lax.broadcasted_iota(jnp.int32, (rows, LANES), 0)
    hot = jnp.concatenate(
        [
            jnp.where(wanted_ref[line : line + 1, :] == row, 1.0, 0.0).astype(jnp.bfloat16)
            for line in range(lines)
        ],
        axis=1,
    )
    out_ref[...] = jnp.dot(
        hot, returned_ref[...], preferred_element_type=jnp.float32
    ).astype(out_ref.dtype)


def scatter(wanted, returned, shard_rows):
    slots, features = returned.shape
    tile = min(256, shard_rows)
    return pl.pallas_call(
        scatter_kernel,
        out_shape=jax.ShapeDtypeStruct((shard_rows, features), jnp.bfloat16),
        grid=(shard_rows // tile,),
        in_specs=[whole(wanted.shape), whole((slots, features))],
        out_specs=pl.BlockSpec((tile, features), lambda t: (t, 0)),
        compiler_params=params(32),
        cost_estimate=cost(
            2 * shard_rows * slots * features, 2 * (slots + shard_rows) * features
        ),
        name="scatter_rows",
    )(wanted, returned)


def local(queries, positives, passages, negatives):
    shards = lax.axis_size("idx")
    shard_rows, width = passages.shape
    ids = negatives.reshape(1, -1)
    slots = ids.shape[1]
    capacity = slots // shards
    scale = 3.0 / math.sqrt(width)
    chunks = max(1, min(FETCH_CHUNKS, capacity // 16))
    size = capacity // chunks
    features = width // RETURN_CHUNKS

    request = build_request(ids, shards, shard_rows)
    wanted = lax.all_to_all(request, "idx", split_axis=0, concat_axis=0, tiled=True)
    pos_logit = scale * jnp.sum(
        queries.astype(jnp.float32) * positives.astype(jnp.float32), axis=1
    )

    fetched = []
    for chunk in range(chunks):
        picked = pick(wanted, passages, chunk, chunks)
        part = lax.all_to_all(picked, "idx", split_axis=0, concat_axis=0, tiled=True)
        fetched.append(part.reshape(shards * size, width))
    earlier = [
        chunk_logits(request, fetched[chunk], queries, chunk, chunks, scale)
        for chunk in range(chunks - 1)
    ]
    weights, loss, coef, first_grad = softmax_weights(
        request, pos_logit.reshape(1, -1), earlier, fetched[-1], queries, scale, features
    )

    lines = wanted.reshape(slots // LANES, LANES)
    sums = []
    for index in range(RETURN_CHUNKS):
        grad = (
            first_grad
            if index == 0
            else row_grad(weights, queries, shards, chunks, features, index)
        )
        returned = lax.all_to_all(
            grad.reshape(shards, capacity, features), "idx", split_axis=0, concat_axis=0, tiled=True
        )
        own = scatter(lines, returned.reshape(slots, features), shard_rows)
        other = lax.ppermute(own, "enc", [(0, 1), (1, 0)])
        sums.append((own.astype(jnp.float32) + other.astype(jnp.float32)).astype(jnp.bfloat16))
    grad_passages = jnp.concatenate(sums, axis=1)

    rows_by_slot = jnp.concatenate(fetched, axis=0)
    grad_queries = lax.dot_general(
        weights, rows_by_slot, (((0,), (0,)), ((), ())), preferred_element_type=jnp.float32
    )
    grad_queries = grad_queries + coef.reshape(-1, 1) * positives.astype(jnp.float32)
    return (loss.reshape(-1), grad_queries.astype(jnp.bfloat16), grad_passages)


def solution(mesh):
    placed = (
        P(("idx", "enc"), None),
        P(("idx", "enc"), None),
        P("idx", None),
        P(("idx", "enc"), None),
    )
    return jax.shard_map(
        local,
        mesh=mesh,
        in_specs=placed,
        out_specs=(P(("idx", "enc")), P(("idx", "enc"), None), P("idx", None)),
        check_vma=False,
    )
```

```python
import functools
import math

import jax
import jax.numpy as jnp
from jax import lax
from jax.experimental import pallas as pl
from jax.experimental.pallas import tpu as pltpu
from jax.sharding import PartitionSpec as P

LSCALE = 32
DEAD = -1e30
LANES = 128
MIB = 1 << 20
GROUP_SLOTS = 256
WINDOW = 4
SWAP = [(0, 1), (1, 0)]


def params(vmem_mib):
    return pltpu.CompilerParams(vmem_limit_bytes=vmem_mib * MIB)


def cost(flops, bytes_accessed, transcendentals=0):
    return pl.CostEstimate(
        flops=int(flops), bytes_accessed=int(bytes_accessed), transcendentals=int(transcendentals)
    )


def whole(shape):
    return pl.BlockSpec(shape, lambda *_: (0,) * len(shape))


SCALAR = pl.BlockSpec(memory_space=pltpu.SMEM)
UNREAD = pl.BlockSpec(memory_space=pl.ANY)


def request_kernel(shard_rows, ids_ref, out_ref):
    shards, capacity = out_ref.shape
    count = ids_ref.shape[1]
    ids = ids_ref[...]
    base = lax.broadcasted_iota(jnp.int32, (shards, 1), 0) * shard_rows
    row = ids - base
    mine = (row >= 0) & (row < shard_rows)
    one = jnp.where(mine, 1.0, 0.0)
    high = jnp.where(mine, row // 128, 0).astype(jnp.float32)
    low = jnp.where(mine, row % 128, 0).astype(jnp.float32)
    before = (
        lax.broadcasted_iota(jnp.int32, (LANES, LANES), 0)
        < lax.broadcasted_iota(jnp.int32, (LANES, LANES), 1)
    ).astype(jnp.bfloat16)
    carry = jnp.zeros((shards, 1), jnp.float32)
    places = []
    for start in range(0, count, LANES):
        part = one[:, start : start + LANES]
        inside = jnp.dot(part.astype(jnp.bfloat16), before, preferred_element_type=jnp.float32)
        rank = jnp.sum(part * (inside + carry), axis=0, keepdims=True)
        carry = carry + jnp.sum(part, axis=1, keepdims=True)
        slot = lax.broadcasted_iota(jnp.int32, (capacity, LANES), 0).astype(jnp.float32)
        places.append(jnp.where(slot == rank, 1.0, 0.0))
    place = jnp.concatenate(places, axis=1).astype(jnp.bfloat16)
    parts = jnp.concatenate([one, high, low], axis=0).astype(jnp.bfloat16)
    packed = lax.dot_general(
        parts, place, (((1,), (1,)), ((), ())), preferred_element_type=jnp.float32
    )
    filled = packed[:shards] > 0.5
    rows = packed[shards : 2 * shards] * 128.0 + packed[2 * shards :]
    out_ref[...] = jnp.where(filled, rows.astype(jnp.int32), -1)


def build_request(ids, shards, shard_rows):
    count = ids.shape[1]
    capacity = count // shards
    return pl.pallas_call(
        functools.partial(request_kernel, shard_rows),
        out_shape=jax.ShapeDtypeStruct((shards, capacity), jnp.int32),
        compiler_params=params(16),
        cost_estimate=cost(2 * 3 * shards * count * capacity, 16384),
        name="build_request",
    )(ids)


def as_columns(lines):
    blocks = []
    for line in lines:
        for start in range(0, line.shape[1], LANES):
            piece = line[:, start : start + LANES]
            blocks.append(jnp.broadcast_to(piece, (LANES, piece.shape[1])).T)
    return jnp.concatenate(blocks, axis=0)


def partner_line(table_ref, me, offset):
    return table_ref[pl.ds(jnp.bitwise_xor(me, offset), 1), :]


def pick_kernel(offsets, me_ref, wanted_ref, passages_ref, *refs):
    out_refs = refs[-len(offsets) :]
    rows = passages_ref.shape[0]
    me = me_ref[0]
    wanted = as_columns([partner_line(wanted_ref, me, o).astype(jnp.float32) for o in offsets])
    lane = lax.broadcasted_iota(jnp.int32, wanted.shape, 1)
    hot = jnp.concatenate(
        [
            jnp.where(wanted == (lane + start).astype(jnp.float32), 1.0, 0.0).astype(jnp.bfloat16)
            for start in range(0, rows, LANES)
        ],
        axis=1,
    )
    picked = jnp.dot(hot, passages_ref[...], preferred_element_type=jnp.float32)
    picked = picked.astype(jnp.bfloat16)
    size = out_refs[0].shape[0]
    for place, ref in enumerate(out_refs):
        ref[...] = picked[place * size : (place + 1) * size]


def pick(me, wanted, passages, offsets, after):
    shards, capacity = wanted.shape
    rows, width = passages.shape
    block = jax.ShapeDtypeStruct((capacity, width), jnp.bfloat16)
    return pl.pallas_call(
        functools.partial(pick_kernel, offsets),
        out_shape=[block] * len(offsets),
        in_specs=[SCALAR, whole(wanted.shape), whole(passages.shape)] + [UNREAD] * len(after),
        out_specs=[whole(block.shape)] * len(offsets),
        grid=(1,),
        compiler_params=params(32),
        cost_estimate=cost(
            2 * len(offsets) * capacity * rows * width,
            2 * (rows + len(offsets) * capacity) * width,
        ),
        name="pick_rows",
    )(me, wanted, passages, *after)


def logits_kernel(offsets, scale, me_ref, request_ref, top_ref, total_ref, queries_ref, *refs):
    fetched_refs = refs[: len(offsets)]
    exps_ref, new_top_ref, new_total_ref = refs[len(offsets) :]
    me = me_ref[0]
    request = [partner_line(request_ref, me, o).astype(jnp.float32) for o in offsets]
    live = as_columns(request) >= 0.0
    fetched = jnp.concatenate([ref[...] for ref in fetched_refs], axis=0)
    logits = lax.dot_general(
        fetched, queries_ref[...], (((1,), (1,)), ((), ())), preferred_element_type=jnp.float32
    )
    for start in range(0, logits.shape[1], LANES):
        lanes = slice(start, start + LANES)
        part = jnp.where(live, scale * logits[:, lanes], DEAD)
        old_top = top_ref[:, lanes]
        top = jnp.maximum(old_top, jnp.max(part, axis=0, keepdims=True))
        exps = jnp.exp(part - top)
        exps_ref[:, lanes] = exps
        new_top_ref[:, lanes] = top
        new_total_ref[:, lanes] = total_ref[:, lanes] * jnp.exp(old_top - top) + jnp.sum(
            exps, axis=0, keepdims=True
        )


def group_logits(me, request, top, total, queries, fetched, offsets, scale):
    capacity, width = fetched[0].shape
    slots = capacity * len(offsets)
    count = queries.shape[0]
    tile = min(512, count)
    line = pl.BlockSpec((1, tile), lambda t: (0, t))
    shape = jax.ShapeDtypeStruct((1, count), jnp.float32)
    return pl.pallas_call(
        functools.partial(logits_kernel, offsets, scale),
        out_shape=(jax.ShapeDtypeStruct((slots, count), jnp.float32), shape, shape),
        grid=(count // tile,),
        in_specs=[
            SCALAR,
            whole(request.shape),
            line,
            line,
            pl.BlockSpec((tile, width), lambda t: (t, 0)),
        ]
        + [whole(fetched[0].shape)] * len(offsets),
        out_specs=(pl.BlockSpec((slots, tile), lambda t: (0, t)), line, line),
        compiler_params=params(32),
        cost_estimate=cost(
            2 * slots * width * count,
            2 * (slots + count) * width + 4 * slots * count,
            slots * count,
        ),
        name="group_logits",
    )(me, request, top, total, queries, *fetched)


def row_grad_kernel(factor, after, exps_ref, own_top_ref, top_ref, total_ref, queries_ref, *refs):
    weights_ref, *out_refs, sum_ref = refs[after:]
    share = factor * jnp.exp(own_top_ref[...] - top_ref[...]) / total_ref[...]
    weights = (exps_ref[...] * share).astype(jnp.bfloat16)
    weights_ref[...] = weights
    value = jnp.dot(weights, queries_ref[...], preferred_element_type=jnp.float32)
    step = pl.program_id(0)

    @pl.when(step == 0)
    def _():
        sum_ref[...] = value

    @pl.when(step > 0)
    def _():
        sum_ref[...] += value

    @pl.when(step == pl.num_programs(0) - 1)
    def _():
        size = out_refs[0].shape[0]
        for place, ref in enumerate(out_refs):
            ref[...] = sum_ref[place * size : (place + 1) * size].astype(jnp.bfloat16)


def row_grad(exps, own_top, top, total, queries, parts, factor, after):
    slots, count = exps.shape
    width = queries.shape[1]
    tile = min(512, count)
    line = pl.BlockSpec((1, tile), lambda t: (0, t))
    column = pl.BlockSpec((slots, tile), lambda t: (0, t))
    block = jax.ShapeDtypeStruct((slots // parts, width), jnp.bfloat16)
    weights, *grads = pl.pallas_call(
        functools.partial(row_grad_kernel, factor, len(after)),
        out_shape=[jax.ShapeDtypeStruct((slots, count), jnp.bfloat16)] + [block] * parts,
        grid=(count // tile,),
        in_specs=[column, line, line, line, pl.BlockSpec((tile, width), lambda t: (t, 0))]
        + [UNREAD] * len(after),
        out_specs=[column] + [whole(block.shape)] * parts,
        scratch_shapes=[pltpu.VMEM((slots, width), jnp.float32)],
        compiler_params=params(32),
        cost_estimate=cost(
            2 * slots * width * count, 2 * (slots + count) * width + 6 * slots * count
        ),
        name="row_grad",
    )(exps, own_top, top, total, queries, *after)
    return weights, grads


def query_kernel(factor, groups, pos_ref, top_ref, total_ref, positives_ref, *refs):
    weights_refs = refs[:groups]
    fetched_refs = refs[groups:-2]
    grad_ref, loss_ref = refs[-2:]
    per = len(fetched_refs) // groups
    pos, top, total = pos_ref[...], top_ref[...], total_ref[...]
    loss_ref[...] = top + jnp.log(total) - pos
    coef = as_columns([factor * (jnp.exp(pos - top) / total - 1.0)])
    value = jnp.concatenate(
        [
            coef * positives_ref[:, start : start + LANES].astype(jnp.float32)
            for start in range(0, positives_ref.shape[1], LANES)
        ],
        axis=1,
    )
    for group, ref in enumerate(weights_refs):
        rows = jnp.concatenate(
            [one[...] for one in fetched_refs[group * per : (group + 1) * per]], axis=0
        )
        value = value + lax.dot_general(
            ref[...], rows, (((0,), (0,)), ((), ())), preferred_element_type=jnp.float32
        )
    grad_ref[...] = value.astype(jnp.bfloat16)


def query_grad(pos, top, total, positives, weights, fetched, factor):
    count, width = positives.shape
    tile = min(256, count)
    line = pl.BlockSpec((1, tile), lambda t: (0, t))
    slots = weights[0].shape[0]
    return pl.pallas_call(
        functools.partial(query_kernel, factor, len(weights)),
        out_shape=(
            jax.ShapeDtypeStruct((count, width), jnp.bfloat16),
            jax.ShapeDtypeStruct((1, count), jnp.float32),
        ),
        grid=(count // tile,),
        in_specs=[line, line, line, pl.BlockSpec((tile, width), lambda t: (t, 0))]
        + [pl.BlockSpec((slots, tile), lambda t: (0, t))] * len(weights)
        + [whole(fetched[0].shape)] * len(fetched),
        out_specs=(pl.BlockSpec((tile, width), lambda t: (t, 0)), line),
        compiler_params=params(40),
        cost_estimate=cost(
            2 * len(weights) * slots * width * count,
            2 * len(weights) * slots * (width + count) + 4 * count * width,
        ),
        name="query_grad",
    )(pos, top, total, positives, *weights, *fetched)


def scatter_kernel(offsets, first, me_ref, own_ref, other_ref, *refs):
    count = len(offsets)
    own_refs, other_refs = refs[:count], refs[count : 2 * count]
    out_ref = refs[-1]
    rows = out_ref.shape[0]
    me = me_ref[0]
    row = pl.program_id(0) * rows + lax.broadcasted_iota(jnp.int32, (rows, 1), 0)

    def added(table_ref, value_refs):
        hot = jnp.concatenate(
            [
                jnp.where(partner_line(table_ref, me, o) == row, 1.0, 0.0).astype(jnp.bfloat16)
                for o in offsets
            ],
            axis=1,
        )
        values = jnp.concatenate([ref[...] for ref in value_refs], axis=0)
        return jnp.dot(hot, values, preferred_element_type=jnp.float32)

    value = added(own_ref, own_refs) + added(other_ref, other_refs)
    if not first:
        value = refs[2 * count][...] + value
    out_ref[...] = value.astype(out_ref.dtype)


def scatter(me, wanted, other_wanted, own, other, offsets, sums, shard_rows, dtype):
    capacity, width = own[0].shape
    tile = min(256, shard_rows)
    block = pl.BlockSpec((tile, width), lambda t: (t, 0))
    extra = [] if sums is None else [sums]
    return pl.pallas_call(
        functools.partial(scatter_kernel, offsets, sums is None),
        out_shape=jax.ShapeDtypeStruct((shard_rows, width), dtype),
        grid=(shard_rows // tile,),
        in_specs=[SCALAR, whole(wanted.shape), whole(wanted.shape)]
        + [whole(own[0].shape)] * (2 * len(offsets))
        + [block] * len(extra),
        out_specs=block,
        compiler_params=params(32),
        cost_estimate=cost(
            4 * shard_rows * len(offsets) * capacity * width,
            4 * len(offsets) * capacity * width + 8 * shard_rows * width,
        ),
        name="scatter_rows",
    )(me, wanted, other_wanted, *own, *other, *extra)


def partner_groups(shards, per):
    half = shards // 2
    quarter = max(1, half // 2)
    far = [half + part * quarter + place for place in range(quarter) for part in range(half // quarter)]
    near = list(range(quarter, half)) + list(range(1, quarter)) + [0]
    far = [far[i : i + per] for i in range(0, half, per)]
    near = [near[i : i + per] for i in range(0, half, per)]
    order = [near[-1]]
    for place, group in enumerate(far):
        order.append(group)
        if place < len(near) - 1:
            order.append(near[place])
    if len(far) == len(near):
        order[-1], order[-2] = order[-1], order[-2]
    return [tuple(group) for group in order]


def exchange(value, offset, shards):
    if offset == 0:
        return value
    return lax.ppermute(value, "idx", [(i, i ^ offset) for i in range(shards)])


def local(queries, positives, passages, negatives):
    shards = lax.axis_size("idx")
    shard_rows, width = passages.shape
    ids = negatives.reshape(1, -1)
    slots = ids.shape[1]
    capacity = slots // shards
    scale = 3.0 / math.sqrt(width)
    factor = LSCALE * scale
    per = max(1, min(shards // 2, GROUP_SLOTS // capacity))
    groups = partner_groups(shards, per)
    me = lax.axis_index("idx").astype(jnp.int32).reshape(1)

    request = build_request(ids, shards, shard_rows)
    wanted = lax.all_to_all(request, "idx", split_axis=0, concat_axis=0, tiled=True)
    other_wanted = lax.ppermute(wanted, "enc", SWAP)
    pos_logit = scale * jnp.sum(
        queries.astype(jnp.float32) * positives.astype(jnp.float32), axis=1
    )
    pos_logit = pos_logit.reshape(1, -1)

    fetched = []
    for place, offsets in enumerate(groups):
        after = fetched[place - WINDOW][-1:] if place >= WINDOW else []
        picked = pick(me, wanted, passages, offsets, after)
        fetched.append([exchange(v, o, shards) for v, o in zip(picked, offsets)])

    top, total = pos_logit, jnp.ones_like(pos_logit)
    exps, tops = [], []
    for offsets, rows in zip(groups, fetched):
        value, top, total = group_logits(me, request, top, total, queries, rows, offsets, scale)
        exps.append(value)
        tops.append(top)

    order = list(range(1, len(groups)))
    order.insert(1, 0)
    weights = [None] * len(groups)
    returned = []
    sums = None
    for step, place in enumerate(order):
        offsets = groups[place]
        after = returned[step - WINDOW][-1:] if step >= WINDOW else []
        weights[place], grads = row_grad(
            exps[place], tops[place], top, total, queries, len(offsets), factor, after
        )
        returned.append([exchange(v, o, shards) for v, o in zip(grads, offsets)])
    for step, place in enumerate(order):
        own = returned[step]
        other = [lax.ppermute(v, "enc", SWAP) for v in own]
        final = step == len(order) - 1
        sums = scatter(
            me,
            wanted,
            other_wanted,
            own,
            other,
            groups[place],
            sums,
            shard_rows,
            jnp.bfloat16 if final else jnp.float32,
        )

    rows = [value for group in fetched for value in group]
    grad_queries, loss = query_grad(pos_logit, top, total, positives, weights, rows, factor)
    return (loss.reshape(-1), grad_queries, sums)


def solution(mesh):
    placed = (
        P(("idx", "enc"), None),
        P(("idx", "enc"), None),
        P("idx", None),
        P(("idx", "enc"), None),
    )
    return jax.shard_map(
        local,
        mesh=mesh,
        in_specs=placed,
        out_specs=(P(("idx", "enc")), P(("idx", "enc"), None), P("idx", None)),
        check_vma=False,
    )
```

```python
import functools
import math

import jax
import jax.numpy as jnp
from jax import lax
from jax.experimental import pallas as pl
from jax.experimental.pallas import tpu as pltpu
from jax.sharding import PartitionSpec as P

LSCALE = 32
DEAD = -1e30
LANES = 128
MIB = 1 << 20
GROUP_SLOTS = 256
SHARE = 0.01
FAR_FLIGHT = 2
NEAR_FLIGHT = 3
SWAP = [(0, 1), (1, 0)]


def params(vmem_mib):
    return pltpu.CompilerParams(vmem_limit_bytes=vmem_mib * MIB)


def cost(flops, bytes_accessed, transcendentals=0):
    return pl.CostEstimate(
        flops=int(flops * SHARE), bytes_accessed=int(bytes_accessed * SHARE), transcendentals=0
    )


def whole(shape):
    return pl.BlockSpec(shape, lambda *_: (0,) * len(shape))


SCALAR = pl.BlockSpec(memory_space=pltpu.SMEM)
UNREAD = pl.BlockSpec(memory_space=pl.ANY)


def request_kernel(shard_rows, ids_ref, out_ref):
    shards, capacity = out_ref.shape
    count = ids_ref.shape[1]
    ids = ids_ref[...]
    base = lax.broadcasted_iota(jnp.int32, (shards, 1), 0) * shard_rows
    row = ids - base
    mine = (row >= 0) & (row < shard_rows)
    one = jnp.where(mine, 1.0, 0.0)
    high = jnp.where(mine, row // 128, 0).astype(jnp.float32)
    low = jnp.where(mine, row % 128, 0).astype(jnp.float32)
    before = (
        lax.broadcasted_iota(jnp.int32, (LANES, LANES), 0)
        < lax.broadcasted_iota(jnp.int32, (LANES, LANES), 1)
    ).astype(jnp.bfloat16)
    carry = jnp.zeros((shards, 1), jnp.float32)
    places = []
    for start in range(0, count, LANES):
        part = one[:, start : start + LANES]
        inside = jnp.dot(part.astype(jnp.bfloat16), before, preferred_element_type=jnp.float32)
        rank = jnp.sum(part * (inside + carry), axis=0, keepdims=True)
        carry = carry + jnp.sum(part, axis=1, keepdims=True)
        slot = lax.broadcasted_iota(jnp.int32, (capacity, LANES), 0).astype(jnp.float32)
        places.append(jnp.where(slot == rank, 1.0, 0.0))
    place = jnp.concatenate(places, axis=1).astype(jnp.bfloat16)
    parts = jnp.concatenate([one, high, low], axis=0).astype(jnp.bfloat16)
    packed = lax.dot_general(
        parts, place, (((1,), (1,)), ((), ())), preferred_element_type=jnp.float32
    )
    filled = packed[:shards] > 0.5
    rows = packed[shards : 2 * shards] * 128.0 + packed[2 * shards :]
    out_ref[...] = jnp.where(filled, rows.astype(jnp.int32), -1)


def build_request(ids, shards, shard_rows):
    count = ids.shape[1]
    capacity = count // shards
    return pl.pallas_call(
        functools.partial(request_kernel, shard_rows),
        out_shape=jax.ShapeDtypeStruct((shards, capacity), jnp.int32),
        compiler_params=params(16),
        cost_estimate=cost(2 * 3 * shards * count * capacity, 16384),
        name="build_request",
    )(ids)


def as_columns(lines):
    blocks = []
    for line in lines:
        for start in range(0, line.shape[1], LANES):
            piece = line[:, start : start + LANES]
            blocks.append(jnp.broadcast_to(piece, (LANES, piece.shape[1])).T)
    return jnp.concatenate(blocks, axis=0)


def partner_line(table_ref, me, offset):
    return table_ref[pl.ds(jnp.bitwise_xor(me, offset), 1), :]


def pick_kernel(offsets, me_ref, wanted_ref, passages_ref, *refs):
    out_refs = refs[-len(offsets) :]
    rows = passages_ref.shape[0]
    me = me_ref[0]
    wanted = as_columns([partner_line(wanted_ref, me, o).astype(jnp.float32) for o in offsets])
    lane = lax.broadcasted_iota(jnp.int32, wanted.shape, 1)
    hot = jnp.concatenate(
        [
            jnp.where(wanted == (lane + start).astype(jnp.float32), 1.0, 0.0).astype(jnp.bfloat16)
            for start in range(0, rows, LANES)
        ],
        axis=1,
    )
    picked = jnp.dot(hot, passages_ref[...], preferred_element_type=jnp.float32)
    picked = picked.astype(jnp.bfloat16)
    size = out_refs[0].shape[0]
    for place, ref in enumerate(out_refs):
        ref[...] = picked[place * size : (place + 1) * size]


def pick(me, wanted, passages, offsets, after):
    shards, capacity = wanted.shape
    rows, width = passages.shape
    block = jax.ShapeDtypeStruct((capacity, width), jnp.bfloat16)
    return pl.pallas_call(
        functools.partial(pick_kernel, offsets),
        out_shape=[block] * len(offsets),
        in_specs=[SCALAR, whole(wanted.shape), whole(passages.shape)] + [UNREAD] * len(after),
        out_specs=[whole(block.shape)] * len(offsets),
        grid=(1,),
        compiler_params=params(32),
        cost_estimate=cost(
            2 * len(offsets) * capacity * rows * width,
            2 * (rows + len(offsets) * capacity) * width,
        ),
        name="pick_rows",
    )(me, wanted, passages, *after)


def logits_kernel(offsets, scale, me_ref, request_ref, top_ref, total_ref, queries_ref, *refs):
    fetched_refs = refs[: len(offsets)]
    exps_ref, new_top_ref, new_total_ref = refs[len(offsets) :]
    me = me_ref[0]
    request = [partner_line(request_ref, me, o).astype(jnp.float32) for o in offsets]
    live = as_columns(request) >= 0.0
    fetched = jnp.concatenate([ref[...] for ref in fetched_refs], axis=0)
    logits = lax.dot_general(
        fetched, queries_ref[...], (((1,), (1,)), ((), ())), preferred_element_type=jnp.float32
    )
    for start in range(0, logits.shape[1], LANES):
        lanes = slice(start, start + LANES)
        part = jnp.where(live, scale * logits[:, lanes], DEAD)
        old_top = top_ref[:, lanes]
        top = jnp.maximum(old_top, jnp.max(part, axis=0, keepdims=True))
        exps = jnp.exp(part - top)
        exps_ref[:, lanes] = exps
        new_top_ref[:, lanes] = top
        new_total_ref[:, lanes] = total_ref[:, lanes] * jnp.exp(old_top - top) + jnp.sum(
            exps, axis=0, keepdims=True
        )


def group_logits(me, request, top, total, queries, fetched, offsets, scale):
    capacity, width = fetched[0].shape
    slots = capacity * len(offsets)
    count = queries.shape[0]
    tile = min(512, count)
    line = pl.BlockSpec((1, tile), lambda t: (0, t))
    shape = jax.ShapeDtypeStruct((1, count), jnp.float32)
    return pl.pallas_call(
        functools.partial(logits_kernel, offsets, scale),
        out_shape=(jax.ShapeDtypeStruct((slots, count), jnp.float32), shape, shape),
        grid=(count // tile,),
        in_specs=[
            SCALAR,
            whole(request.shape),
            line,
            line,
            pl.BlockSpec((tile, width), lambda t: (t, 0)),
        ]
        + [whole(fetched[0].shape)] * len(offsets),
        out_specs=(pl.BlockSpec((slots, tile), lambda t: (0, t)), line, line),
        compiler_params=params(32),
        cost_estimate=cost(
            2 * slots * width * count,
            2 * (slots + count) * width + 4 * slots * count,
            slots * count,
        ),
        name="group_logits",
    )(me, request, top, total, queries, *fetched)


def row_grad_kernel(factor, after, exps_ref, own_top_ref, top_ref, total_ref, queries_ref, *refs):
    weights_ref, *out_refs, sum_ref = refs[after:]
    share = factor * jnp.exp(own_top_ref[...] - top_ref[...]) / total_ref[...]
    weights = (exps_ref[...] * share).astype(jnp.bfloat16)
    weights_ref[...] = weights
    value = jnp.dot(weights, queries_ref[...], preferred_element_type=jnp.float32)
    step = pl.program_id(0)

    @pl.when(step == 0)
    def _():
        sum_ref[...] = value

    @pl.when(step > 0)
    def _():
        sum_ref[...] += value

    @pl.when(step == pl.num_programs(0) - 1)
    def _():
        size = out_refs[0].shape[0]
        for place, ref in enumerate(out_refs):
            ref[...] = sum_ref[place * size : (place + 1) * size].astype(jnp.bfloat16)


def row_grad(exps, own_top, top, total, queries, parts, factor, after):
    slots, count = exps.shape
    width = queries.shape[1]
    tile = min(512, count)
    line = pl.BlockSpec((1, tile), lambda t: (0, t))
    column = pl.BlockSpec((slots, tile), lambda t: (0, t))
    block = jax.ShapeDtypeStruct((slots // parts, width), jnp.bfloat16)
    weights, *grads = pl.pallas_call(
        functools.partial(row_grad_kernel, factor, len(after)),
        out_shape=[jax.ShapeDtypeStruct((slots, count), jnp.bfloat16)] + [block] * parts,
        grid=(count // tile,),
        in_specs=[column, line, line, line, pl.BlockSpec((tile, width), lambda t: (t, 0))]
        + [UNREAD] * len(after),
        out_specs=[column] + [whole(block.shape)] * parts,
        scratch_shapes=[pltpu.VMEM((slots, width), jnp.float32)],
        compiler_params=params(32),
        cost_estimate=cost(
            2 * slots * width * count, 2 * (slots + count) * width + 6 * slots * count
        ),
        name="row_grad",
    )(exps, own_top, top, total, queries, *after)
    return weights, grads


def query_kernel(factor, groups, pos_ref, top_ref, total_ref, positives_ref, *refs):
    weights_refs = refs[:groups]
    fetched_refs = refs[groups:-2]
    grad_ref, loss_ref = refs[-2:]
    per = len(fetched_refs) // groups
    pos, top, total = pos_ref[...], top_ref[...], total_ref[...]
    loss_ref[...] = top + jnp.log(total) - pos
    coef = as_columns([factor * (jnp.exp(pos - top) / total - 1.0)])
    value = jnp.concatenate(
        [
            coef * positives_ref[:, start : start + LANES].astype(jnp.float32)
            for start in range(0, positives_ref.shape[1], LANES)
        ],
        axis=1,
    )
    for group, ref in enumerate(weights_refs):
        rows = jnp.concatenate(
            [one[...] for one in fetched_refs[group * per : (group + 1) * per]], axis=0
        )
        value = value + lax.dot_general(
            ref[...], rows, (((0,), (0,)), ((), ())), preferred_element_type=jnp.float32
        )
    grad_ref[...] = value.astype(jnp.bfloat16)


def query_grad(pos, top, total, positives, weights, fetched, factor):
    count, width = positives.shape
    tile = min(256, count)
    line = pl.BlockSpec((1, tile), lambda t: (0, t))
    slots = weights[0].shape[0]
    return pl.pallas_call(
        functools.partial(query_kernel, factor, len(weights)),
        out_shape=(
            jax.ShapeDtypeStruct((count, width), jnp.bfloat16),
            jax.ShapeDtypeStruct((1, count), jnp.float32),
        ),
        grid=(count // tile,),
        in_specs=[line, line, line, pl.BlockSpec((tile, width), lambda t: (t, 0))]
        + [pl.BlockSpec((slots, tile), lambda t: (0, t))] * len(weights)
        + [whole(fetched[0].shape)] * len(fetched),
        out_specs=(pl.BlockSpec((tile, width), lambda t: (t, 0)), line),
        compiler_params=params(40),
        cost_estimate=cost(
            2 * len(weights) * slots * width * count,
            2 * len(weights) * slots * (width + count) + 4 * count * width,
        ),
        name="query_grad",
    )(pos, top, total, positives, *weights, *fetched)


def scatter_kernel(offsets, both, bases, place_ref, own_ref, other_ref, *refs):
    count = len(offsets)
    base_refs, value_refs, out_ref = refs[:bases], refs[bases:-1], refs[-1]
    rows = out_ref.shape[0]
    me = place_ref[0]
    row = pl.program_id(0) * rows + lax.broadcasted_iota(jnp.int32, (rows, 1), 0)
    lines = [partner_line(own_ref, me, o) for o in offsets]
    values = [ref[...] for ref in value_refs[:count]]
    if both:
        lead = place_ref[1] == 0
        other_lines = [partner_line(other_ref, me, o) for o in offsets]
        other_values = [ref[...] for ref in value_refs[count:]]
        pairs = [
            (jnp.concatenate(x, axis=axis), jnp.concatenate(y, axis=axis))
            for x, y, axis in ((lines, other_lines, 1), (values, other_values, 0))
        ]
        (line, other_line), (value, other_value) = pairs
        lines = [jnp.where(lead, line, other_line), jnp.where(lead, other_line, line)]
        values = [jnp.where(lead, value, other_value), jnp.where(lead, other_value, value)]
    hot = jnp.concatenate(
        [jnp.where(line == row, 1.0, 0.0).astype(jnp.bfloat16) for line in lines], axis=1
    )
    total = jnp.dot(hot, jnp.concatenate(values, axis=0), preferred_element_type=jnp.float32)
    if bases:
        base = base_refs[0][...]
        for ref in base_refs[1:]:
            base = base + ref[...]
        total = base + total
    out_ref[...] = total.astype(out_ref.dtype)


def scatter(place, wanted, other_wanted, own, other, offsets, bases, shard_rows, dtype):
    capacity, width = own[0].shape
    tile = min(256, shard_rows)
    block = pl.BlockSpec((tile, width), lambda t: (t, 0))
    values = [*own, *other]
    return pl.pallas_call(
        functools.partial(scatter_kernel, offsets, bool(other), len(bases)),
        out_shape=jax.ShapeDtypeStruct((shard_rows, width), dtype),
        grid=(shard_rows // tile,),
        in_specs=[SCALAR, whole(wanted.shape), whole(wanted.shape)]
        + [block] * len(bases)
        + [whole(own[0].shape)] * len(values),
        out_specs=block,
        compiler_params=params(32),
        cost_estimate=cost(
            2 * shard_rows * len(values) * capacity * width,
            2 * len(values) * capacity * width + 4 * (1 + len(bases)) * shard_rows * width,
        ),
        name="scatter_rows",
    )(place, wanted, other_wanted, *bases, *values)


def stage_kernel(rows_ref, out_ref):
    out_ref[...] = rows_ref[...]


def stage(passages):
    rows, width = passages.shape
    block = pl.BlockSpec((min(512, rows), width), lambda t: (t, 0))
    return pl.pallas_call(
        stage_kernel,
        out_shape=jax.ShapeDtypeStruct(passages.shape, passages.dtype),
        grid=(rows // block.block_shape[0],),
        in_specs=[block],
        out_specs=block,
        compiler_params=params(16),
        cost_estimate=cost(0, 4 * rows * width),
        name="stage_rows",
    )(passages)


def partners(shards):
    half = shards // 2
    quarter = max(1, half // 2)
    far = [half + part * quarter + place for place in range(quarter) for part in range(half // quarter)]
    near = list(range(quarter, half)) + list(range(1, quarter)) + [0]
    return far, near


def in_groups(offsets, per):
    return [tuple(offsets[i : i + per]) for i in range(0, len(offsets), per)]


def behind(value, earlier):
    if not earlier:
        return value
    return lax.optimization_barrier((value, *earlier))[0]


def exchange_chain(values, offsets, flight, shards, extra):
    received = {}
    for place, offset in enumerate(offsets):
        value = values[offset]
        if offset == 0:
            received[offset] = value
            continue
        earlier = [received[offsets[place - flight]]] if place >= flight else []
        if place in extra:
            earlier = earlier + extra[place](received)
        value = behind(value, earlier)
        received[offset] = lax.ppermute(value, "idx", [(i, i ^ offset) for i in range(shards)])
    return received


def local(queries, positives, passages, negatives):
    shards = lax.axis_size("idx")
    shard_rows, width = passages.shape
    ids = negatives.reshape(1, -1)
    slots = ids.shape[1]
    capacity = slots // shards
    scale = 3.0 / math.sqrt(width)
    factor = LSCALE * scale
    per = max(1, min(shards // 8, GROUP_SLOTS // capacity))
    far, near = partners(shards)
    far_groups, near_groups = in_groups(far, per), in_groups(near, per)
    me = lax.axis_index("idx").astype(jnp.int32)
    place = jnp.stack([me, lax.axis_index("enc").astype(jnp.int32)])

    request = build_request(ids, shards, shard_rows)
    wanted = lax.all_to_all(request, "idx", split_axis=0, concat_axis=0, tiled=True)
    other_wanted = lax.ppermute(wanted, "enc", SWAP)
    staged = stage(passages)
    pos_logit = scale * jnp.sum(
        queries.astype(jnp.float32) * positives.astype(jnp.float32), axis=1
    )
    pos_logit = pos_logit.reshape(1, -1)

    ahead = (FAR_FLIGHT + per - 1) // per
    picks = far_groups[:ahead] + near_groups[:1] + far_groups[ahead:] + near_groups[1:]
    picked, last = {}, []
    for group in picks:
        values = pick(behind(place, last), wanted, staged, group, [])
        picked.update(zip(group, values))
        last = values[-1:]
    fetched = exchange_chain(picked, near, NEAR_FLIGHT, shards, {})
    fetched.update(exchange_chain(picked, far, FAR_FLIGHT, shards, {}))

    top, total = pos_logit, jnp.ones_like(pos_logit)
    groups = [group for pair in zip(near_groups, far_groups) for group in pair]
    exps, tops = {}, {}
    for group in groups:
        rows = [fetched[o] for o in group]
        exps[group], top, total = group_logits(
            place, request, top, total, queries, rows, group, scale
        )
        tops[group] = top

    weights, grads, last = {}, {}, []
    for group in picks:
        weights[group], values = row_grad(
            exps[group],
            behind(tops[group], last),
            top,
            total,
            queries,
            len(group),
            factor,
            [],
        )
        grads.update(zip(group, values))
        last = values[-1:]
    grad_queries, loss = query_grad(
        pos_logit,
        top,
        total,
        positives,
        [weights[group] for group in groups],
        [fetched[o] for group in groups for o in group],
        factor,
    )

    def scattered(returned, offsets, bases, both, dtype=jnp.float32):
        own = [returned[o] for o in offsets]
        if both:
            own[0] = behind(own[0], bases[:1] if len(bases) == 1 else [])
        other = [lax.ppermute(v, "enc", SWAP) for v in own] if both else []
        return scatter(
            place, wanted, other_wanted, own, other, offsets, bases, shard_rows, dtype
        )

    split = len(far_groups) // 2
    early = [group for pair in zip(near_groups, far_groups[:split]) for group in pair]
    early += near_groups[split:]
    late = far_groups[split:]
    half = len(late[-1]) // 2
    late = late[:-1] + [late[-1][:half], late[-1][half:]]
    sums = []
    near_returned = exchange_chain(
        grads, near, NEAR_FLIGHT, shards, {len(near) - 2: lambda _: [grad_queries]}
    )

    def early_sums(far_returned):
        returned = {**near_returned, **far_returned}
        for one, two in zip(early[::2], early[1::2]):
            if two == early[-1]:
                sums[0] = behind(sums[0], [far_returned[o] for o in late[0]])
            sums[:] = [scattered(returned, one + two, sums, False)]
        return list(sums)

    far_returned = exchange_chain(
        grads, far, FAR_FLIGHT, shards, {len(far) - 1: early_sums}
    )
    sums = sums + [lax.ppermute(sums[0], "enc", SWAP)]
    for group in late[:-1]:
        sums = [scattered(far_returned, group, sums, True)]
    grad_passages = scattered(far_returned, late[-1], sums, True, jnp.bfloat16)
    return (loss.reshape(-1), grad_queries, grad_passages)


def solution(mesh):
    placed = (
        P(("idx", "enc"), None),
        P(("idx", "enc"), None),
        P("idx", None),
        P(("idx", "enc"), None),
    )
    return jax.shard_map(
        local,
        mesh=mesh,
        in_specs=placed,
        out_specs=(P(("idx", "enc")), P(("idx", "enc"), None), P("idx", None)),
        check_vma=False,
    )
```

```python
import functools
import math

import jax
import jax.numpy as jnp
from jax import lax
from jax.experimental import pallas as pl
from jax.experimental.pallas import tpu as pltpu
from jax.sharding import PartitionSpec as P

LSCALE = 32
DEAD = -1e30
LANES = 128
MIB = 1 << 20
GROUP_SLOTS = 256
SHARE = 0.01
FETCH_FLIGHT = 5
RETURN_FLIGHT = 4
LAST_FLIGHT = 3
PICK_PARTS = 4
QUERY_TILE = 256
SWAP = [(0, 1), (1, 0)]


def params(vmem_mib):
    return pltpu.CompilerParams(vmem_limit_bytes=vmem_mib * MIB)


def cost(flops, bytes_accessed, transcendentals=0):
    return pl.CostEstimate(
        flops=int(flops * SHARE), bytes_accessed=int(bytes_accessed * SHARE), transcendentals=0
    )


def whole(shape):
    return pl.BlockSpec(shape, lambda *_: (0,) * len(shape))


SCALAR = pl.BlockSpec(memory_space=pltpu.SMEM)
IN_HBM = pl.BlockSpec(memory_space=pl.ANY)
IN_VMEM = pl.BlockSpec(memory_space=pltpu.VMEM)


def request_kernel(shard_rows, ids_ref, out_ref):
    shards, capacity = out_ref.shape
    count = ids_ref.shape[1]
    ids = ids_ref[...]
    base = lax.broadcasted_iota(jnp.int32, (shards, 1), 0) * shard_rows
    row = ids - base
    mine = (row >= 0) & (row < shard_rows)
    one = jnp.where(mine, 1.0, 0.0)
    high = jnp.where(mine, row // 128, 0).astype(jnp.float32)
    low = jnp.where(mine, row % 128, 0).astype(jnp.float32)
    before = (
        lax.broadcasted_iota(jnp.int32, (LANES, LANES), 0)
        < lax.broadcasted_iota(jnp.int32, (LANES, LANES), 1)
    ).astype(jnp.bfloat16)
    carry = jnp.zeros((shards, 1), jnp.float32)
    places = []
    for start in range(0, count, LANES):
        part = one[:, start : start + LANES]
        inside = jnp.dot(part.astype(jnp.bfloat16), before, preferred_element_type=jnp.float32)
        rank = jnp.sum(part * (inside + carry), axis=0, keepdims=True)
        carry = carry + jnp.sum(part, axis=1, keepdims=True)
        slot = lax.broadcasted_iota(jnp.int32, (capacity, LANES), 0).astype(jnp.float32)
        places.append(jnp.where(slot == rank, 1.0, 0.0))
    place = jnp.concatenate(places, axis=1).astype(jnp.bfloat16)
    parts = jnp.concatenate([one, high, low], axis=0).astype(jnp.bfloat16)
    packed = lax.dot_general(
        parts, place, (((1,), (1,)), ((), ())), preferred_element_type=jnp.float32
    )
    filled = packed[:shards] > 0.5
    rows = packed[shards : 2 * shards] * 128.0 + packed[2 * shards :]
    out_ref[...] = jnp.where(filled, rows.astype(jnp.int32), -1)


def build_request(ids, shards, shard_rows):
    count = ids.shape[1]
    capacity = count // shards
    return pl.pallas_call(
        functools.partial(request_kernel, shard_rows),
        out_shape=jax.ShapeDtypeStruct((shards, capacity), jnp.int32),
        compiler_params=params(16),
        cost_estimate=cost(2 * 3 * shards * count * capacity, 16384),
        name="build_request",
    )(ids)


def partner(position, offset, shards):
    shift, flip = offset
    return jnp.bitwise_xor(jnp.bitwise_and(position + shift, shards - 1), flip)


def inverse(offset, shards):
    return ((shards - offset[0]) % shards, offset[1])


def as_columns(lines):
    blocks = []
    for line in lines:
        for start in range(0, line.shape[1], LANES):
            piece = line[:, start : start + LANES]
            blocks.append(jnp.broadcast_to(piece, (LANES, piece.shape[1])).T)
    return jnp.concatenate(blocks, axis=0)


def partner_line(table_ref, me, offset):
    return table_ref[pl.ds(partner(me, offset, table_ref.shape[0]), 1), :]


def pick_kernel(offsets, place_ref, wanted_ref, passages_ref, *refs):
    *out_refs, rows_ref, arrived = refs
    rows = passages_ref.shape[0]
    part = rows // PICK_PARTS
    copies = []
    for index in range(PICK_PARTS):
        span = pl.ds(index * part, part)
        copies.append(
            pltpu.make_async_copy(passages_ref.at[span], rows_ref.at[span], arrived.at[index])
        )
        copies[-1].start()
    me = place_ref[0]
    wanted = as_columns([partner_line(wanted_ref, me, o).astype(jnp.float32) for o in offsets])
    lane = lax.broadcasted_iota(jnp.int32, wanted.shape, 1).astype(jnp.float32)
    picked = None
    for index in range(PICK_PARTS):
        first = index * part
        hot = jnp.concatenate(
            [
                jnp.where(wanted == lane + float(start), 1.0, 0.0).astype(jnp.bfloat16)
                for start in range(first, first + part, LANES)
            ],
            axis=1,
        )
        copies[index].wait()
        value = jnp.dot(
            hot, rows_ref[first : first + part, :], preferred_element_type=jnp.float32
        )
        picked = value if picked is None else picked + value
    picked = picked.astype(jnp.bfloat16)
    size = out_refs[0].shape[0]
    for index, ref in enumerate(out_refs):
        ref[...] = picked[index * size : (index + 1) * size]


def pick(place, wanted, passages, offsets):
    shards, capacity = wanted.shape
    rows, width = passages.shape
    block = jax.ShapeDtypeStruct((capacity, width), jnp.bfloat16)
    return pl.pallas_call(
        functools.partial(pick_kernel, offsets),
        out_shape=[block] * len(offsets),
        in_specs=[SCALAR, IN_VMEM, IN_HBM],
        out_specs=[IN_VMEM] * len(offsets),
        scratch_shapes=[
            pltpu.VMEM((rows, width), passages.dtype),
            pltpu.SemaphoreType.DMA((PICK_PARTS,)),
        ],
        compiler_params=params(16),
        cost_estimate=cost(
            2 * len(offsets) * capacity * rows * width,
            2 * (rows + len(offsets) * capacity) * width,
        ),
        name="pick_rows",
    )(place, wanted, passages)


def logits_kernel(offsets, scale, place_ref, request_ref, top_ref, total_ref, queries_ref, *refs):
    fetched_refs = refs[: len(offsets)]
    exps_ref, new_top_ref, new_total_ref = refs[len(offsets) :]
    me = place_ref[0]
    request = [partner_line(request_ref, me, o).astype(jnp.float32) for o in offsets]
    live = as_columns(request) >= 0.0
    fetched = jnp.concatenate([ref[...] for ref in fetched_refs], axis=0)
    for first in range(0, queries_ref.shape[0], QUERY_TILE):
        logits = lax.dot_general(
            fetched,
            queries_ref[first : first + QUERY_TILE, :],
            (((1,), (1,)), ((), ())),
            preferred_element_type=jnp.float32,
        )
        for start in range(0, QUERY_TILE, LANES):
            lanes = slice(first + start, first + start + LANES)
            part = jnp.where(live, scale * logits[:, start : start + LANES], DEAD)
            old_top = top_ref[:, lanes]
            top = jnp.maximum(old_top, jnp.max(part, axis=0, keepdims=True))
            exps = jnp.exp(part - top)
            exps_ref[:, lanes] = exps
            new_top_ref[:, lanes] = top
            new_total_ref[:, lanes] = total_ref[:, lanes] * jnp.exp(old_top - top) + jnp.sum(
                exps, axis=0, keepdims=True
            )


def group_logits(place, request, top, total, queries, fetched, offsets, scale):
    capacity, width = fetched[0].shape
    slots = capacity * len(offsets)
    count = queries.shape[0]
    shape = jax.ShapeDtypeStruct((1, count), jnp.float32)
    return pl.pallas_call(
        functools.partial(logits_kernel, offsets, scale),
        out_shape=(jax.ShapeDtypeStruct((slots, count), jnp.float32), shape, shape),
        in_specs=[SCALAR] + [IN_VMEM] * (4 + len(offsets)),
        out_specs=(IN_VMEM,) * 3,
        compiler_params=params(24),
        cost_estimate=cost(
            2 * slots * width * count,
            2 * (slots + count) * width + 4 * slots * count,
            slots * count,
        ),
        name="group_logits",
    )(place, request, top, total, queries, *fetched)


def row_grad_kernel(factor, exps_ref, own_top_ref, top_ref, total_ref, queries_ref, *refs):
    weights_ref, *out_refs = refs
    share = factor * jnp.exp(own_top_ref[...] - top_ref[...]) / total_ref[...]
    weights = (exps_ref[...] * share).astype(jnp.bfloat16)
    weights_ref[...] = weights
    value = jnp.dot(weights, queries_ref[...], preferred_element_type=jnp.float32)
    value = value.astype(jnp.bfloat16)
    size = out_refs[0].shape[0]
    for index, ref in enumerate(out_refs):
        ref[...] = value[index * size : (index + 1) * size]


def row_grad(exps, own_top, top, total, queries, parts, factor):
    slots, count = exps.shape
    width = queries.shape[1]
    block = jax.ShapeDtypeStruct((slots // parts, width), jnp.bfloat16)
    weights, *grads = pl.pallas_call(
        functools.partial(row_grad_kernel, factor),
        out_shape=[jax.ShapeDtypeStruct((slots, count), jnp.bfloat16)] + [block] * parts,
        in_specs=[IN_VMEM] * 5,
        out_specs=[IN_VMEM] * (1 + parts),
        compiler_params=params(24),
        cost_estimate=cost(
            2 * slots * width * count, 2 * (slots + count) * width + 6 * slots * count
        ),
        name="row_grad",
    )(exps, own_top, top, total, queries)
    return weights, grads


def query_kernel(factor, groups, pos_ref, top_ref, total_ref, positives_ref, *refs):
    weights_refs = refs[:groups]
    fetched_refs = refs[groups:-2]
    grad_ref, loss_ref = refs[-2:]
    per = len(fetched_refs) // groups
    pos, top, total = pos_ref[...], top_ref[...], total_ref[...]
    loss_ref[...] = top + jnp.log(total) - pos
    coef = as_columns([factor * (jnp.exp(pos - top) / total - 1.0)])
    value = jnp.concatenate(
        [
            coef * positives_ref[:, start : start + LANES].astype(jnp.float32)
            for start in range(0, positives_ref.shape[1], LANES)
        ],
        axis=1,
    )
    for group, ref in enumerate(weights_refs):
        rows = jnp.concatenate(
            [one[...] for one in fetched_refs[group * per : (group + 1) * per]], axis=0
        )
        value = value + lax.dot_general(
            ref[...], rows, (((0,), (0,)), ((), ())), preferred_element_type=jnp.float32
        )
    grad_ref[...] = value.astype(jnp.bfloat16)


def query_grad(pos, top, total, positives, weights, fetched, factor):
    count, width = positives.shape
    tile = min(256, count)
    line = pl.BlockSpec((1, tile), lambda t: (0, t))
    slots = weights[0].shape[0]
    return pl.pallas_call(
        functools.partial(query_kernel, factor, len(weights)),
        out_shape=(
            jax.ShapeDtypeStruct((count, width), jnp.bfloat16),
            jax.ShapeDtypeStruct((1, count), jnp.float32),
        ),
        grid=(count // tile,),
        in_specs=[line, line, line, pl.BlockSpec((tile, width), lambda t: (t, 0))]
        + [pl.BlockSpec((slots, tile), lambda t: (0, t))] * len(weights)
        + [whole(fetched[0].shape)] * len(fetched),
        out_specs=(pl.BlockSpec((tile, width), lambda t: (t, 0)), line),
        compiler_params=params(40),
        cost_estimate=cost(
            2 * len(weights) * slots * width * count,
            2 * len(weights) * slots * (width + count) + 4 * count * width,
        ),
        name="query_grad",
    )(pos, top, total, positives, *weights, *fetched)


def scatter_kernel(offsets, both, bases, place_ref, own_ref, other_ref, *refs):
    count = len(offsets)
    base_refs, value_refs, out_ref = refs[:bases], refs[bases:-1], refs[-1]
    rows = out_ref.shape[0]
    me = place_ref[0]
    row = pl.program_id(0) * rows + lax.broadcasted_iota(jnp.int32, (rows, 1), 0)
    lines = [partner_line(own_ref, me, o) for o in offsets]
    values = [ref[...] for ref in value_refs[:count]]
    if both:
        lead = place_ref[1] == 0
        other_lines = [partner_line(other_ref, me, o) for o in offsets]
        other_values = [ref[...] for ref in value_refs[count:]]
        pairs = [
            (jnp.concatenate(x, axis=axis), jnp.concatenate(y, axis=axis))
            for x, y, axis in ((lines, other_lines, 1), (values, other_values, 0))
        ]
        (line, other_line), (value, other_value) = pairs
        lines = [jnp.where(lead, line, other_line), jnp.where(lead, other_line, line)]
        values = [jnp.where(lead, value, other_value), jnp.where(lead, other_value, value)]
    hot = jnp.concatenate(
        [jnp.where(line == row, 1.0, 0.0).astype(jnp.bfloat16) for line in lines], axis=1
    )
    total = jnp.dot(hot, jnp.concatenate(values, axis=0), preferred_element_type=jnp.float32)
    if bases:
        base = base_refs[0][...]
        for ref in base_refs[1:]:
            base = base + ref[...]
        total = base + total
    out_ref[...] = total.astype(out_ref.dtype)


def scatter(place, wanted, other_wanted, own, other, offsets, bases, shard_rows, dtype):
    capacity, width = own[0].shape
    tile = min(256, shard_rows)
    block = pl.BlockSpec((tile, width), lambda t: (t, 0))
    values = [*own, *other]
    return pl.pallas_call(
        functools.partial(scatter_kernel, offsets, bool(other), len(bases)),
        out_shape=jax.ShapeDtypeStruct((shard_rows, width), dtype),
        grid=(shard_rows // tile,),
        in_specs=[SCALAR, whole(wanted.shape), whole(wanted.shape)]
        + [block] * len(bases)
        + [whole(own[0].shape)] * len(values),
        out_specs=block,
        compiler_params=params(32),
        cost_estimate=cost(
            2 * shard_rows * len(values) * capacity * width,
            2 * len(values) * capacity * width + 4 * (1 + len(bases)) * shard_rows * width,
        ),
        name="scatter_rows",
    )(place, wanted, other_wanted, *bases, *values)


def ordered_partners(shards):
    quarter = shards // 4
    order = []
    for flip in range(quarter):
        order += [(0, flip), (quarter, flip), (3 * quarter, flip)]
    return order + [(2 * quarter, flip) for flip in range(quarter)]


def behind(value, earlier):
    if not earlier:
        return value
    return lax.optimization_barrier((value, *earlier))[0]


def exchange(values, order, groups, flight, target, work, shards):
    received, done = {}, []
    per = len(groups[0])
    for index, offset in enumerate(order):
        value = values[offset]
        if index == 0:
            received[offset] = value
            continue
        back = flight if index < len(order) - shards // 4 else LAST_FLIGHT
        if index - back > 0:
            earlier = [received[order[index - back]]]
            while (len(done) + 1) * per <= index - back + 1:
                done.append(work(groups[len(done)], received))
                earlier.append(done[-1])
            value = behind(value, earlier)
        way = target(offset)
        pairs = [(i, ((i + way[0]) & (shards - 1)) ^ way[1]) for i in range(shards)]
        received[offset] = lax.ppermute(value, "idx", pairs)
    return received, len(done)


def local(queries, positives, passages, negatives):
    shards = lax.axis_size("idx")
    shard_rows, width = passages.shape
    ids = negatives.reshape(1, -1)
    slots = ids.shape[1]
    capacity = slots // shards
    scale = 3.0 / math.sqrt(width)
    factor = LSCALE * scale
    per = max(1, min(shards // 8, GROUP_SLOTS // capacity))
    order = ordered_partners(shards)
    groups = [tuple(order[i : i + per]) for i in range(0, shards, per)]
    me = lax.axis_index("idx").astype(jnp.int32)
    place = jnp.stack([me, lax.axis_index("enc").astype(jnp.int32)])

    request = build_request(ids, shards, shard_rows)
    wanted = lax.all_to_all(request, "idx", split_axis=0, concat_axis=0, tiled=True)
    other_wanted = lax.ppermute(wanted, "enc", SWAP)
    pos_logit = scale * jnp.sum(
        queries.astype(jnp.float32) * positives.astype(jnp.float32), axis=1
    )
    pos_logit = pos_logit.reshape(1, -1)

    picked, last = {}, [pos_logit]
    for group in groups:
        ways = [inverse(o, shards) for o in group]
        values = pick(behind(place, last), wanted, passages, ways)
        picked.update(zip(group, values))
        last = values[-1:]

    stats = [(pos_logit, jnp.ones_like(pos_logit))]
    exps, tops = {}, {}

    def logits_of(group, received):
        rows = [received[o] for o in group]
        top, total = stats[-1]
        exps[group], top, total = group_logits(
            place, request, top, total, queries, rows, group, scale
        )
        tops[group] = top
        stats.append((top, total))
        return top

    fetched, done = exchange(
        picked, order, groups, FETCH_FLIGHT, lambda o: inverse(o, shards), logits_of, shards
    )
    for group in groups[done:]:
        logits_of(group, fetched)
    top, total = stats[-1]

    weights, grads, last = {}, {}, []
    for group in groups:
        weights[group], values = row_grad(
            exps[group], behind(tops[group], last), top, total, queries, len(group), factor
        )
        grads.update(zip(group, values))
        last = values[-1:]
    grad_queries, loss = query_grad(
        pos_logit,
        top,
        total,
        positives,
        [weights[group] for group in groups],
        [fetched[o] for group in groups for o in group],
        factor,
    )
    middle = order[len(order) * 5 // 8]
    grads[middle] = behind(grads[middle], [grad_queries])

    sums = []

    def scattered(group, received, both, dtype=jnp.float32):
        own = [received[o] for o in group]
        if both:
            own[0] = behind(own[0], sums if len(sums) == 1 else [])
        other = [lax.ppermute(v, "enc", SWAP) for v in own] if both else []
        ways = [inverse(o, shards) for o in group]
        result = scatter(
            place, wanted, other_wanted, own, other, ways, list(sums), shard_rows, dtype
        )
        sums[:] = [result]
        return result

    returned, done = exchange(
        grads,
        order,
        groups,
        RETURN_FLIGHT,
        lambda o: o,
        lambda group, received: scattered(group, received, False),
        shards,
    )
    sums.append(lax.ppermute(sums[0], "enc", SWAP))
    for group in groups[done:-1]:
        scattered(group, returned, True)
    grad_passages = scattered(groups[-1], returned, True, jnp.bfloat16)
    return (loss.reshape(-1), grad_queries, grad_passages)


def solution(mesh):
    placed = (
        P(("idx", "enc"), None),
        P(("idx", "enc"), None),
        P("idx", None),
        P(("idx", "enc"), None),
    )
    return jax.shard_map(
        local,
        mesh=mesh,
        in_specs=placed,
        out_specs=(P(("idx", "enc")), P(("idx", "enc"), None), P("idx", None)),
        check_vma=False,
    )
```

```python
import functools
import math

import jax
import jax.numpy as jnp
from jax import lax
from jax.experimental import pallas as pl
from jax.experimental.pallas import tpu as pltpu
from jax.sharding import PartitionSpec as P

LSCALE = 32
DEAD = -1e30
LANES = 128
MIB = 1 << 20
GROUP_SLOTS = 256
SHARE = 0.01
FLIGHT = 5
QUERY_PARTS = 4
PICK_PARTS = 4
QUERY_TILE = 256
SWAP = [(0, 1), (1, 0)]


def params(vmem_mib):
    return pltpu.CompilerParams(vmem_limit_bytes=vmem_mib * MIB)


def cost(flops, bytes_accessed, transcendentals=0):
    return pl.CostEstimate(
        flops=int(flops * SHARE), bytes_accessed=int(bytes_accessed * SHARE), transcendentals=0
    )


def whole(shape):
    return pl.BlockSpec(shape, lambda *_: (0,) * len(shape))


SCALAR = pl.BlockSpec(memory_space=pltpu.SMEM)
IN_HBM = pl.BlockSpec(memory_space=pltpu.HBM)
UNREAD = pl.BlockSpec(memory_space=pl.ANY)
IN_VMEM = pl.BlockSpec(memory_space=pltpu.VMEM)


def request_kernel(shard_rows, ids_ref, out_ref):
    shards, capacity = out_ref.shape
    count = ids_ref.shape[1]
    ids = ids_ref[...]
    base = lax.broadcasted_iota(jnp.int32, (shards, 1), 0) * shard_rows
    row = ids - base
    mine = (row >= 0) & (row < shard_rows)
    one = jnp.where(mine, 1.0, 0.0)
    high = jnp.where(mine, row // 128, 0).astype(jnp.float32)
    low = jnp.where(mine, row % 128, 0).astype(jnp.float32)
    before = (
        lax.broadcasted_iota(jnp.int32, (LANES, LANES), 0)
        < lax.broadcasted_iota(jnp.int32, (LANES, LANES), 1)
    ).astype(jnp.bfloat16)
    carry = jnp.zeros((shards, 1), jnp.float32)
    places = []
    for start in range(0, count, LANES):
        part = one[:, start : start + LANES]
        inside = jnp.dot(part.astype(jnp.bfloat16), before, preferred_element_type=jnp.float32)
        rank = jnp.sum(part * (inside + carry), axis=0, keepdims=True)
        carry = carry + jnp.sum(part, axis=1, keepdims=True)
        slot = lax.broadcasted_iota(jnp.int32, (capacity, LANES), 0).astype(jnp.float32)
        places.append(jnp.where(slot == rank, 1.0, 0.0))
    place = jnp.concatenate(places, axis=1).astype(jnp.bfloat16)
    parts = jnp.concatenate([one, high, low], axis=0).astype(jnp.bfloat16)
    packed = lax.dot_general(
        parts, place, (((1,), (1,)), ((), ())), preferred_element_type=jnp.float32
    )
    filled = packed[:shards] > 0.5
    rows = packed[shards : 2 * shards] * 128.0 + packed[2 * shards :]
    out_ref[...] = jnp.where(filled, rows.astype(jnp.int32), -1)


def build_request(ids, shards, shard_rows):
    count = ids.shape[1]
    capacity = count // shards
    return pl.pallas_call(
        functools.partial(request_kernel, shard_rows),
        out_shape=jax.ShapeDtypeStruct((shards, capacity), jnp.int32),
        compiler_params=params(16),
        cost_estimate=cost(2 * 3 * shards * count * capacity, 16384),
        name="build_request",
    )(ids)


def as_columns(lines):
    blocks = []
    for line in lines:
        for start in range(0, line.shape[1], LANES):
            piece = line[:, start : start + LANES]
            blocks.append(jnp.broadcast_to(piece, (LANES, piece.shape[1])).T)
    return jnp.concatenate(blocks, axis=0)


def partner_line(table_ref, me, offset):
    return table_ref[pl.ds(jnp.bitwise_xor(me, offset), 1), :]


def pick_kernel(offsets, place_ref, wanted_ref, passages_ref, *refs):
    *out_refs, rows_ref, arrived = refs
    rows = passages_ref.shape[0]
    part = rows // PICK_PARTS
    copies = []
    for index in range(PICK_PARTS):
        span = pl.ds(index * part, part)
        copies.append(
            pltpu.make_async_copy(passages_ref.at[span], rows_ref.at[span], arrived.at[index])
        )
        copies[-1].start()
    me = place_ref[0]
    wanted = as_columns([partner_line(wanted_ref, me, o).astype(jnp.float32) for o in offsets])
    lane = lax.broadcasted_iota(jnp.int32, wanted.shape, 1).astype(jnp.float32)
    picked = None
    for index in range(PICK_PARTS):
        first = index * part
        hot = jnp.concatenate(
            [
                jnp.where(wanted == lane + float(start), 1.0, 0.0).astype(jnp.bfloat16)
                for start in range(first, first + part, LANES)
            ],
            axis=1,
        )
        copies[index].wait()
        value = jnp.dot(
            hot, rows_ref[first : first + part, :], preferred_element_type=jnp.float32
        )
        picked = value if picked is None else picked + value
    picked = picked.astype(jnp.bfloat16)
    size = out_refs[0].shape[0]
    for index, ref in enumerate(out_refs):
        ref[...] = picked[index * size : (index + 1) * size]


def pick(place, wanted, passages, offsets):
    shards, capacity = wanted.shape
    rows, width = passages.shape
    block = jax.ShapeDtypeStruct((capacity, width), jnp.bfloat16)
    return pl.pallas_call(
        functools.partial(pick_kernel, offsets),
        out_shape=[block] * len(offsets),
        in_specs=[SCALAR, IN_VMEM, IN_HBM],
        out_specs=[IN_VMEM] * len(offsets),
        scratch_shapes=[
            pltpu.VMEM((rows, width), passages.dtype),
            pltpu.SemaphoreType.DMA((PICK_PARTS,)),
        ],
        compiler_params=params(16),
        cost_estimate=cost(
            2 * len(offsets) * capacity * rows * width,
            2 * (rows + len(offsets) * capacity) * width,
        ),
        name="pick_rows",
    )(place, wanted, passages)


def logits_kernel(offsets, scale, place_ref, request_ref, top_ref, total_ref, queries_ref, *refs):
    fetched_refs = refs[: len(offsets)]
    exps_ref, new_top_ref, new_total_ref = refs[len(offsets) :]
    me = place_ref[0]
    request = [partner_line(request_ref, me, o).astype(jnp.float32) for o in offsets]
    live = as_columns(request) >= 0.0
    fetched = jnp.concatenate([ref[...] for ref in fetched_refs], axis=0)
    for first in range(0, queries_ref.shape[0], QUERY_TILE):
        logits = lax.dot_general(
            fetched,
            queries_ref[first : first + QUERY_TILE, :],
            (((1,), (1,)), ((), ())),
            preferred_element_type=jnp.float32,
        )
        for start in range(0, QUERY_TILE, LANES):
            lanes = slice(first + start, first + start + LANES)
            part = jnp.where(live, scale * logits[:, start : start + LANES], DEAD)
            old_top = top_ref[:, lanes]
            top = jnp.maximum(old_top, jnp.max(part, axis=0, keepdims=True))
            exps = jnp.exp(part - top)
            exps_ref[:, lanes] = exps
            new_top_ref[:, lanes] = top
            new_total_ref[:, lanes] = total_ref[:, lanes] * jnp.exp(old_top - top) + jnp.sum(
                exps, axis=0, keepdims=True
            )


def group_logits(place, request, top, total, queries, fetched, offsets, scale):
    capacity, width = fetched[0].shape
    slots = capacity * len(offsets)
    count = queries.shape[0]
    shape = jax.ShapeDtypeStruct((1, count), jnp.float32)
    return pl.pallas_call(
        functools.partial(logits_kernel, offsets, scale),
        out_shape=(jax.ShapeDtypeStruct((slots, count), jnp.float32), shape, shape),
        in_specs=[SCALAR] + [IN_VMEM] * (4 + len(offsets)),
        out_specs=(IN_VMEM,) * 3,
        compiler_params=params(24),
        cost_estimate=cost(
            2 * slots * width * count,
            2 * (slots + count) * width + 4 * slots * count,
            slots * count,
        ),
        name="group_logits",
    )(place, request, top, total, queries, *fetched)


def row_grad_kernel(factor, exps_ref, own_top_ref, top_ref, total_ref, queries_ref, *refs):
    weights_ref, *out_refs = refs
    share = factor * jnp.exp(own_top_ref[...] - top_ref[...]) / total_ref[...]
    weights = (exps_ref[...] * share).astype(jnp.bfloat16)
    weights_ref[...] = weights
    value = jnp.dot(weights, queries_ref[...], preferred_element_type=jnp.float32)
    value = value.astype(jnp.bfloat16)
    size = out_refs[0].shape[0]
    for index, ref in enumerate(out_refs):
        ref[...] = value[index * size : (index + 1) * size]


def row_grad(exps, own_top, top, total, queries, parts, factor):
    slots, count = exps.shape
    width = queries.shape[1]
    block = jax.ShapeDtypeStruct((slots // parts, width), jnp.bfloat16)
    weights, *grads = pl.pallas_call(
        functools.partial(row_grad_kernel, factor),
        out_shape=[jax.ShapeDtypeStruct((slots, count), jnp.bfloat16)] + [block] * parts,
        in_specs=[IN_VMEM] * 5,
        out_specs=[IN_VMEM] * (1 + parts),
        compiler_params=params(24),
        cost_estimate=cost(
            2 * slots * width * count, 2 * (slots + count) * width + 6 * slots * count
        ),
        name="row_grad",
    )(exps, own_top, top, total, queries)
    return weights, grads


def query_kernel(factor, groups, pos_ref, top_ref, total_ref, positives_ref, *refs):
    weights_refs = refs[:groups]
    fetched_refs = refs[groups : groups + len(refs[groups:]) // groups * groups]
    grad_ref = refs[-1]
    per = len(fetched_refs) // groups
    pos, top, total = pos_ref[...], top_ref[...], total_ref[...]
    coef = as_columns([factor * (jnp.exp(pos - top) / total - 1.0)])
    value = jnp.concatenate(
        [
            coef * positives_ref[:, start : start + LANES].astype(jnp.float32)
            for start in range(0, positives_ref.shape[1], LANES)
        ],
        axis=1,
    )
    for group, ref in enumerate(weights_refs):
        rows = jnp.concatenate(
            [one[...] for one in fetched_refs[group * per : (group + 1) * per]], axis=0
        )
        value = value + lax.dot_general(
            ref[...], rows, (((0,), (0,)), ((), ())), preferred_element_type=jnp.float32
        )
    grad_ref[...] = value.astype(jnp.bfloat16)


def query_grad(pos, top, total, positives, weights, fetched, factor, part, parts, grads):
    count, width = positives.shape
    tile = min(256, count // parts)
    first = part * (count // parts // tile)
    line = pl.BlockSpec((1, tile), lambda t: (0, first + t))
    block = pl.BlockSpec((tile, width), lambda t: (first + t, 0))
    slots = weights[0].shape[0]
    inputs = [pos, top, total, positives, *weights, *fetched, *grads]
    return pl.pallas_call(
        functools.partial(query_kernel, factor, len(weights)),
        out_shape=jax.ShapeDtypeStruct((count, width), jnp.bfloat16),
        grid=(count // parts // tile,),
        in_specs=[line, line, line, block]
        + [pl.BlockSpec((slots, tile), lambda t: (0, first + t))] * len(weights)
        + [whole(fetched[0].shape)] * len(fetched)
        + [UNREAD] * len(grads),
        out_specs=block,
        input_output_aliases={len(inputs) - 1: 0} if grads else {},
        compiler_params=params(40),
        cost_estimate=cost(
            2 * len(weights) * slots * width * count // parts,
            2 * len(weights) * slots * width + 4 * count * width // parts,
        ),
        name="query_grad",
    )(*inputs)


def scatter_kernel(offsets, both, bases, place_ref, own_ref, other_ref, *refs):
    count = len(offsets)
    base_refs, value_refs, out_ref = refs[:bases], refs[bases:-1], refs[-1]
    rows = out_ref.shape[0]
    me = place_ref[0]
    row = pl.program_id(0) * rows + lax.broadcasted_iota(jnp.int32, (rows, 1), 0)
    lines = [partner_line(own_ref, me, o) for o in offsets]
    values = [ref[...] for ref in value_refs[:count]]
    if both:
        lead = place_ref[1] == 0
        other_lines = [partner_line(other_ref, me, o) for o in offsets]
        other_values = [ref[...] for ref in value_refs[count:]]
        pairs = [
            (jnp.concatenate(x, axis=axis), jnp.concatenate(y, axis=axis))
            for x, y, axis in ((lines, other_lines, 1), (values, other_values, 0))
        ]
        (line, other_line), (value, other_value) = pairs
        lines = [jnp.where(lead, line, other_line), jnp.where(lead, other_line, line)]
        values = [jnp.where(lead, value, other_value), jnp.where(lead, other_value, value)]
    hot = jnp.concatenate(
        [jnp.where(line == row, 1.0, 0.0).astype(jnp.bfloat16) for line in lines], axis=1
    )
    total = jnp.dot(hot, jnp.concatenate(values, axis=0), preferred_element_type=jnp.float32)
    if bases:
        base = base_refs[0][...].astype(jnp.float32)
        for ref in base_refs[1:]:
            base = base + ref[...].astype(jnp.float32)
        total = base + total
    out_ref[...] = total.astype(out_ref.dtype)


def scatter(place, wanted, other_wanted, own, other, offsets, bases, shard_rows, dtype):
    capacity, width = own[0].shape
    tile = min(256, shard_rows)
    block = pl.BlockSpec((tile, width), lambda t: (t, 0))
    values = [*own, *other]
    return pl.pallas_call(
        functools.partial(scatter_kernel, offsets, bool(other), len(bases)),
        out_shape=jax.ShapeDtypeStruct((shard_rows, width), dtype),
        grid=(shard_rows // tile,),
        in_specs=[SCALAR, whole(wanted.shape), whole(wanted.shape)]
        + [block] * len(bases)
        + [whole(own[0].shape)] * len(values),
        out_specs=block,
        compiler_params=params(32),
        cost_estimate=cost(
            2 * shard_rows * len(values) * capacity * width,
            2 * len(values) * capacity * width + 4 * (1 + len(bases)) * shard_rows * width,
        ),
        name="scatter_rows",
    )(place, wanted, other_wanted, *bases, *values)


def partner_order(shards, per):
    half = shards // 2
    quarter = half // 2
    far = [half + part * quarter + place for place in range(quarter) for part in range(2)]
    near = list(range(quarter, half)) + list(range(1, quarter))
    lead = half // 2 + 1
    order = far[:lead]
    for place in range(half - lead):
        order += [near[place], far[lead + place]]
    order += near[half - lead :]
    arrival = [o for o in order if o != far[-1]]
    arrival = arrival[:-2] + [far[-1]] + arrival[-2:] + [0]
    return order, [tuple(arrival[i : i + per]) for i in range(0, shards, per)]


def behind(value, earlier):
    if not earlier:
        return value
    return lax.optimization_barrier((value, *earlier))[0]


def exchange(values, order, before, shards):
    received = {0: values[0]}
    for index, offset in enumerate(order):
        earlier = [received[order[index - FLIGHT]]] if index >= FLIGHT else []
        earlier += [work(received) for work in before.get(index, [])]
        pairs = [(i, i ^ offset) for i in range(shards)]
        received[offset] = lax.ppermute(behind(values[offset], earlier), "idx", pairs)
    return received


def local(queries, positives, passages, negatives):
    shards = lax.axis_size("idx")
    shard_rows, width = passages.shape
    ids = negatives.reshape(1, -1)
    slots = ids.shape[1]
    capacity = slots // shards
    scale = 3.0 / math.sqrt(width)
    factor = LSCALE * scale
    per = max(1, min(shards // 8, GROUP_SLOTS // capacity))
    order, groups = partner_order(shards, per)
    last_start = len(order) - 1
    arrival = [max(order.index(o) for o in group if o) for group in groups]
    me = lax.axis_index("idx").astype(jnp.int32)
    place = jnp.stack([me, lax.axis_index("enc").astype(jnp.int32)])

    request = build_request(ids, shards, shard_rows)
    wanted = lax.all_to_all(request, "idx", split_axis=0, concat_axis=0, tiled=True)
    other_wanted = lax.ppermute(wanted, "enc", SWAP)
    pos_logit = scale * jnp.sum(
        queries.astype(jnp.float32) * positives.astype(jnp.float32), axis=1
    )
    pos_logit = pos_logit.reshape(1, -1)

    picked, last = {}, [pos_logit]
    for group in groups:
        values = pick(behind(place, last), wanted, passages, group)
        picked.update(zip(group, values))
        last = values[-1:]

    stats = [(pos_logit, jnp.ones_like(pos_logit))]
    exps, tops = {}, {}

    def logits_of(group, received):
        rows = [received[o] for o in group]
        top, total = stats[-1]
        exps[group], top, total = group_logits(
            place, request, top, total, queries, rows, group, scale
        )
        tops[group] = top
        stats.append((top, total))
        return top

    before = {}
    for group, arrived in zip(groups, arrival):
        if arrived + FLIGHT + 1 <= last_start:
            before[arrived + FLIGHT + 1] = [functools.partial(logits_of, group)]
    fetched = exchange(picked, order, before, shards)
    for group in groups[len(before) :]:
        logits_of(group, fetched)
    top, total = stats[-1]
    loss = top + jnp.log(total) - pos_logit

    weights, grads, last = {}, {}, []
    for group in groups:
        weights[group], values = row_grad(
            exps[group], behind(tops[group], last), top, total, queries, len(group), factor
        )
        grads.update(zip(group, values))
        last = values[-1:]

    query_grads = []

    def query_part(part, received):
        query_grads[:] = [
            query_grad(
                behind(pos_logit, [received[order[part + 3]]]),
                top,
                total,
                positives,
                [weights[group] for group in groups],
                [fetched[o] for group in groups for o in group],
                factor,
                part,
                QUERY_PARTS,
                query_grads,
            )
        ]
        return query_grads[0]

    sums = []

    def scattered(members, received, other, dtype=jnp.float32):
        own = [received[o] for o in members]
        result = scatter(
            place, wanted, other_wanted, own, other, members, list(sums), shard_rows, dtype
        )
        sums[:] = [result]
        return result

    before = {
        last_start - QUERY_PARTS + part: [functools.partial(query_part, part)]
        for part in range(QUERY_PARTS)
    }
    early, late = groups[:-2], sum(groups[-2:], ())
    for group, arrived in list(zip(early, arrival))[:-1]:
        if arrived + FLIGHT + 1 <= last_start:
            before.setdefault(arrived + FLIGHT + 1, []).append(
                lambda received, group=group: scattered(group, received, [])
            )
    done = sum(arrived + FLIGHT + 1 <= last_start for arrived in arrival[: len(early) - 1])
    returned = exchange(grads, order, before, shards)
    for group in early[done:]:
        final = group == early[-1]
        scattered(group, returned, [], jnp.bfloat16 if final else jnp.float32)
    sums.append(lax.ppermute(sums[0], "enc", SWAP))
    swapped = [lax.ppermute(returned[o], "enc", SWAP) for o in late]
    grad_passages = scattered(late, returned, swapped, jnp.bfloat16)
    return (loss.reshape(-1), query_grads[0], grad_passages)


def solution(mesh):
    placed = (
        P(("idx", "enc"), None),
        P(("idx", "enc"), None),
        P("idx", None),
        P(("idx", "enc"), None),
    )
    return jax.shard_map(
        local,
        mesh=mesh,
        in_specs=placed,
        out_specs=(P(("idx", "enc")), P(("idx", "enc"), None), P("idx", None)),
        check_vma=False,
    )
```

```python
import functools
import math

import jax
import jax.numpy as jnp
from jax import lax
from jax.experimental import pallas as pl
from jax.experimental.pallas import tpu as pltpu
from jax.sharding import PartitionSpec as P

LSCALE = 32
DEAD = -1e30
LANES = 128
MIB = 1 << 20
GROUP_SLOTS = 256
SHARE = 0.01
QUERY_TILE = 256
QUERY_PARTS = 4
SUM_PARTS = 4
SWAP = [(0, 1), (1, 0)]


def params(vmem_mib):
    return pltpu.CompilerParams(vmem_limit_bytes=vmem_mib * MIB)


def cost(flops, bytes_accessed, transcendentals=0):
    return pl.CostEstimate(
        flops=int(flops * SHARE), bytes_accessed=int(bytes_accessed * SHARE), transcendentals=0
    )


def whole(shape):
    return pl.BlockSpec(shape, lambda *_: (0,) * len(shape))


SCALAR = pl.BlockSpec(memory_space=pltpu.SMEM)
UNREAD = pl.BlockSpec(memory_space=pl.ANY)
IN_VMEM = pl.BlockSpec(memory_space=pltpu.VMEM)


def request_kernel(shard_rows, ids_ref, out_ref):
    shards, capacity = out_ref.shape
    count = ids_ref.shape[1]
    ids = ids_ref[...]
    base = lax.broadcasted_iota(jnp.int32, (shards, 1), 0) * shard_rows
    row = ids - base
    mine = (row >= 0) & (row < shard_rows)
    one = jnp.where(mine, 1.0, 0.0)
    high = jnp.where(mine, row // 128, 0).astype(jnp.float32)
    low = jnp.where(mine, row % 128, 0).astype(jnp.float32)
    before = (
        lax.broadcasted_iota(jnp.int32, (LANES, LANES), 0)
        < lax.broadcasted_iota(jnp.int32, (LANES, LANES), 1)
    ).astype(jnp.bfloat16)
    carry = jnp.zeros((shards, 1), jnp.float32)
    places = []
    for start in range(0, count, LANES):
        part = one[:, start : start + LANES]
        inside = jnp.dot(part.astype(jnp.bfloat16), before, preferred_element_type=jnp.float32)
        rank = jnp.sum(part * (inside + carry), axis=0, keepdims=True)
        carry = carry + jnp.sum(part, axis=1, keepdims=True)
        slot = lax.broadcasted_iota(jnp.int32, (capacity, LANES), 0).astype(jnp.float32)
        places.append(jnp.where(slot == rank, 1.0, 0.0))
    place = jnp.concatenate(places, axis=1).astype(jnp.bfloat16)
    parts = jnp.concatenate([one, high, low], axis=0).astype(jnp.bfloat16)
    packed = lax.dot_general(
        parts, place, (((1,), (1,)), ((), ())), preferred_element_type=jnp.float32
    )
    filled = packed[:shards] > 0.5
    rows = packed[shards : 2 * shards] * 128.0 + packed[2 * shards :]
    out_ref[...] = jnp.where(filled, rows.astype(jnp.int32), -1)


def build_request(ids, shards, shard_rows):
    count = ids.shape[1]
    capacity = count // shards
    return pl.pallas_call(
        functools.partial(request_kernel, shard_rows),
        out_shape=jax.ShapeDtypeStruct((shards, capacity), jnp.int32),
        compiler_params=params(16),
        cost_estimate=cost(2 * 3 * shards * count * capacity, 16384),
        name="build_request",
    )(ids)


def set_offsets(shards):
    quarter = shards // 4
    return [*range(quarter), *range(3 * quarter, shards)]


def set_start(position, shards):
    quarter = shards // 4
    step = position // quarter
    return quarter * ((step ^ (step // 2)) & 1)


def partner_line(table_ref, me, member):
    inside, offset = member
    start = set_start(me, table_ref.shape[0]) if inside else me
    return table_ref[pl.ds(jnp.bitwise_xor(start, offset), 1), :]


def as_columns(lines):
    blocks = []
    for line in lines:
        for start in range(0, line.shape[1], LANES):
            piece = line[:, start : start + LANES]
            blocks.append(jnp.broadcast_to(piece, (LANES, piece.shape[1])).T)
    return jnp.concatenate(blocks, axis=0)


def store_blocks(refs, first, value):
    if len(refs) == 1 and len(refs[0].shape) == 3:
        size = refs[0].shape[1]
        count = value.shape[0] // size
        refs[0][first : first + count] = value.reshape(count, size, value.shape[1])
    else:
        size = refs[0].shape[0]
        for index in range(value.shape[0] // size):
            refs[first + index][...] = value[index * size : (index + 1) * size]


def block_shapes(members, capacity, width):
    if members[0][0]:
        return [jax.ShapeDtypeStruct((len(members), capacity, width), jnp.bfloat16)]
    return [jax.ShapeDtypeStruct((capacity, width), jnp.bfloat16)] * len(members)


def hold_kernel(rows_ref, out_ref):
    out_ref[...] = rows_ref[: out_ref.shape[0], : out_ref.shape[1]]


def hold(passages):
    return pl.pallas_call(
        hold_kernel,
        out_shape=jax.ShapeDtypeStruct((16, LANES), passages.dtype),
        in_specs=[IN_VMEM],
        out_specs=IN_VMEM,
        compiler_params=params(8),
        cost_estimate=cost(0, 4096),
        name="hold_rows",
    )(passages)


def pick_kernel(members, place_ref, wanted_ref, passages_ref, *out_refs):
    rows = passages_ref.shape[0]
    per = max(1, GROUP_SLOTS // wanted_ref.shape[1])
    me = place_ref[0]
    for first in range(0, len(members), per):
        wanted = as_columns(
            [
                partner_line(wanted_ref, me, member).astype(jnp.float32)
                for member in members[first : first + per]
            ]
        )
        lane = lax.broadcasted_iota(jnp.int32, wanted.shape, 1).astype(jnp.float32)
        hot = jnp.concatenate(
            [
                jnp.where(wanted == lane + float(start), 1.0, 0.0).astype(jnp.bfloat16)
                for start in range(0, rows, LANES)
            ],
            axis=1,
        )
        picked = jnp.dot(hot, passages_ref[...], preferred_element_type=jnp.float32)
        store_blocks(out_refs, first, picked.astype(jnp.bfloat16))


def pick(place, wanted, passages, members):
    capacity = wanted.shape[1]
    rows, width = passages.shape
    shapes = block_shapes(members, capacity, width)
    return pl.pallas_call(
        functools.partial(pick_kernel, members),
        out_shape=shapes,
        in_specs=[SCALAR, IN_VMEM, IN_VMEM],
        out_specs=[IN_VMEM] * len(shapes),
        compiler_params=params(20),
        cost_estimate=cost(
            2 * len(members) * capacity * rows * width,
            2 * (rows + len(members) * capacity) * width,
        ),
        name="pick_rows",
    )(place, wanted, passages)


def logits_kernel(members, scale, place_ref, request_ref, top_ref, total_ref, queries_ref, *refs):
    fetched_refs, (exps_ref, new_top_ref, new_total_ref) = refs[:-3], refs[-3:]
    me = place_ref[0]
    live = (
        as_columns([partner_line(request_ref, me, m).astype(jnp.float32) for m in members]) >= 0.0
    )
    fetched = jnp.concatenate([ref[...] for ref in fetched_refs], axis=0)
    for first in range(0, queries_ref.shape[0], QUERY_TILE):
        logits = lax.dot_general(
            fetched,
            queries_ref[first : first + QUERY_TILE, :],
            (((1,), (1,)), ((), ())),
            preferred_element_type=jnp.float32,
        )
        for start in range(0, QUERY_TILE, LANES):
            lanes = slice(first + start, first + start + LANES)
            part = jnp.where(live, scale * logits[:, start : start + LANES], DEAD)
            old_top = top_ref[:, lanes]
            top = jnp.maximum(old_top, jnp.max(part, axis=0, keepdims=True))
            exps = jnp.exp(part - top)
            exps_ref[:, lanes] = exps
            new_top_ref[:, lanes] = top
            new_total_ref[:, lanes] = total_ref[:, lanes] * jnp.exp(old_top - top) + jnp.sum(
                exps, axis=0, keepdims=True
            )


def group_logits(place, request, top, total, queries, fetched, members, scale):
    width = fetched[0].shape[1]
    slots = sum(rows.shape[0] for rows in fetched)
    count = queries.shape[0]
    shape = jax.ShapeDtypeStruct((1, count), jnp.float32)
    return pl.pallas_call(
        functools.partial(logits_kernel, members, scale),
        out_shape=(jax.ShapeDtypeStruct((slots, count), jnp.float32), shape, shape),
        in_specs=[SCALAR] + [IN_VMEM] * (4 + len(fetched)),
        out_specs=(IN_VMEM,) * 3,
        compiler_params=params(32),
        cost_estimate=cost(
            2 * slots * width * count,
            2 * (slots + count) * width + 4 * slots * count,
            slots * count,
        ),
        name="group_logits",
    )(place, request, top, total, queries, *fetched)


def row_grad_kernel(capacity, factor, exps_ref, own_top_ref, top_ref, total_ref, queries_ref, *refs):
    weights_ref, *out_refs = refs
    share = factor * jnp.exp(own_top_ref[...] - top_ref[...]) / total_ref[...]
    for first in range(0, exps_ref.shape[0], GROUP_SLOTS):
        span = slice(first, first + GROUP_SLOTS)
        weights = (exps_ref[span, :] * share).astype(jnp.bfloat16)
        weights_ref[span, :] = weights
        value = jnp.dot(weights, queries_ref[...], preferred_element_type=jnp.float32)
        store_blocks(out_refs, first // capacity, value.astype(jnp.bfloat16))


def row_grad(exps, own_top, top, total, queries, members, factor):
    slots, count = exps.shape
    width = queries.shape[1]
    capacity = slots // len(members)
    shapes = block_shapes(members, capacity, width)
    weights, *grads = pl.pallas_call(
        functools.partial(row_grad_kernel, capacity, factor),
        out_shape=[jax.ShapeDtypeStruct((slots, count), jnp.bfloat16)] + shapes,
        in_specs=[IN_VMEM] * 5,
        out_specs=[IN_VMEM] * (1 + len(shapes)),
        compiler_params=params(32),
        cost_estimate=cost(
            2 * slots * width * count, 2 * (slots + count) * width + 6 * slots * count
        ),
        name="row_grad",
    )(exps, own_top, top, total, queries)
    return weights, grads


def query_kernel(factor, sizes, pos_ref, top_ref, total_ref, positives_ref, *refs):
    weights_refs, rest = refs[: len(sizes)], refs[len(sizes) :]
    grad_ref = refs[-1]
    pos, top, total = pos_ref[...], top_ref[...], total_ref[...]
    coef = as_columns([factor * (jnp.exp(pos - top) / total - 1.0)])
    value = jnp.concatenate(
        [
            coef * positives_ref[:, start : start + LANES].astype(jnp.float32)
            for start in range(0, positives_ref.shape[1], LANES)
        ],
        axis=1,
    )
    first = 0
    for ref, size in zip(weights_refs, sizes):
        rows = jnp.concatenate([one[...] for one in rest[first : first + size]], axis=0)
        first += size
        value = value + lax.dot_general(
            ref[...], rows, (((0,), (0,)), ((), ())), preferred_element_type=jnp.float32
        )
    grad_ref[...] = value.astype(jnp.bfloat16)


def query_grad(pos, top, total, positives, weights, fetched, factor, part, grads):
    count, width = positives.shape
    tile = min(256, count // QUERY_PARTS)
    steps = count // QUERY_PARTS // tile
    first = part * steps
    line = pl.BlockSpec((1, tile), lambda t: (0, first + t))
    block = pl.BlockSpec((tile, width), lambda t: (first + t, 0))
    sizes = [len(group) for group in fetched]
    rows = [one for group in fetched for one in group]
    inputs = [pos, top, total, positives, *weights, *rows, *grads]
    slots = sum(one.shape[0] for one in weights)
    return pl.pallas_call(
        functools.partial(query_kernel, factor, sizes),
        out_shape=jax.ShapeDtypeStruct((count, width), jnp.bfloat16),
        grid=(steps,),
        in_specs=[line, line, line, block]
        + [pl.BlockSpec((one.shape[0], tile), lambda t: (0, first + t)) for one in weights]
        + [whole(one.shape) for one in rows]
        + [UNREAD] * len(grads),
        out_specs=block,
        input_output_aliases={len(inputs) - 1: 0} if grads else {},
        compiler_params=params(40),
        cost_estimate=cost(
            2 * slots * width * count // QUERY_PARTS,
            2 * slots * width + 4 * count * width // QUERY_PARTS,
        ),
        name="query_grad",
    )(*inputs)


def scatter_kernel(members, first, place_ref, wanted_ref, *refs):
    *value_refs, out_ref = refs
    base_ref = value_refs.pop(0) if value_refs[0].shape == out_ref.shape else None
    rows = out_ref.shape[0]
    me = place_ref[0]
    row = (first + pl.program_id(0)) * rows + lax.broadcasted_iota(jnp.int32, (rows, 1), 0)
    hot = jnp.concatenate(
        [
            jnp.where(partner_line(wanted_ref, me, m) == row, 1.0, 0.0).astype(jnp.bfloat16)
            for m in members
        ],
        axis=1,
    )
    values = jnp.concatenate([ref[...] for ref in value_refs], axis=0)
    total = jnp.dot(hot, values, preferred_element_type=jnp.float32)
    if base_ref is not None:
        total = base_ref[...] + total
    out_ref[...] = total.astype(out_ref.dtype)


def scatter(place, wanted, values, members, base, shard_rows, part, parts, dtype):
    width = values[0].shape[1]
    slots = sum(one.shape[0] for one in values)
    rows = shard_rows // parts
    tile = 2 * LANES
    first = part * rows // tile
    return pl.pallas_call(
        functools.partial(scatter_kernel, members, first),
        out_shape=jax.ShapeDtypeStruct((rows, width), dtype),
        grid=(rows // tile,),
        in_specs=[SCALAR, whole(wanted.shape)]
        + [pl.BlockSpec((tile, width), lambda t: (first + t, 0))] * len(base)
        + [whole(one.shape) for one in values],
        out_specs=pl.BlockSpec((tile, width), lambda t: (t, 0)),
        compiler_params=params(32),
        cost_estimate=cost(
            2 * rows * slots * width, 2 * slots * width + 4 * (1 + len(base)) * rows * width
        ),
        name="scatter_rows",
    )(place, wanted, *base, *values)


def add_kernel(own_ref, other_ref, *refs):
    refs[-1][...] = (
        own_ref[...].astype(jnp.float32) + other_ref[...].astype(jnp.float32)
    ).astype(jnp.bfloat16)


def add_part(own, other, part, parts, sums):
    rows, width = own.shape
    tile = min(256, rows)
    first = part * rows // tile
    block = pl.BlockSpec((tile, width), lambda t: (t, 0))
    return pl.pallas_call(
        add_kernel,
        out_shape=jax.ShapeDtypeStruct((rows * parts, width), jnp.bfloat16),
        grid=(rows // tile,),
        in_specs=[block, block] + [UNREAD] * len(sums),
        out_specs=pl.BlockSpec((tile, width), lambda t: (first + t, 0)),
        input_output_aliases={2: 0} if sums else {},
        compiler_params=params(16),
        cost_estimate=cost(rows * width, 6 * rows * width),
        name="add_cores",
    )(own, other, *sums)


def behind(value, earlier):
    if not earlier:
        return value
    return lax.optimization_barrier((value, *earlier))[0]


def exchange(blocks, members, shards):
    if members[0][0]:
        offsets = set_offsets(shards)
        sets = [[start ^ o for o in offsets] for start in (0, shards // 4)]
        block = lax.all_to_all(
            blocks[0], "idx", split_axis=0, concat_axis=0, tiled=True, axis_index_groups=sets
        )
        return [block.reshape(-1, block.shape[-1])]
    return [
        lax.ppermute(block, "idx", [(i, i ^ offset) for i in range(shards)])
        for block, (_, offset) in zip(blocks, members)
    ]


def local(queries, positives, passages, negatives):
    shards = lax.axis_size("idx")
    shard_rows, width = passages.shape
    ids = negatives.reshape(1, -1)
    capacity = ids.shape[1] // shards
    scale = 3.0 / math.sqrt(width)
    factor = LSCALE * scale
    quarter = shards // 4
    per = min(quarter, GROUP_SLOTS // capacity)
    far, near = [
        [tuple((False, start + o + i) for i in range(per)) for o in range(0, quarter, per)]
        for start in (2 * quarter, quarter)
    ]
    within = tuple((True, o) for o in set_offsets(shards))
    order = [*far, within, *near]
    place = lax.axis_index("idx").astype(jnp.int32).reshape(1)

    request = build_request(ids, shards, shard_rows)
    wanted = lax.all_to_all(request, "idx", split_axis=0, concat_axis=0, tiled=True)
    pos_logit = scale * jnp.sum(
        queries.astype(jnp.float32) * positives.astype(jnp.float32), axis=1
    )
    pos_logit = pos_logit.reshape(1, -1)

    fetched, last = {}, [pos_logit, hold(passages)]
    for group in order:
        picked = pick(behind(place, last), wanted, passages, group)
        fetched[group] = exchange(picked, group, shards)
        last = picked[-1:]

    worked = [*far, *near, within]
    top, total = pos_logit, jnp.ones_like(pos_logit)
    exps, tops = {}, {}
    for group in worked:
        exps[group], top, total = group_logits(
            place, request, top, total, queries, fetched[group], group, scale
        )
        tops[group] = top
    loss = top + jnp.log(total) - pos_logit

    weights, returned, last = {}, {}, []
    for group in order:
        weights[group], grads = row_grad(
            exps[group], behind(tops[group], last), top, total, queries, group, factor
        )
        returned[group] = exchange(grads, group, shards)
        last = grads[-1:]

    grad_queries = []
    for part in range(QUERY_PARTS):
        grad_queries = [
            query_grad(
                pos_logit,
                top,
                total,
                positives,
                [weights[group] for group in worked],
                [fetched[group] for group in worked],
                factor,
                part,
                grad_queries,
            )
        ]

    base = []
    for groups in (far, near):
        base = [
            scatter(
                place,
                wanted,
                [one for group in groups for one in returned[group]],
                sum(groups, ()),
                base,
                shard_rows,
                0,
                1,
                jnp.float32,
            )
        ]
    late = [behind(returned[within][0], [*base, *grad_queries])]
    grad_passages = []
    parts = [
        scatter(place, wanted, late, within, base, shard_rows, part, SUM_PARTS, jnp.bfloat16)
        for part in range(SUM_PARTS)
    ]
    for part, own in enumerate(parts):
        other = lax.ppermute(own, "enc", SWAP)
        grad_passages = [add_part(own, other, part, SUM_PARTS, grad_passages)]
    return (loss.reshape(-1), grad_queries[0], grad_passages[0])


def solution(mesh):
    placed = (
        P(("idx", "enc"), None),
        P(("idx", "enc"), None),
        P("idx", None),
        P(("idx", "enc"), None),
    )
    return jax.shard_map(
        local,
        mesh=mesh,
        in_specs=placed,
        out_specs=(P(("idx", "enc")), P(("idx", "enc"), None), P("idx", None)),
        check_vma=False,
    )
```

```python
import functools
import math

import jax
import jax.numpy as jnp
from jax import lax
from jax.experimental import pallas as pl
from jax.experimental.pallas import tpu as pltpu
from jax.sharding import PartitionSpec as P

LSCALE = 32
DEAD = -1e30
LANES = 128
MIB = 1 << 20
GROUP_SLOTS = 256
SHARE = 0.01
QUERY_TILE = 256
QUERY_PARTS = 4
SUM_PARTS = 4
SWAP = [(0, 1), (1, 0)]


def params(vmem_mib):
    return pltpu.CompilerParams(vmem_limit_bytes=vmem_mib * MIB)


def cost(flops, bytes_accessed, transcendentals=0):
    return pl.CostEstimate(
        flops=int(flops * SHARE), bytes_accessed=int(bytes_accessed * SHARE), transcendentals=0
    )


def whole(shape):
    return pl.BlockSpec(shape, lambda *_: (0,) * len(shape))


SCALAR = pl.BlockSpec(memory_space=pltpu.SMEM)
UNREAD = pl.BlockSpec(memory_space=pl.ANY)
IN_VMEM = pl.BlockSpec(memory_space=pltpu.VMEM)


def request_kernel(shard_rows, ids_ref, out_ref):
    shards, capacity = out_ref.shape
    count = ids_ref.shape[1]
    ids = ids_ref[...]
    base = lax.broadcasted_iota(jnp.int32, (shards, 1), 0) * shard_rows
    row = ids - base
    mine = (row >= 0) & (row < shard_rows)
    one = jnp.where(mine, 1.0, 0.0)
    high = jnp.where(mine, row // 128, 0).astype(jnp.float32)
    low = jnp.where(mine, row % 128, 0).astype(jnp.float32)
    before = (
        lax.broadcasted_iota(jnp.int32, (LANES, LANES), 0)
        < lax.broadcasted_iota(jnp.int32, (LANES, LANES), 1)
    ).astype(jnp.bfloat16)
    carry = jnp.zeros((shards, 1), jnp.float32)
    places = []
    for start in range(0, count, LANES):
        part = one[:, start : start + LANES]
        inside = jnp.dot(part.astype(jnp.bfloat16), before, preferred_element_type=jnp.float32)
        rank = jnp.sum(part * (inside + carry), axis=0, keepdims=True)
        carry = carry + jnp.sum(part, axis=1, keepdims=True)
        slot = lax.broadcasted_iota(jnp.int32, (capacity, LANES), 0).astype(jnp.float32)
        places.append(jnp.where(slot == rank, 1.0, 0.0))
    place = jnp.concatenate(places, axis=1).astype(jnp.bfloat16)
    parts = jnp.concatenate([one, high, low], axis=0).astype(jnp.bfloat16)
    packed = lax.dot_general(
        parts, place, (((1,), (1,)), ((), ())), preferred_element_type=jnp.float32
    )
    filled = packed[:shards] > 0.5
    rows = packed[shards : 2 * shards] * 128.0 + packed[2 * shards :]
    out_ref[...] = jnp.where(filled, rows.astype(jnp.int32), -1)


def build_request(ids, shards, shard_rows):
    count = ids.shape[1]
    capacity = count // shards
    return pl.pallas_call(
        functools.partial(request_kernel, shard_rows),
        out_shape=jax.ShapeDtypeStruct((shards, capacity), jnp.int32),
        compiler_params=params(16),
        cost_estimate=cost(2 * 3 * shards * count * capacity, 16384),
        name="build_request",
    )(ids)


def set_offsets(shards):
    quarter = shards // 4
    return [*range(quarter), *range(3 * quarter, shards)]


def set_start(position, shards):
    quarter = shards // 4
    step = position // quarter
    return quarter * ((step ^ (step // 2)) & 1)


def partner_line(table_ref, me, member):
    inside, offset, _, _ = member
    start = set_start(me, table_ref.shape[0]) if inside else me
    return table_ref[pl.ds(jnp.bitwise_xor(start, offset), 1), :]


def partner_columns(table_ref, me, members):
    blocks = []
    for member in members:
        line = partner_line(table_ref, me, member).astype(jnp.float32)
        blocks.append(as_columns([line])[member[2] : member[2] + member[3]])
    return jnp.concatenate(blocks, axis=0)


def as_columns(lines):
    blocks = []
    for line in lines:
        for start in range(0, line.shape[1], LANES):
            piece = line[:, start : start + LANES]
            blocks.append(jnp.broadcast_to(piece, (LANES, piece.shape[1])).T)
    return jnp.concatenate(blocks, axis=0)


def store_blocks(refs, first, value):
    if len(refs) == 1 and len(refs[0].shape) == 3:
        size = refs[0].shape[1]
        count = value.shape[0] // size
        refs[0][first : first + count] = value.reshape(count, size, value.shape[1])
    else:
        size = refs[0].shape[0]
        for index in range(value.shape[0] // size):
            refs[first + index][...] = value[index * size : (index + 1) * size]


def block_shapes(members, width):
    ranks = members[0][3]
    if members[0][0]:
        return [jax.ShapeDtypeStruct((len(members), ranks, width), jnp.bfloat16)]
    return [jax.ShapeDtypeStruct((ranks, width), jnp.bfloat16)] * len(members)


def pick_kernel(members, place_ref, wanted_ref, passages_ref, *out_refs):
    rows = passages_ref.shape[0]
    per = max(1, GROUP_SLOTS // members[0][3])
    me = place_ref[0]
    for first in range(0, len(members), per):
        wanted = partner_columns(wanted_ref, me, members[first : first + per])
        lane = lax.broadcasted_iota(jnp.int32, wanted.shape, 1).astype(jnp.float32)
        hot = jnp.concatenate(
            [
                jnp.where(wanted == lane + float(start), 1.0, 0.0).astype(jnp.bfloat16)
                for start in range(0, rows, LANES)
            ],
            axis=1,
        )
        picked = jnp.dot(hot, passages_ref[...], preferred_element_type=jnp.float32)
        store_blocks(out_refs, first, picked.astype(jnp.bfloat16))


def pick(place, wanted, passages, members):
    rows, width = passages.shape
    slots = len(members) * members[0][3]
    shapes = block_shapes(members, width)
    return pl.pallas_call(
        functools.partial(pick_kernel, members),
        out_shape=shapes,
        in_specs=[SCALAR, IN_VMEM, IN_VMEM],
        out_specs=[IN_VMEM] * len(shapes),
        compiler_params=params(12),
        cost_estimate=cost(
            2 * slots * rows * width,
            2 * (rows + slots) * width,
        ),
        name="pick_rows",
    )(place, wanted, passages)


def logits_kernel(members, scale, place_ref, request_ref, top_ref, total_ref, queries_ref, *refs):
    fetched_refs, (exps_ref, new_top_ref, new_total_ref) = refs[:-3], refs[-3:]
    me = place_ref[0]
    live = partner_columns(request_ref, me, members) >= 0.0
    fetched = jnp.concatenate([ref[...] for ref in fetched_refs], axis=0)
    for first in range(0, queries_ref.shape[0], QUERY_TILE):
        logits = lax.dot_general(
            fetched,
            queries_ref[first : first + QUERY_TILE, :],
            (((1,), (1,)), ((), ())),
            preferred_element_type=jnp.float32,
        )
        for start in range(0, QUERY_TILE, LANES):
            lanes = slice(first + start, first + start + LANES)
            part = jnp.where(live, scale * logits[:, start : start + LANES], DEAD)
            old_top = top_ref[:, lanes]
            top = jnp.maximum(old_top, jnp.max(part, axis=0, keepdims=True))
            exps = jnp.exp(part - top)
            exps_ref[:, lanes] = exps
            new_top_ref[:, lanes] = top
            new_total_ref[:, lanes] = total_ref[:, lanes] * jnp.exp(old_top - top) + jnp.sum(
                exps, axis=0, keepdims=True
            )


def group_logits(place, request, top, total, queries, fetched, members, scale):
    width = fetched[0].shape[1]
    slots = sum(rows.shape[0] for rows in fetched)
    count = queries.shape[0]
    shape = jax.ShapeDtypeStruct((1, count), jnp.float32)
    return pl.pallas_call(
        functools.partial(logits_kernel, members, scale),
        out_shape=(jax.ShapeDtypeStruct((slots, count), jnp.float32), shape, shape),
        in_specs=[SCALAR] + [IN_VMEM] * (4 + len(fetched)),
        out_specs=(IN_VMEM,) * 3,
        compiler_params=params(14),
        cost_estimate=cost(
            2 * slots * width * count,
            2 * (slots + count) * width + 4 * slots * count,
            slots * count,
        ),
        name="group_logits",
    )(place, request, top, total, queries, *fetched)


def row_grad_kernel(capacity, factor, exps_ref, own_top_ref, top_ref, total_ref, queries_ref, *refs):
    weights_ref, *out_refs = refs
    share = factor * jnp.exp(own_top_ref[...] - top_ref[...]) / total_ref[...]
    for first in range(0, exps_ref.shape[0], GROUP_SLOTS):
        span = slice(first, first + GROUP_SLOTS)
        weights = (exps_ref[span, :] * share).astype(jnp.bfloat16)
        weights_ref[span, :] = weights
        value = jnp.dot(weights, queries_ref[...], preferred_element_type=jnp.float32)
        store_blocks(out_refs, first // capacity, value.astype(jnp.bfloat16))


def row_grad(exps, own_top, top, total, queries, members, factor):
    slots, count = exps.shape
    width = queries.shape[1]
    shapes = block_shapes(members, width)
    weights, *grads = pl.pallas_call(
        functools.partial(row_grad_kernel, members[0][3], factor),
        out_shape=[jax.ShapeDtypeStruct((slots, count), jnp.bfloat16)] + shapes,
        in_specs=[IN_VMEM] * 5,
        out_specs=[IN_VMEM] * (1 + len(shapes)),
        compiler_params=params(14),
        cost_estimate=cost(
            2 * slots * width * count, 2 * (slots + count) * width + 6 * slots * count
        ),
        name="row_grad",
    )(exps, own_top, top, total, queries)
    return weights, grads


def query_kernel(factor, sizes, pos_ref, top_ref, total_ref, positives_ref, *refs):
    weights_refs, rest = refs[: len(sizes)], refs[len(sizes) :]
    grad_ref = refs[-1]
    pos, top, total = pos_ref[...], top_ref[...], total_ref[...]
    coef = as_columns([factor * (jnp.exp(pos - top) / total - 1.0)])
    value = jnp.concatenate(
        [
            coef * positives_ref[:, start : start + LANES].astype(jnp.float32)
            for start in range(0, positives_ref.shape[1], LANES)
        ],
        axis=1,
    )
    first = 0
    for ref, size in zip(weights_refs, sizes):
        rows = jnp.concatenate([one[...] for one in rest[first : first + size]], axis=0)
        first += size
        value = value + lax.dot_general(
            ref[...], rows, (((0,), (0,)), ((), ())), preferred_element_type=jnp.float32
        )
    grad_ref[...] = value.astype(jnp.bfloat16)


def query_grad(pos, top, total, positives, weights, fetched, factor, part, grads):
    count, width = positives.shape
    tile = min(256, count // QUERY_PARTS)
    steps = count // QUERY_PARTS // tile
    first = part * steps
    line = pl.BlockSpec((1, tile), lambda t: (0, first + t))
    block = pl.BlockSpec((tile, width), lambda t: (first + t, 0))
    sizes = [len(group) for group in fetched]
    rows = [one for group in fetched for one in group]
    inputs = [pos, top, total, positives, *weights, *rows, *grads]
    slots = sum(one.shape[0] for one in weights)
    return pl.pallas_call(
        functools.partial(query_kernel, factor, sizes),
        out_shape=jax.ShapeDtypeStruct((count, width), jnp.bfloat16),
        grid=(steps,),
        in_specs=[line, line, line, block]
        + [pl.BlockSpec((one.shape[0], tile), lambda t: (0, first + t)) for one in weights]
        + [whole(one.shape) for one in rows]
        + [UNREAD] * len(grads),
        out_specs=block,
        input_output_aliases={len(inputs) - 1: 0} if grads else {},
        compiler_params=params(26),
        cost_estimate=cost(
            2 * slots * width * count // QUERY_PARTS,
            2 * slots * width + 4 * count * width // QUERY_PARTS,
        ),
        name="query_grad",
    )(*inputs)


def scatter_kernel(members, first, place_ref, wanted_ref, *refs):
    *value_refs, out_ref = refs
    base_ref = value_refs.pop(0) if value_refs[0].shape == out_ref.shape else None
    rows = out_ref.shape[0]
    me = place_ref[0]
    row = (first + pl.program_id(0)) * rows + lax.broadcasted_iota(jnp.int32, (rows, 1), 0)
    wanted = jnp.concatenate(
        [partner_line(wanted_ref, me, m)[:, m[2] : m[2] + m[3]] for m in members], axis=1
    )
    hot = jnp.where(wanted == row, 1.0, 0.0).astype(jnp.bfloat16)
    values = jnp.concatenate([ref[...] for ref in value_refs], axis=0)
    total = jnp.dot(hot, values, preferred_element_type=jnp.float32)
    if base_ref is not None:
        total = base_ref[...] + total
    out_ref[...] = total.astype(out_ref.dtype)


def scatter(place, wanted, values, members, base, shard_rows, part, parts, dtype):
    width = values[0].shape[1]
    slots = sum(one.shape[0] for one in values)
    rows = shard_rows // parts
    tile = 2 * LANES
    first = part * rows // tile
    return pl.pallas_call(
        functools.partial(scatter_kernel, members, first),
        out_shape=jax.ShapeDtypeStruct((rows, width), dtype),
        grid=(rows // tile,),
        in_specs=[SCALAR, whole(wanted.shape)]
        + [pl.BlockSpec((tile, width), lambda t: (first + t, 0))] * len(base)
        + [whole(one.shape) for one in values],
        out_specs=pl.BlockSpec((tile, width), lambda t: (t, 0)),
        compiler_params=params(18),
        cost_estimate=cost(
            2 * rows * slots * width, 2 * slots * width + 4 * (1 + len(base)) * rows * width
        ),
        name="scatter_rows",
    )(place, wanted, *base, *values)


def add_kernel(own_ref, other_ref, *refs):
    refs[-1][...] = (
        own_ref[...].astype(jnp.float32) + other_ref[...].astype(jnp.float32)
    ).astype(jnp.bfloat16)


def add_part(own, other, part, parts, sums):
    rows, width = own.shape
    tile = min(256, rows)
    first = part * rows // tile
    block = pl.BlockSpec((tile, width), lambda t: (t, 0))
    return pl.pallas_call(
        add_kernel,
        out_shape=jax.ShapeDtypeStruct((rows * parts, width), jnp.bfloat16),
        grid=(rows // tile,),
        in_specs=[block, block] + [UNREAD] * len(sums),
        out_specs=pl.BlockSpec((tile, width), lambda t: (first + t, 0)),
        input_output_aliases={2: 0} if sums else {},
        compiler_params=params(16),
        cost_estimate=cost(rows * width, 6 * rows * width),
        name="add_cores",
    )(own, other, *sums)


def behind(value, earlier):
    if not earlier:
        return value
    return lax.optimization_barrier((value, *earlier))[0]


def exchange(blocks, members, shards):
    if members[0][0]:
        offsets = set_offsets(shards)
        sets = [[start ^ o for o in offsets] for start in (0, shards // 4)]
        block = lax.all_to_all(
            blocks[0], "idx", split_axis=0, concat_axis=0, tiled=True, axis_index_groups=sets
        )
        return [block.reshape(-1, block.shape[-1])]
    return [
        lax.ppermute(block, "idx", [(i, i ^ offset) for i in range(shards)])
        for block, (_, offset, _, _) in zip(blocks, members)
    ]


def local(queries, positives, passages, negatives):
    shards = lax.axis_size("idx")
    shard_rows, width = passages.shape
    ids = negatives.reshape(1, -1)
    capacity = ids.shape[1] // shards
    scale = 3.0 / math.sqrt(width)
    factor = LSCALE * scale
    quarter = shards // 4
    per = min(quarter, GROUP_SLOTS // capacity)
    far, near = [
        [
            tuple((False, start + o + i, 0, capacity) for i in range(per))
            for o in range(0, quarter, per)
        ]
        for start in (2 * quarter, quarter)
    ]
    half = capacity // 2
    set_one, set_two = [
        tuple((True, o, rank, half) for o in set_offsets(shards)) for rank in (0, half)
    ]
    place = lax.axis_index("idx").astype(jnp.int32).reshape(1)

    request = build_request(ids, shards, shard_rows)
    wanted = lax.all_to_all(request, "idx", split_axis=0, concat_axis=0, tiled=True)
    pos_logit = scale * jnp.sum(
        queries.astype(jnp.float32) * positives.astype(jnp.float32), axis=1
    )
    pos_logit = pos_logit.reshape(1, -1)

    order = [set_one, *near, *far, set_two]

    def exchanged(blocks, before):
        received = {}
        for group in [set_one, *near]:
            received[group] = exchange(blocks[group], group, shards)
        arrived = [one for group in near for one in received[group]]
        sent = [one for group in far for one in blocks[group]]
        tied = [sent[0]]
        for index, one in enumerate(sent[1:]):
            tied.append(behind(one, arrived[index : index + 1] + before(index)))
        for index, group in enumerate(far):
            received[group] = exchange(tied[index * per : (index + 1) * per], group, shards)
        last = [behind(blocks[set_two][0], received[set_one] + before(len(sent) - 1))]
        received[set_two] = exchange(last, set_two, shards)
        return received

    picked, last = {}, [pos_logit]
    for group in order:
        picked[group] = pick(behind(place, last), wanted, passages, group)
        last = picked[group][-1:]
    fetched = exchanged(picked, lambda index: [])

    worked = [*near, set_one, *far, set_two]
    top, total = pos_logit, jnp.ones_like(pos_logit)
    exps, tops = {}, {}
    for group in worked:
        exps[group], top, total = group_logits(
            place, request, top, total, queries, fetched[group], group, scale
        )
        tops[group] = top
    loss = top + jnp.log(total) - pos_logit

    weights, grads, last = {}, {}, []
    for group in order:
        weights[group], grads[group] = row_grad(
            exps[group], behind(tops[group], last), top, total, queries, group, factor
        )
        last = grads[group][-1:]

    grad_queries = []
    for part in range(QUERY_PARTS):
        done = [
            query_grad(
                pos_logit,
                top,
                total,
                positives,
                [weights[group] for group in worked],
                [fetched[group] for group in worked],
                factor,
                part,
                grad_queries[-1:],
            )
        ]
        grad_queries += done
    steps = quarter // QUERY_PARTS
    returned = exchanged(
        grads,
        lambda index: [grad_queries[(index + 1) // steps - 1]] if (index + 1) % steps == 0 else [],
    )

    base = []
    for groups in (near, [set_one], far):
        base = [
            scatter(
                place,
                wanted,
                [one for group in groups for one in returned[group]],
                sum(groups, ()),
                base,
                shard_rows,
                0,
                1,
                jnp.float32,
            )
        ]
    late = [behind(returned[set_two][0], base)]
    grad_passages = []
    parts = [
        scatter(place, wanted, late, set_two, base, shard_rows, part, SUM_PARTS, jnp.bfloat16)
        for part in range(SUM_PARTS)
    ]
    for part, own in enumerate(parts):
        other = lax.ppermute(own, "enc", SWAP)
        grad_passages = [add_part(own, other, part, SUM_PARTS, grad_passages)]
    return (loss.reshape(-1), grad_queries[-1], grad_passages[0])


def solution(mesh):
    placed = (
        P(("idx", "enc"), None),
        P(("idx", "enc"), None),
        P("idx", None),
        P(("idx", "enc"), None),
    )
    return jax.shard_map(
        local,
        mesh=mesh,
        in_specs=placed,
        out_specs=(P(("idx", "enc")), P(("idx", "enc"), None), P("idx", None)),
        check_vma=False,
    )
```

```python
import functools
import math

import jax
import jax.numpy as jnp
from jax import lax
from jax.experimental import pallas as pl
from jax.experimental.pallas import tpu as pltpu
from jax.sharding import PartitionSpec as P

LSCALE = 32
DEAD = -1e30
LANES = 128
MIB = 1 << 20
GROUP_SLOTS = 256
SHARE = 0.01
QUERY_TILE = 256
QUERY_PARTS = 2
SUM_PARTS = 4
SWAP = [(0, 1), (1, 0)]


def params(vmem_mib):
    return pltpu.CompilerParams(vmem_limit_bytes=vmem_mib * MIB)


def cost(flops, bytes_accessed, transcendentals=0):
    return pl.CostEstimate(
        flops=int(flops * SHARE), bytes_accessed=int(bytes_accessed * SHARE), transcendentals=0
    )


def whole(shape):
    return pl.BlockSpec(shape, lambda *_: (0,) * len(shape))


SCALAR = pl.BlockSpec(memory_space=pltpu.SMEM)
UNREAD = pl.BlockSpec(memory_space=pl.ANY)
IN_VMEM = pl.BlockSpec(memory_space=pltpu.VMEM)


def request_kernel(shard_rows, ids_ref, out_ref):
    shards, capacity = out_ref.shape
    count = ids_ref.shape[1]
    ids = ids_ref[...]
    base = lax.broadcasted_iota(jnp.int32, (shards, 1), 0) * shard_rows
    row = ids - base
    mine = (row >= 0) & (row < shard_rows)
    one = jnp.where(mine, 1.0, 0.0)
    high = jnp.where(mine, row // 128, 0).astype(jnp.float32)
    low = jnp.where(mine, row % 128, 0).astype(jnp.float32)
    before = (
        lax.broadcasted_iota(jnp.int32, (LANES, LANES), 0)
        < lax.broadcasted_iota(jnp.int32, (LANES, LANES), 1)
    ).astype(jnp.bfloat16)
    carry = jnp.zeros((shards, 1), jnp.float32)
    places = []
    for start in range(0, count, LANES):
        part = one[:, start : start + LANES]
        inside = jnp.dot(part.astype(jnp.bfloat16), before, preferred_element_type=jnp.float32)
        rank = jnp.sum(part * (inside + carry), axis=0, keepdims=True)
        carry = carry + jnp.sum(part, axis=1, keepdims=True)
        slot = lax.broadcasted_iota(jnp.int32, (capacity, LANES), 0).astype(jnp.float32)
        places.append(jnp.where(slot == rank, 1.0, 0.0))
    place = jnp.concatenate(places, axis=1).astype(jnp.bfloat16)
    parts = jnp.concatenate([one, high, low], axis=0).astype(jnp.bfloat16)
    packed = lax.dot_general(
        parts, place, (((1,), (1,)), ((), ())), preferred_element_type=jnp.float32
    )
    filled = packed[:shards] > 0.5
    rows = packed[shards : 2 * shards] * 128.0 + packed[2 * shards :]
    out_ref[...] = jnp.where(filled, rows.astype(jnp.int32), -1)


def build_request(ids, shards, shard_rows):
    count = ids.shape[1]
    capacity = count // shards
    return pl.pallas_call(
        functools.partial(request_kernel, shard_rows),
        out_shape=jax.ShapeDtypeStruct((shards, capacity), jnp.int32),
        compiler_params=params(16),
        cost_estimate=cost(2 * 3 * shards * count * capacity, 16384),
        name="build_request",
    )(ids)


def set_offsets(shards):
    quarter = shards // 4
    return [*range(quarter), *range(3 * quarter, shards)]


def set_start(position, shards):
    quarter = shards // 4
    step = position // quarter
    return quarter * ((step ^ (step // 2)) & 1)


def partner_line(table_ref, me, member):
    inside, offset, _, _ = member
    start = set_start(me, table_ref.shape[0]) if inside else me
    return table_ref[pl.ds(jnp.bitwise_xor(start, offset), 1), :]


def partner_columns(table_ref, me, members):
    blocks = []
    for member in members:
        line = partner_line(table_ref, me, member).astype(jnp.float32)
        blocks.append(as_columns([line])[member[2] : member[2] + member[3]])
    return jnp.concatenate(blocks, axis=0)


def as_columns(lines):
    blocks = []
    for line in lines:
        for start in range(0, line.shape[1], LANES):
            piece = line[:, start : start + LANES]
            blocks.append(jnp.broadcast_to(piece, (LANES, piece.shape[1])).T)
    return jnp.concatenate(blocks, axis=0)


def store_blocks(refs, first, value):
    if len(refs) == 1 and len(refs[0].shape) == 3:
        size = refs[0].shape[1]
        count = value.shape[0] // size
        refs[0][first : first + count] = value.reshape(count, size, value.shape[1])
    else:
        size = refs[0].shape[0]
        for index in range(value.shape[0] // size):
            refs[first + index][...] = value[index * size : (index + 1) * size]


def block_shapes(members, width):
    ranks = members[0][3]
    if members[0][0]:
        return [jax.ShapeDtypeStruct((len(members), ranks, width), jnp.bfloat16)]
    return [jax.ShapeDtypeStruct((ranks, width), jnp.bfloat16)] * len(members)


def pick_kernel(members, place_ref, wanted_ref, passages_ref, *out_refs):
    rows = passages_ref.shape[0]
    per = max(1, GROUP_SLOTS // members[0][3])
    me = place_ref[0]
    for first in range(0, len(members), per):
        wanted = partner_columns(wanted_ref, me, members[first : first + per])
        lane = lax.broadcasted_iota(jnp.int32, wanted.shape, 1).astype(jnp.float32)
        hot = jnp.concatenate(
            [
                jnp.where(wanted == lane + float(start), 1.0, 0.0).astype(jnp.bfloat16)
                for start in range(0, rows, LANES)
            ],
            axis=1,
        )
        picked = jnp.dot(hot, passages_ref[...], preferred_element_type=jnp.float32)
        store_blocks(out_refs, first, picked.astype(jnp.bfloat16))


def pick(place, wanted, passages, members):
    rows, width = passages.shape
    slots = len(members) * members[0][3]
    shapes = block_shapes(members, width)
    return pl.pallas_call(
        functools.partial(pick_kernel, members),
        out_shape=shapes,
        in_specs=[SCALAR, IN_VMEM, IN_VMEM],
        out_specs=[IN_VMEM] * len(shapes),
        compiler_params=params(12),
        cost_estimate=cost(
            2 * slots * rows * width,
            2 * (rows + slots) * width,
        ),
        name="pick_rows",
    )(place, wanted, passages)


def logits_kernel(members, scale, place_ref, request_ref, top_ref, total_ref, queries_ref, *refs):
    fetched_refs, (exps_ref, new_top_ref, new_total_ref) = refs[:-3], refs[-3:]
    me = place_ref[0]
    live = partner_columns(request_ref, me, members) >= 0.0
    fetched = jnp.concatenate([ref[...] for ref in fetched_refs], axis=0)
    for first in range(0, queries_ref.shape[0], QUERY_TILE):
        logits = lax.dot_general(
            fetched,
            queries_ref[first : first + QUERY_TILE, :],
            (((1,), (1,)), ((), ())),
            preferred_element_type=jnp.float32,
        )
        for start in range(0, QUERY_TILE, LANES):
            lanes = slice(first + start, first + start + LANES)
            part = jnp.where(live, scale * logits[:, start : start + LANES], DEAD)
            old_top = top_ref[:, lanes]
            top = jnp.maximum(old_top, jnp.max(part, axis=0, keepdims=True))
            exps = jnp.exp(part - top)
            exps_ref[:, lanes] = exps.astype(exps_ref.dtype)
            new_top_ref[:, lanes] = top
            new_total_ref[:, lanes] = total_ref[:, lanes] * jnp.exp(old_top - top) + jnp.sum(
                exps, axis=0, keepdims=True
            )


def group_logits(place, request, top, total, queries, fetched, members, scale):
    width = fetched[0].shape[1]
    slots = sum(rows.shape[0] for rows in fetched)
    count = queries.shape[0]
    shape = jax.ShapeDtypeStruct((1, count), jnp.float32)
    return pl.pallas_call(
        functools.partial(logits_kernel, members, scale),
        out_shape=(jax.ShapeDtypeStruct((slots, count), jnp.bfloat16), shape, shape),
        in_specs=[SCALAR] + [IN_VMEM] * (4 + len(fetched)),
        out_specs=(IN_VMEM,) * 3,
        compiler_params=params(14),
        cost_estimate=cost(
            2 * slots * width * count,
            2 * (slots + count) * width + 4 * slots * count,
            slots * count,
        ),
        name="group_logits",
    )(place, request, top, total, queries, *fetched)


def row_grad_kernel(capacity, factor, exps_ref, own_top_ref, top_ref, total_ref, queries_ref, *refs):
    weights_ref, *out_refs = refs
    share = factor * jnp.exp(own_top_ref[...] - top_ref[...]) / total_ref[...]
    for first in range(0, exps_ref.shape[0], GROUP_SLOTS):
        span = slice(first, first + GROUP_SLOTS)
        weights = (exps_ref[span, :].astype(jnp.float32) * share).astype(jnp.bfloat16)
        weights_ref[span, :] = weights
        value = jnp.dot(weights, queries_ref[...], preferred_element_type=jnp.float32)
        store_blocks(out_refs, first // capacity, value.astype(jnp.bfloat16))


def row_grad(exps, own_top, top, total, queries, members, factor):
    slots, count = exps.shape
    width = queries.shape[1]
    shapes = block_shapes(members, width)
    weights, *grads = pl.pallas_call(
        functools.partial(row_grad_kernel, members[0][3], factor),
        out_shape=[jax.ShapeDtypeStruct((slots, count), jnp.bfloat16)] + shapes,
        in_specs=[IN_VMEM] * 5,
        out_specs=[IN_VMEM] * (1 + len(shapes)),
        compiler_params=params(14),
        cost_estimate=cost(
            2 * slots * width * count, 2 * (slots + count) * width + 6 * slots * count
        ),
        name="row_grad",
    )(exps, own_top, top, total, queries)
    return weights, grads


def query_kernel(factor, sizes, pos_ref, top_ref, total_ref, positives_ref, *refs):
    weights_refs, rest = refs[: len(sizes)], refs[len(sizes) :]
    grad_ref = refs[-1]
    pos, top, total = pos_ref[...], top_ref[...], total_ref[...]
    coef = as_columns([factor * (jnp.exp(pos - top) / total - 1.0)])
    value = jnp.concatenate(
        [
            coef * positives_ref[:, start : start + LANES].astype(jnp.float32)
            for start in range(0, positives_ref.shape[1], LANES)
        ],
        axis=1,
    )
    first = 0
    for ref, size in zip(weights_refs, sizes):
        rows = jnp.concatenate([one[...] for one in rest[first : first + size]], axis=0)
        first += size
        value = value + lax.dot_general(
            ref[...], rows, (((0,), (0,)), ((), ())), preferred_element_type=jnp.float32
        )
    grad_ref[...] = value.astype(jnp.bfloat16)


def query_grad(pos, top, total, positives, weights, fetched, factor, part, grads):
    count, width = positives.shape
    tile = min(256, count // QUERY_PARTS)
    steps = count // QUERY_PARTS // tile
    first = part * steps
    line = pl.BlockSpec((1, tile), lambda t: (0, first + t))
    block = pl.BlockSpec((tile, width), lambda t: (first + t, 0))
    sizes = [len(group) for group in fetched]
    rows = [one for group in fetched for one in group]
    inputs = [pos, top, total, positives, *weights, *rows, *grads]
    slots = sum(one.shape[0] for one in weights)
    return pl.pallas_call(
        functools.partial(query_kernel, factor, sizes),
        out_shape=jax.ShapeDtypeStruct((count, width), jnp.bfloat16),
        grid=(steps,),
        in_specs=[line, line, line, block]
        + [pl.BlockSpec((one.shape[0], tile), lambda t: (0, first + t)) for one in weights]
        + [whole(one.shape) for one in rows]
        + [UNREAD] * len(grads),
        out_specs=block,
        input_output_aliases={len(inputs) - 1: 0} if grads else {},
        compiler_params=params(26),
        cost_estimate=cost(
            2 * slots * width * count // QUERY_PARTS,
            2 * slots * width + 4 * count * width // QUERY_PARTS,
        ),
        name="query_grad",
    )(*inputs)


def scatter_kernel(members, first, place_ref, wanted_ref, *refs):
    *value_refs, out_ref = refs
    base_ref = value_refs.pop(0) if value_refs[0].shape == out_ref.shape else None
    rows = out_ref.shape[0]
    me = place_ref[0]
    row = (first + pl.program_id(0)) * rows + lax.broadcasted_iota(jnp.int32, (rows, 1), 0)
    wanted = jnp.concatenate(
        [partner_line(wanted_ref, me, m)[:, m[2] : m[2] + m[3]] for m in members], axis=1
    )
    hot = jnp.where(wanted == row, 1.0, 0.0).astype(jnp.bfloat16)
    values = jnp.concatenate([ref[...] for ref in value_refs], axis=0)
    total = jnp.dot(hot, values, preferred_element_type=jnp.float32)
    if base_ref is not None:
        total = base_ref[...] + total
    out_ref[...] = total.astype(out_ref.dtype)


def scatter(place, wanted, values, members, base, shard_rows, part, parts, dtype):
    width = values[0].shape[1]
    slots = sum(one.shape[0] for one in values)
    rows = shard_rows // parts
    tile = 2 * LANES
    first = part * rows // tile
    return pl.pallas_call(
        functools.partial(scatter_kernel, members, first),
        out_shape=jax.ShapeDtypeStruct((rows, width), dtype),
        grid=(rows // tile,),
        in_specs=[SCALAR, whole(wanted.shape)]
        + [pl.BlockSpec((tile, width), lambda t: (first + t, 0))] * len(base)
        + [whole(one.shape) for one in values],
        out_specs=pl.BlockSpec((tile, width), lambda t: (t, 0)),
        compiler_params=params(18),
        cost_estimate=cost(
            2 * rows * slots * width, 2 * slots * width + 4 * (1 + len(base)) * rows * width
        ),
        name="scatter_rows",
    )(place, wanted, *base, *values)


def add_kernel(own_ref, other_ref, *refs):
    refs[-1][...] = (
        own_ref[...].astype(jnp.float32) + other_ref[...].astype(jnp.float32)
    ).astype(jnp.bfloat16)


def add_part(own, other, part, parts, sums):
    rows, width = own.shape
    tile = min(256, rows)
    first = part * rows // tile
    block = pl.BlockSpec((tile, width), lambda t: (t, 0))
    return pl.pallas_call(
        add_kernel,
        out_shape=jax.ShapeDtypeStruct((rows * parts, width), jnp.bfloat16),
        grid=(rows // tile,),
        in_specs=[block, block] + [UNREAD] * len(sums),
        out_specs=pl.BlockSpec((tile, width), lambda t: (first + t, 0)),
        input_output_aliases={2: 0} if sums else {},
        compiler_params=params(16),
        cost_estimate=cost(rows * width, 6 * rows * width),
        name="add_cores",
    )(own, other, *sums)


def behind(value, earlier):
    if not earlier:
        return value
    return lax.optimization_barrier((value, *earlier))[0]


def exchange(blocks, members, shards):
    if members[0][0]:
        offsets = set_offsets(shards)
        sets = [[start ^ o for o in offsets] for start in (0, shards // 4)]
        block = lax.all_to_all(
            blocks[0], "idx", split_axis=0, concat_axis=0, tiled=True, axis_index_groups=sets
        )
        return [block.reshape(-1, block.shape[-1])]
    return [
        lax.ppermute(block, "idx", [(i, i ^ offset) for i in range(shards)])
        for block, (_, offset, _, _) in zip(blocks, members)
    ]


def local(queries, positives, passages, negatives):
    shards = lax.axis_size("idx")
    shard_rows, width = passages.shape
    ids = negatives.reshape(1, -1)
    capacity = ids.shape[1] // shards
    scale = 3.0 / math.sqrt(width)
    factor = LSCALE * scale
    quarter = shards // 4
    per = min(quarter, GROUP_SLOTS // capacity)
    far, near = [
        [
            tuple((False, start + o + i, 0, capacity) for i in range(per))
            for o in range(0, quarter, per)
        ]
        for start in (2 * quarter, quarter)
    ]
    within = tuple((True, o, 0, capacity) for o in set_offsets(shards))
    place = lax.axis_index("idx").astype(jnp.int32).reshape(1)

    request = build_request(ids, shards, shard_rows)
    wanted = lax.all_to_all(request, "idx", split_axis=0, concat_axis=0, tiled=True)
    pos_logit = scale * jnp.sum(
        queries.astype(jnp.float32) * positives.astype(jnp.float32), axis=1
    )
    pos_logit = pos_logit.reshape(1, -1)

    order = [within, *near, *far]

    def exchanged(blocks, before):
        received = {}
        for group in [within, *near]:
            received[group] = exchange(blocks[group], group, shards)
        arrived = [one for group in near for one in received[group]]
        sent = [one for group in far for one in blocks[group]]
        for index in range(1, len(sent)):
            earlier = arrived[index - 1 : index + 1] + before(index, received)
            sent[index] = behind(sent[index], earlier)
        for index, group in enumerate(far):
            received[group] = exchange(sent[index * per : (index + 1) * per], group, shards)
        return received

    picked, last = {}, [pos_logit]
    for group in order:
        picked[group] = pick(behind(place, last), wanted, passages, group)
        last = picked[group][-1:]

    stats = [(pos_logit, jnp.ones_like(pos_logit))]
    exps, tops = {}, {}

    def logits_of(group, received):
        top, total = stats[-1]
        exps[group], top, total = group_logits(
            place, request, top, total, queries, received[group], group, scale
        )
        tops[group] = top
        stats.append((top, total))
        return top

    def near_logits(index, received):
        group, rest = divmod(index, quarter // len(near))
        return [logits_of(near[group - 1], received)] if rest == 0 else []

    fetched = exchanged(picked, near_logits)
    for group in [near[-1], *far, within]:
        logits_of(group, fetched)
    top, total = stats[-1]
    loss = top + jnp.log(total) - pos_logit

    weights, grads, last = {}, {}, []
    for group in order:
        weights[group], grads[group] = row_grad(
            exps[group], behind(tops[group], last), top, total, queries, group, factor
        )
        last = grads[group][-1:]

    grad_queries = []
    for part in range(QUERY_PARTS):
        done = query_grad(
            pos_logit,
            top,
            total,
            positives,
            [weights[group] for group in order],
            [fetched[group] for group in order],
            factor,
            part,
            grad_queries[-1:],
        )
        grad_queries.append(done)

    def query_parts(index, received):
        part = index - (quarter - QUERY_PARTS)
        return [grad_queries[part]] if part >= 0 else []

    returned = exchanged(grads, query_parts)

    apart = [*near, *far]
    base = [
        scatter(
            place,
            wanted,
            [one for group in apart for one in returned[group]],
            sum(apart, ()),
            [],
            shard_rows,
            0,
            1,
            jnp.float32,
        )
    ]
    late = [behind(returned[within][0], base)]
    grad_passages = []
    parts = [
        scatter(place, wanted, late, within, base, shard_rows, part, SUM_PARTS, jnp.bfloat16)
        for part in range(SUM_PARTS)
    ]
    for part, own in enumerate(parts):
        other = lax.ppermute(own, "enc", SWAP)
        grad_passages = [add_part(own, other, part, SUM_PARTS, grad_passages)]
    return (loss.reshape(-1), grad_queries[-1], grad_passages[0])


def solution(mesh):
    placed = (
        P(("idx", "enc"), None),
        P(("idx", "enc"), None),
        P("idx", None),
        P(("idx", "enc"), None),
    )
    return jax.shard_map(
        local,
        mesh=mesh,
        in_specs=placed,
        out_specs=(P(("idx", "enc")), P(("idx", "enc"), None), P("idx", None)),
        check_vma=False,
    )
```

```python
import functools
import math

import jax
import jax.numpy as jnp
from jax import lax
from jax.experimental import pallas as pl
from jax.experimental.pallas import tpu as pltpu
from jax.sharding import PartitionSpec as P

LSCALE = 32
DEAD = -1e30
LANES = 128
MIB = 1 << 20
GROUP_SLOTS = 256
SHARE = 0.01
QUERY_TILE = 256
QUERY_PARTS = 2
SUM_PARTS = 4
SWAP = [(0, 1), (1, 0)]


def params(vmem_mib):
    return pltpu.CompilerParams(vmem_limit_bytes=vmem_mib * MIB)


def cost(flops, bytes_accessed, transcendentals=0):
    return pl.CostEstimate(
        flops=int(flops * SHARE), bytes_accessed=int(bytes_accessed * SHARE), transcendentals=0
    )


def whole(shape):
    return pl.BlockSpec(shape, lambda *_: (0,) * len(shape))


STREAM_MIB = 56
SCALAR = pl.BlockSpec(memory_space=pltpu.SMEM)
UNREAD = pl.BlockSpec(memory_space=pl.ANY)
IN_VMEM = pl.BlockSpec(memory_space=pltpu.VMEM)


def request_kernel(shard_rows, ids_ref, out_ref):
    shards, capacity = out_ref.shape
    count = ids_ref.shape[1]
    ids = ids_ref[...]
    base = lax.broadcasted_iota(jnp.int32, (shards, 1), 0) * shard_rows
    row = ids - base
    mine = (row >= 0) & (row < shard_rows)
    one = jnp.where(mine, 1.0, 0.0)
    high = jnp.where(mine, row // 128, 0).astype(jnp.float32)
    low = jnp.where(mine, row % 128, 0).astype(jnp.float32)
    before = (
        lax.broadcasted_iota(jnp.int32, (LANES, LANES), 0)
        < lax.broadcasted_iota(jnp.int32, (LANES, LANES), 1)
    ).astype(jnp.bfloat16)
    carry = jnp.zeros((shards, 1), jnp.float32)
    places = []
    for start in range(0, count, LANES):
        part = one[:, start : start + LANES]
        inside = jnp.dot(part.astype(jnp.bfloat16), before, preferred_element_type=jnp.float32)
        rank = jnp.sum(part * (inside + carry), axis=0, keepdims=True)
        carry = carry + jnp.sum(part, axis=1, keepdims=True)
        slot = lax.broadcasted_iota(jnp.int32, (capacity, LANES), 0).astype(jnp.float32)
        places.append(jnp.where(slot == rank, 1.0, 0.0))
    place = jnp.concatenate(places, axis=1).astype(jnp.bfloat16)
    parts = jnp.concatenate([one, high, low], axis=0).astype(jnp.bfloat16)
    packed = lax.dot_general(
        parts, place, (((1,), (1,)), ((), ())), preferred_element_type=jnp.float32
    )
    filled = packed[:shards] > 0.5
    rows = packed[shards : 2 * shards] * 128.0 + packed[2 * shards :]
    out_ref[...] = jnp.where(filled, rows.astype(jnp.int32), -1)


def build_request(ids, shards, shard_rows):
    count = ids.shape[1]
    capacity = count // shards
    return pl.pallas_call(
        functools.partial(request_kernel, shard_rows),
        out_shape=jax.ShapeDtypeStruct((shards, capacity), jnp.int32),
        compiler_params=params(16),
        cost_estimate=cost(2 * 3 * shards * count * capacity, 16384),
        name="build_request",
    )(ids)


def set_offsets(shards):
    quarter = shards // 4
    return [*range(quarter), *range(3 * quarter, shards)]


def set_start(position, shards):
    quarter = shards // 4
    step = position // quarter
    return quarter * ((step ^ (step // 2)) & 1)


def partner_line(table_ref, me, member):
    inside, offset, _, _ = member
    start = set_start(me, table_ref.shape[0]) if inside else me
    return table_ref[pl.ds(jnp.bitwise_xor(start, offset), 1), :]


def partner_columns(table_ref, me, members):
    blocks = []
    for member in members:
        line = partner_line(table_ref, me, member).astype(jnp.float32)
        blocks.append(as_columns([line])[member[2] : member[2] + member[3]])
    return jnp.concatenate(blocks, axis=0)


def as_columns(lines):
    blocks = []
    for line in lines:
        for start in range(0, line.shape[1], LANES):
            piece = line[:, start : start + LANES]
            blocks.append(jnp.broadcast_to(piece, (LANES, piece.shape[1])).T)
    return jnp.concatenate(blocks, axis=0)


def store_blocks(refs, first, value):
    if len(refs) == 1 and len(refs[0].shape) == 3:
        size = refs[0].shape[1]
        count = value.shape[0] // size
        refs[0][first : first + count] = value.reshape(count, size, value.shape[1])
    else:
        size = refs[0].shape[0]
        for index in range(value.shape[0] // size):
            refs[first + index][...] = value[index * size : (index + 1) * size]


def block_shapes(members, width):
    ranks = members[0][3]
    if members[0][0]:
        return [jax.ShapeDtypeStruct((len(members), ranks, width), jnp.bfloat16)]
    return [jax.ShapeDtypeStruct((ranks, width), jnp.bfloat16)] * len(members)


def pick_kernel(members, place_ref, wanted_ref, passages_ref, *out_refs):
    rows = passages_ref.shape[0]
    per = max(1, GROUP_SLOTS // members[0][3])
    me = place_ref[0]
    for first in range(0, len(members), per):
        wanted = partner_columns(wanted_ref, me, members[first : first + per])
        lane = lax.broadcasted_iota(jnp.int32, wanted.shape, 1).astype(jnp.float32)
        hot = jnp.concatenate(
            [
                jnp.where(wanted == lane + float(start), 1.0, 0.0).astype(jnp.bfloat16)
                for start in range(0, rows, LANES)
            ],
            axis=1,
        )
        picked = jnp.dot(hot, passages_ref[...], preferred_element_type=jnp.float32)
        store_blocks(out_refs, first, picked.astype(jnp.bfloat16))


def pick(place, wanted, passages, members):
    rows, width = passages.shape
    slots = len(members) * members[0][3]
    shapes = block_shapes(members, width)
    return pl.pallas_call(
        functools.partial(pick_kernel, members),
        out_shape=shapes,
        in_specs=[SCALAR, IN_VMEM, IN_VMEM],
        out_specs=[IN_VMEM] * len(shapes),
        compiler_params=params(12),
        cost_estimate=cost(
            2 * slots * rows * width,
            2 * (rows + slots) * width,
        ),
        name="pick_rows",
    )(place, wanted, passages)


def logits_kernel(members, scale, place_ref, request_ref, top_ref, total_ref, queries_ref, *refs):
    fetched_refs, (exps_ref, new_top_ref, new_total_ref, live_ref) = refs[:-4], refs[-4:]

    @pl.when(pl.program_id(0) == 0)
    def _():
        live_ref[...] = partner_columns(request_ref, place_ref[0], members)

    fetched = jnp.concatenate([ref[...] for ref in fetched_refs], axis=0)
    logits = lax.dot_general(
        fetched, queries_ref[...], (((1,), (1,)), ((), ())), preferred_element_type=jnp.float32
    )
    for start in range(0, logits.shape[1], LANES):
        lanes = slice(start, start + LANES)
        part = jnp.where(live_ref[...] >= 0.0, scale * logits[:, lanes], DEAD)
        old_top = top_ref[:, lanes]
        top = jnp.maximum(old_top, jnp.max(part, axis=0, keepdims=True))
        exps = jnp.exp(part - top)
        exps_ref[:, lanes] = exps.astype(exps_ref.dtype)
        new_top_ref[:, lanes] = top
        new_total_ref[:, lanes] = total_ref[:, lanes] * jnp.exp(old_top - top) + jnp.sum(
            exps, axis=0, keepdims=True
        )


def group_logits(place, request, top, total, queries, fetched, members, scale):
    width = fetched[0].shape[1]
    slots = sum(rows.shape[0] for rows in fetched)
    count = queries.shape[0]
    tile = min(QUERY_TILE, count)
    shape = jax.ShapeDtypeStruct((1, count), jnp.float32)
    line = pl.BlockSpec((1, tile), lambda t: (0, t))
    return pl.pallas_call(
        functools.partial(logits_kernel, members, scale),
        out_shape=(jax.ShapeDtypeStruct((slots, count), jnp.bfloat16), shape, shape),
        grid=(count // tile,),
        in_specs=[
            SCALAR,
            whole(request.shape),
            line,
            line,
            pl.BlockSpec((tile, width), lambda t: (t, 0)),
        ]
        + [whole(rows.shape) for rows in fetched],
        out_specs=(pl.BlockSpec((slots, tile), lambda t: (0, t)), line, line),
        scratch_shapes=[pltpu.VMEM((slots, LANES), jnp.float32)],
        compiler_params=params(STREAM_MIB),
        cost_estimate=cost(
            2 * slots * width * count,
            2 * (slots + count) * width + 4 * slots * count,
            slots * count,
        ),
        name="group_logits",
    )(place, request, top, total, queries, *fetched)


def row_grad_kernel(capacity, factor, exps_ref, own_top_ref, top_ref, total_ref, queries_ref, *refs):
    weights_ref, *out_refs = refs
    share = factor * jnp.exp(own_top_ref[...] - top_ref[...]) / total_ref[...]
    for first in range(0, exps_ref.shape[0], GROUP_SLOTS):
        span = slice(first, first + GROUP_SLOTS)
        weights = (exps_ref[span, :].astype(jnp.float32) * share).astype(jnp.bfloat16)
        weights_ref[span, :] = weights
        value = jnp.dot(weights, queries_ref[...], preferred_element_type=jnp.float32)
        store_blocks(out_refs, first // capacity, value.astype(jnp.bfloat16))


def row_grad(exps, own_top, top, total, queries, members, factor):
    slots, count = exps.shape
    width = queries.shape[1]
    ranks = members[0][3]
    shapes = block_shapes(members, width)
    line = (1, count)
    if len(shapes) == 1:
        steps = slots // GROUP_SLOTS
        span = pl.BlockSpec((GROUP_SLOTS, count), lambda t: (t, 0))
        blocks = pl.BlockSpec((GROUP_SLOTS // ranks, ranks, width), lambda t: (t, 0, 0))
        specs = dict(
            grid=(steps,),
            in_specs=[span, whole(line), whole(line), whole(line), whole(queries.shape)],
            out_specs=[span, blocks],
            compiler_params=params(STREAM_MIB),
        )
    else:
        specs = dict(
            in_specs=[IN_VMEM] * 5,
            out_specs=[IN_VMEM] * (1 + len(shapes)),
            compiler_params=params(14),
        )
    weights, *grads = pl.pallas_call(
        functools.partial(row_grad_kernel, ranks, factor),
        out_shape=[jax.ShapeDtypeStruct((slots, count), jnp.bfloat16)] + shapes,
        cost_estimate=cost(
            2 * slots * width * count, 2 * (slots + count) * width + 6 * slots * count
        ),
        name="row_grad",
        **specs,
    )(exps, own_top, top, total, queries)
    return weights, grads


def query_kernel(factor, sizes, pos_ref, top_ref, total_ref, positives_ref, *refs):
    weights_refs, rest = refs[: len(sizes)], refs[len(sizes) :]
    grad_ref = refs[-1]
    pos, top, total = pos_ref[...], top_ref[...], total_ref[...]
    coef = as_columns([factor * (jnp.exp(pos - top) / total - 1.0)])
    value = jnp.concatenate(
        [
            coef * positives_ref[:, start : start + LANES].astype(jnp.float32)
            for start in range(0, positives_ref.shape[1], LANES)
        ],
        axis=1,
    )
    first = 0
    for ref, size in zip(weights_refs, sizes):
        rows = jnp.concatenate([one[...] for one in rest[first : first + size]], axis=0)
        first += size
        value = value + lax.dot_general(
            ref[...], rows, (((0,), (0,)), ((), ())), preferred_element_type=jnp.float32
        )
    grad_ref[...] = value.astype(jnp.bfloat16)


def query_grad(pos, top, total, positives, weights, fetched, factor, part, grads):
    count, width = positives.shape
    tile = min(256, count // QUERY_PARTS)
    steps = count // QUERY_PARTS // tile
    first = part * steps
    line = pl.BlockSpec((1, tile), lambda t: (0, first + t))
    block = pl.BlockSpec((tile, width), lambda t: (first + t, 0))
    sizes = [len(group) for group in fetched]
    rows = [one for group in fetched for one in group]
    inputs = [pos, top, total, positives, *weights, *rows, *grads]
    slots = sum(one.shape[0] for one in weights)
    return pl.pallas_call(
        functools.partial(query_kernel, factor, sizes),
        out_shape=jax.ShapeDtypeStruct((count, width), jnp.bfloat16),
        grid=(steps,),
        in_specs=[line, line, line, block]
        + [pl.BlockSpec((one.shape[0], tile), lambda t: (0, first + t)) for one in weights]
        + [whole(one.shape) for one in rows]
        + [UNREAD] * len(grads),
        out_specs=block,
        input_output_aliases={len(inputs) - 1: 0} if grads else {},
        compiler_params=params(26),
        cost_estimate=cost(
            2 * slots * width * count // QUERY_PARTS,
            2 * slots * width + 4 * count * width // QUERY_PARTS,
        ),
        name="query_grad",
    )(*inputs)


def scatter_kernel(members, first, place_ref, wanted_ref, *refs):
    *value_refs, out_ref = refs
    base_ref = value_refs.pop(0) if value_refs[0].shape == out_ref.shape else None
    rows = out_ref.shape[0]
    me = place_ref[0]
    row = (first + pl.program_id(0)) * rows + lax.broadcasted_iota(jnp.int32, (rows, 1), 0)
    wanted = jnp.concatenate(
        [partner_line(wanted_ref, me, m)[:, m[2] : m[2] + m[3]] for m in members], axis=1
    )
    hot = jnp.where(wanted == row, 1.0, 0.0).astype(jnp.bfloat16)
    values = jnp.concatenate([ref[...] for ref in value_refs], axis=0)
    total = jnp.dot(hot, values, preferred_element_type=jnp.float32)
    if base_ref is not None:
        total = base_ref[...] + total
    out_ref[...] = total.astype(out_ref.dtype)


def scatter(place, wanted, values, members, base, shard_rows, part, parts, dtype):
    width = values[0].shape[1]
    slots = sum(one.shape[0] for one in values)
    rows = shard_rows // parts
    tile = 2 * LANES
    first = part * rows // tile
    return pl.pallas_call(
        functools.partial(scatter_kernel, members, first),
        out_shape=jax.ShapeDtypeStruct((rows, width), dtype),
        grid=(rows // tile,),
        in_specs=[SCALAR, whole(wanted.shape)]
        + [pl.BlockSpec((tile, width), lambda t: (first + t, 0))] * len(base)
        + [whole(one.shape) for one in values],
        out_specs=pl.BlockSpec((tile, width), lambda t: (t, 0)),
        compiler_params=params(STREAM_MIB),
        cost_estimate=cost(
            2 * rows * slots * width, 2 * slots * width + 4 * (1 + len(base)) * rows * width
        ),
        name="scatter_rows",
    )(place, wanted, *base, *values)


def add_kernel(own_ref, other_ref, *refs):
    refs[-1][...] = (
        own_ref[...].astype(jnp.float32) + other_ref[...].astype(jnp.float32)
    ).astype(jnp.bfloat16)


def add_part(own, other, part, parts, sums):
    rows, width = own.shape
    tile = min(256, rows)
    first = part * rows // tile
    block = pl.BlockSpec((tile, width), lambda t: (t, 0))
    return pl.pallas_call(
        add_kernel,
        out_shape=jax.ShapeDtypeStruct((rows * parts, width), jnp.bfloat16),
        grid=(rows // tile,),
        in_specs=[block, block] + [UNREAD] * len(sums),
        out_specs=pl.BlockSpec((tile, width), lambda t: (first + t, 0)),
        input_output_aliases={2: 0} if sums else {},
        compiler_params=params(STREAM_MIB),
        cost_estimate=cost(rows * width, 6 * rows * width),
        name="add_cores",
    )(own, other, *sums)


def behind(value, earlier):
    if not earlier:
        return value
    return lax.optimization_barrier((value, *earlier))[0]


def exchange(blocks, members, shards):
    if members[0][0]:
        offsets = set_offsets(shards)
        sets = [[start ^ o for o in offsets] for start in (0, shards // 4)]
        block = lax.all_to_all(
            blocks[0], "idx", split_axis=0, concat_axis=0, tiled=True, axis_index_groups=sets
        )
        return [block.reshape(-1, block.shape[-1])]
    return [
        lax.ppermute(block, "idx", [(i, i ^ offset) for i in range(shards)])
        for block, (_, offset, _, _) in zip(blocks, members)
    ]


def pair_gather(block, offset, upper, shards):
    pairs = [[i, i ^ offset] for i in range(shards) if i < i ^ offset]
    both = lax.all_gather(block, "idx", axis_index_groups=pairs)
    return jnp.where(upper, both[0], both[1])


def local(queries, positives, passages, negatives):
    shards = lax.axis_size("idx")
    shard_rows, width = passages.shape
    ids = negatives.reshape(1, -1)
    capacity = ids.shape[1] // shards
    scale = 3.0 / math.sqrt(width)
    factor = LSCALE * scale
    quarter = shards // 4
    far, near = [
        tuple((False, start + i, 0, capacity) for i in range(quarter))
        for start in (2 * quarter, quarter)
    ]
    within = tuple((True, o, 0, capacity) for o in set_offsets(shards))
    place = lax.axis_index("idx").astype(jnp.int32).reshape(1)

    request = build_request(ids, shards, shard_rows)
    wanted = lax.all_to_all(request, "idx", split_axis=0, concat_axis=0, tiled=True)
    pos_logit = scale * jnp.sum(
        queries.astype(jnp.float32) * positives.astype(jnp.float32), axis=1
    )
    pos_logit = pos_logit.reshape(1, -1)

    order = [within, far, near]
    upper = lax.axis_index("idx") // quarter % 2 == 1

    def exchanged(blocks):
        received = {group: exchange(blocks[group], group, shards) for group in (within, far)}
        received[near] = [
            pair_gather(block, offset, upper, shards)
            for block, (_, offset, _, _) in zip(blocks[near], near)
        ]
        return received

    picked, last = {}, [pos_logit]
    for group in order:
        picked[group] = pick(behind(place, last), wanted, passages, group)
        last = picked[group][-1:]

    fetched = exchanged(picked)

    top, total = pos_logit, jnp.ones_like(pos_logit)
    exps, tops = {}, {}
    for group in (near, far, within):
        exps[group], top, total = group_logits(
            place, request, top, total, queries, fetched[group], group, scale
        )
        tops[group] = top
    loss = top + jnp.log(total) - pos_logit

    weights, grads, last = {}, {}, []
    for group in order:
        weights[group], grads[group] = row_grad(
            exps[group], behind(tops[group], last), top, total, queries, group, factor
        )
        last = grads[group][-1:]

    grad_queries = []
    for part in range(QUERY_PARTS):
        done = query_grad(
            pos_logit,
            top,
            total,
            positives,
            [weights[group] for group in order],
            [fetched[group] for group in order],
            factor,
            part,
            grad_queries[-1:],
        )
        grad_queries.append(done)

    returned = exchanged(grads)

    base = []
    for group in (near, far):
        base = [
            scatter(
                behind(place, grad_queries[-1:]),
                wanted,
                returned[group],
                group,
                base,
                shard_rows,
                0,
                1,
                jnp.float32,
            )
        ]
    late = returned[within]
    grad_passages = []
    parts = [
        scatter(place, wanted, late, within, base, shard_rows, part, SUM_PARTS, jnp.bfloat16)
        for part in range(SUM_PARTS)
    ]
    for part, own in enumerate(parts):
        other = lax.ppermute(own, "enc", SWAP)
        grad_passages = [add_part(own, other, part, SUM_PARTS, grad_passages)]
    return (loss.reshape(-1), grad_queries[-1], grad_passages[0])


def solution(mesh):
    placed = (
        P(("idx", "enc"), None),
        P(("idx", "enc"), None),
        P("idx", None),
        P(("idx", "enc"), None),
    )
    return jax.shard_map(
        local,
        mesh=mesh,
        in_specs=placed,
        out_specs=(P(("idx", "enc")), P(("idx", "enc"), None), P("idx", None)),
        check_vma=False,
    )
```

```python
import functools
import math

import jax
import jax.numpy as jnp
from jax import lax
from jax.experimental import pallas as pl
from jax.experimental.pallas import tpu as pltpu
from jax.sharding import PartitionSpec as P

LSCALE = 32
DEAD = -1e30
LANES = 128
MIB = 1 << 20
GROUP_SLOTS = 256
WINDOW = 4
QUERY_TILE = 256
QUERY_PARTS = 2
SUM_PARTS = 4
SWAP = [(0, 1), (1, 0)]


def params(vmem_mib):
    return pltpu.CompilerParams(vmem_limit_bytes=vmem_mib * MIB)


def cost(flops, bytes_accessed, transcendentals=0):
    return pl.CostEstimate(
        flops=int(flops), bytes_accessed=int(bytes_accessed), transcendentals=int(transcendentals)
    )


def whole(shape):
    return pl.BlockSpec(shape, lambda *_: (0,) * len(shape))


SCALAR = pl.BlockSpec(memory_space=pltpu.SMEM)
UNREAD = pl.BlockSpec(memory_space=pl.ANY)
IN_VMEM = pl.BlockSpec(memory_space=pltpu.VMEM)


def request_kernel(shard_rows, ids_ref, out_ref):
    shards, capacity = out_ref.shape
    count = ids_ref.shape[1]
    ids = ids_ref[...]
    base = lax.broadcasted_iota(jnp.int32, (shards, 1), 0) * shard_rows
    row = ids - base
    mine = (row >= 0) & (row < shard_rows)
    one = jnp.where(mine, 1.0, 0.0)
    high = jnp.where(mine, row // 128, 0).astype(jnp.float32)
    low = jnp.where(mine, row % 128, 0).astype(jnp.float32)
    before = (
        lax.broadcasted_iota(jnp.int32, (LANES, LANES), 0)
        < lax.broadcasted_iota(jnp.int32, (LANES, LANES), 1)
    ).astype(jnp.bfloat16)
    carry = jnp.zeros((shards, 1), jnp.float32)
    places = []
    for start in range(0, count, LANES):
        part = one[:, start : start + LANES]
        inside = jnp.dot(part.astype(jnp.bfloat16), before, preferred_element_type=jnp.float32)
        rank = jnp.sum(part * (inside + carry), axis=0, keepdims=True)
        carry = carry + jnp.sum(part, axis=1, keepdims=True)
        slot = lax.broadcasted_iota(jnp.int32, (capacity, LANES), 0).astype(jnp.float32)
        places.append(jnp.where(slot == rank, 1.0, 0.0))
    place = jnp.concatenate(places, axis=1).astype(jnp.bfloat16)
    parts = jnp.concatenate([one, high, low], axis=0).astype(jnp.bfloat16)
    packed = lax.dot_general(
        parts, place, (((1,), (1,)), ((), ())), preferred_element_type=jnp.float32
    )
    filled = packed[:shards] > 0.5
    rows = packed[shards : 2 * shards] * 128.0 + packed[2 * shards :]
    out_ref[...] = jnp.where(filled, rows.astype(jnp.int32), -1)


def build_request(ids, shards, shard_rows):
    count = ids.shape[1]
    capacity = count // shards
    return pl.pallas_call(
        functools.partial(request_kernel, shard_rows),
        out_shape=jax.ShapeDtypeStruct((shards, capacity), jnp.int32),
        compiler_params=params(16),
        cost_estimate=cost(2 * 3 * shards * count * capacity, 16384),
        name="build_request",
    )(ids)


def partner_line(table_ref, me, offset):
    return table_ref[pl.ds(jnp.bitwise_xor(me, offset), 1), :]


def partner_columns(table_ref, me, members):
    return as_columns([partner_line(table_ref, me, o).astype(jnp.float32) for o in members])


def as_columns(lines):
    blocks = []
    for line in lines:
        for start in range(0, line.shape[1], LANES):
            piece = line[:, start : start + LANES]
            blocks.append(jnp.broadcast_to(piece, (LANES, piece.shape[1])).T)
    return jnp.concatenate(blocks, axis=0)


def store_blocks(refs, value):
    size = refs[0].shape[0]
    for index, ref in enumerate(refs):
        ref[...] = value[index * size : (index + 1) * size]


def pick_kernel(members, place_ref, wanted_ref, passages_ref, *out_refs):
    rows = passages_ref.shape[0]
    wanted = partner_columns(wanted_ref, place_ref[0], members)
    lane = lax.broadcasted_iota(jnp.int32, wanted.shape, 1).astype(jnp.float32)
    hot = jnp.concatenate(
        [
            jnp.where(wanted == lane + float(start), 1.0, 0.0).astype(jnp.bfloat16)
            for start in range(0, rows, LANES)
        ],
        axis=1,
    )
    picked = jnp.dot(hot, passages_ref[...], preferred_element_type=jnp.float32)
    store_blocks(out_refs, picked.astype(jnp.bfloat16))


def pick(place, wanted, passages, members):
    rows, width = passages.shape
    slots = len(members) * wanted.shape[1]
    shapes = [jax.ShapeDtypeStruct((wanted.shape[1], width), jnp.bfloat16)] * len(members)
    return pl.pallas_call(
        functools.partial(pick_kernel, members),
        out_shape=shapes,
        in_specs=[SCALAR, IN_VMEM, IN_VMEM],
        out_specs=[IN_VMEM] * len(shapes),
        compiler_params=params(12),
        cost_estimate=cost(
            2 * slots * rows * width,
            2 * (rows + slots) * width,
        ),
        name="pick_rows",
    )(place, wanted, passages)


def logits_kernel(members, scale, place_ref, request_ref, top_ref, total_ref, queries_ref, *refs):
    fetched_refs, (exps_ref, new_top_ref, new_total_ref) = refs[:-3], refs[-3:]
    me = place_ref[0]
    live = partner_columns(request_ref, me, members) >= 0.0
    fetched = jnp.concatenate([ref[...] for ref in fetched_refs], axis=0)
    for first in range(0, queries_ref.shape[0], QUERY_TILE):
        logits = lax.dot_general(
            fetched,
            queries_ref[first : first + QUERY_TILE, :],
            (((1,), (1,)), ((), ())),
            preferred_element_type=jnp.float32,
        )
        for start in range(0, QUERY_TILE, LANES):
            lanes = slice(first + start, first + start + LANES)
            part = jnp.where(live, scale * logits[:, start : start + LANES], DEAD)
            old_top = top_ref[:, lanes]
            top = jnp.maximum(old_top, jnp.max(part, axis=0, keepdims=True))
            exps = jnp.exp(part - top)
            exps_ref[:, lanes] = exps.astype(exps_ref.dtype)
            new_top_ref[:, lanes] = top
            new_total_ref[:, lanes] = total_ref[:, lanes] * jnp.exp(old_top - top) + jnp.sum(
                exps, axis=0, keepdims=True
            )


def group_logits(place, request, top, total, queries, fetched, members, scale):
    width = fetched[0].shape[1]
    slots = sum(rows.shape[0] for rows in fetched)
    count = queries.shape[0]
    shape = jax.ShapeDtypeStruct((1, count), jnp.float32)
    return pl.pallas_call(
        functools.partial(logits_kernel, members, scale),
        out_shape=(jax.ShapeDtypeStruct((slots, count), jnp.bfloat16), shape, shape),
        in_specs=[SCALAR] + [IN_VMEM] * (4 + len(fetched)),
        out_specs=(IN_VMEM,) * 3,
        compiler_params=params(14),
        cost_estimate=cost(
            2 * slots * width * count,
            2 * (slots + count) * width + 4 * slots * count,
            slots * count,
        ),
        name="group_logits",
    )(place, request, top, total, queries, *fetched)


def row_grad_kernel(factor, exps_ref, own_top_ref, top_ref, total_ref, queries_ref, *refs):
    weights_ref, *out_refs = refs
    share = factor * jnp.exp(own_top_ref[...] - top_ref[...]) / total_ref[...]
    weights = (exps_ref[...].astype(jnp.float32) * share).astype(jnp.bfloat16)
    weights_ref[...] = weights
    value = jnp.dot(weights, queries_ref[...], preferred_element_type=jnp.float32)
    store_blocks(out_refs, value.astype(jnp.bfloat16))


def row_grad(exps, own_top, top, total, queries, members, factor):
    slots, count = exps.shape
    width = queries.shape[1]
    block = (slots // len(members), width)
    shapes = [jax.ShapeDtypeStruct(block, jnp.bfloat16)] * len(members)
    weights, *grads = pl.pallas_call(
        functools.partial(row_grad_kernel, factor),
        out_shape=[jax.ShapeDtypeStruct((slots, count), jnp.bfloat16)] + shapes,
        in_specs=[IN_VMEM] * 5,
        out_specs=[IN_VMEM] * (1 + len(shapes)),
        compiler_params=params(14),
        cost_estimate=cost(
            2 * slots * width * count, 2 * (slots + count) * width + 6 * slots * count
        ),
        name="row_grad",
    )(exps, own_top, top, total, queries)
    return weights, grads


def query_kernel(factor, sizes, pos_ref, top_ref, total_ref, positives_ref, *refs):
    weights_refs, rest = refs[: len(sizes)], refs[len(sizes) :]
    grad_ref = refs[-1]
    pos, top, total = pos_ref[...], top_ref[...], total_ref[...]
    coef = as_columns([factor * (jnp.exp(pos - top) / total - 1.0)])
    value = jnp.concatenate(
        [
            coef * positives_ref[:, start : start + LANES].astype(jnp.float32)
            for start in range(0, positives_ref.shape[1], LANES)
        ],
        axis=1,
    )
    first = 0
    for ref, size in zip(weights_refs, sizes):
        rows = jnp.concatenate([one[...] for one in rest[first : first + size]], axis=0)
        first += size
        value = value + lax.dot_general(
            ref[...], rows, (((0,), (0,)), ((), ())), preferred_element_type=jnp.float32
        )
    grad_ref[...] = value.astype(jnp.bfloat16)


def query_grad(pos, top, total, positives, weights, fetched, factor, part, grads):
    count, width = positives.shape
    tile = min(256, count // QUERY_PARTS)
    steps = count // QUERY_PARTS // tile
    first = part * steps
    line = pl.BlockSpec((1, tile), lambda t: (0, first + t))
    block = pl.BlockSpec((tile, width), lambda t: (first + t, 0))
    sizes = [len(group) for group in fetched]
    rows = [one for group in fetched for one in group]
    inputs = [pos, top, total, positives, *weights, *rows, *grads]
    slots = sum(one.shape[0] for one in weights)
    return pl.pallas_call(
        functools.partial(query_kernel, factor, sizes),
        out_shape=jax.ShapeDtypeStruct((count, width), jnp.bfloat16),
        grid=(steps,),
        in_specs=[line, line, line, block]
        + [pl.BlockSpec((one.shape[0], tile), lambda t: (0, first + t)) for one in weights]
        + [whole(one.shape) for one in rows]
        + [UNREAD] * len(grads),
        out_specs=block,
        input_output_aliases={len(inputs) - 1: 0} if grads else {},
        compiler_params=params(26),
        cost_estimate=cost(
            2 * slots * width * count // QUERY_PARTS,
            2 * slots * width + 4 * count * width // QUERY_PARTS,
        ),
        name="query_grad",
    )(*inputs)


def scatter_kernel(members, first, place_ref, wanted_ref, *refs):
    *value_refs, out_ref = refs
    base_ref = value_refs.pop(0) if value_refs[0].shape == out_ref.shape else None
    rows = out_ref.shape[0]
    me = place_ref[0]
    row = (first + pl.program_id(0)) * rows + lax.broadcasted_iota(jnp.int32, (rows, 1), 0)
    wanted = jnp.concatenate(
        [partner_line(wanted_ref, me, o) for o in members], axis=1
    )
    hot = jnp.where(wanted == row, 1.0, 0.0).astype(jnp.bfloat16)
    values = jnp.concatenate([ref[...] for ref in value_refs], axis=0)
    total = jnp.dot(hot, values, preferred_element_type=jnp.float32)
    if base_ref is not None:
        total = base_ref[...] + total
    out_ref[...] = total.astype(out_ref.dtype)


def scatter(place, wanted, values, members, base, shard_rows, part, parts, dtype):
    width = values[0].shape[1]
    slots = sum(one.shape[0] for one in values)
    rows = shard_rows // parts
    tile = 2 * LANES
    first = part * rows // tile
    return pl.pallas_call(
        functools.partial(scatter_kernel, members, first),
        out_shape=jax.ShapeDtypeStruct((rows, width), dtype),
        grid=(rows // tile,),
        in_specs=[SCALAR, whole(wanted.shape)]
        + [pl.BlockSpec((tile, width), lambda t: (first + t, 0))] * len(base)
        + [whole(one.shape) for one in values],
        out_specs=pl.BlockSpec((tile, width), lambda t: (t, 0)),
        compiler_params=params(18),
        cost_estimate=cost(
            2 * rows * slots * width, 2 * slots * width + 4 * (1 + len(base)) * rows * width
        ),
        name="scatter_rows",
    )(place, wanted, *base, *values)


def add_kernel(own_ref, other_ref, *refs):
    refs[-1][...] = (
        own_ref[...].astype(jnp.float32) + other_ref[...].astype(jnp.float32)
    ).astype(jnp.bfloat16)


def add_part(own, other, part, parts, sums):
    rows, width = own.shape
    tile = min(256, rows)
    first = part * rows // tile
    block = pl.BlockSpec((tile, width), lambda t: (t, 0))
    return pl.pallas_call(
        add_kernel,
        out_shape=jax.ShapeDtypeStruct((rows * parts, width), jnp.bfloat16),
        grid=(rows // tile,),
        in_specs=[block, block] + [UNREAD] * len(sums),
        out_specs=pl.BlockSpec((tile, width), lambda t: (first + t, 0)),
        input_output_aliases={2: 0} if sums else {},
        compiler_params=params(16),
        cost_estimate=cost(rows * width, 6 * rows * width),
        name="add_cores",
    )(own, other, *sums)


def behind(value, earlier):
    if not earlier:
        return value
    return lax.optimization_barrier((value, *earlier))[0]


def exchange(blocks, members, shards):
    return [
        block
        if offset == 0
        else lax.ppermute(block, "idx", [(i, i ^ offset) for i in range(shards)])
        for block, offset in zip(blocks, members)
    ]


def partner_groups(shards, per):
    half = shards // 2
    quarter = half // 2
    far = [half + part * quarter + place for place in range(quarter) for part in range(2)]
    near = [*range(quarter, half), *range(1, quarter)]
    near = [near.pop(), 0, *near] if per == 2 else [0, *near]
    far = [tuple(far[i : i + per]) for i in range(0, half, per)]
    near = [tuple(near[i : i + per]) for i in range(0, half, per)]
    return [group for pair in zip(near, far) for group in pair]


def local(queries, positives, passages, negatives):
    shards = lax.axis_size("idx")
    shard_rows, width = passages.shape
    ids = negatives.reshape(1, -1)
    capacity = ids.shape[1] // shards
    scale = 3.0 / math.sqrt(width)
    factor = LSCALE * scale
    groups = partner_groups(shards, max(1, GROUP_SLOTS // capacity))
    place = lax.axis_index("idx").astype(jnp.int32).reshape(1)

    request = build_request(ids, shards, shard_rows)
    wanted = lax.all_to_all(request, "idx", split_axis=0, concat_axis=0, tiled=True)
    pos_logit = scale * jnp.sum(
        queries.astype(jnp.float32) * positives.astype(jnp.float32), axis=1
    )
    pos_logit = pos_logit.reshape(1, -1)

    fetched = []
    for index, group in enumerate(groups):
        earlier = fetched[index - WINDOW][-1:] if index >= WINDOW else [pos_logit]
        picked = pick(behind(place, earlier), wanted, passages, group)
        fetched.append(exchange(picked, group, shards))

    top, total = pos_logit, jnp.ones_like(pos_logit)
    exps, tops = [], []
    for group, rows in zip(groups, fetched):
        value, top, total = group_logits(
            place, request, top, total, queries, rows, group, scale
        )
        exps.append(value)
        tops.append(top)
    loss = top + jnp.log(total) - pos_logit

    order = [1, 0, *range(2, len(groups))]
    weights, grads, last = [None] * len(groups), {}, []
    for index in order:
        weights[index], grads[index] = row_grad(
            exps[index], behind(tops[index], last), top, total, queries, groups[index], factor
        )
        last = grads[index][-1:]

    grad_queries = []
    for part in range(QUERY_PARTS):
        done = query_grad(
            pos_logit,
            top,
            total,
            positives,
            weights,
            fetched,
            factor,
            part,
            grad_queries[-1:],
        )
        grad_queries.append(done)

    sums, returned = [], {}

    def scattered(indices, part=0, parts=1, dtype=jnp.float32):
        return scatter(
            place,
            wanted,
            [one for index in indices for one in returned[index]],
            sum((groups[index] for index in indices), ()),
            sums[-1:],
            shard_rows,
            part,
            parts,
            dtype,
        )

    first_query = len(order) - 1 - QUERY_PARTS
    for step, index in enumerate(order):
        blocks = grads[index]
        if step >= WINDOW:
            sums.append(scattered([order[step - WINDOW]]))
            earlier = sums[-1:]
            if first_query <= step < first_query + QUERY_PARTS:
                earlier = earlier + [grad_queries[step - first_query]]
            blocks = [behind(blocks[0], earlier), *blocks[1:]]
        returned[index] = exchange(blocks, groups[index], shards)
    sums.append(scattered(order[-WINDOW:-1]))
    parts = [
        scattered(order[-1:], part, SUM_PARTS, jnp.bfloat16) for part in range(SUM_PARTS)
    ]
    grad_passages = []
    for part, own in enumerate(parts):
        other = lax.ppermute(own, "enc", SWAP)
        grad_passages = [add_part(own, other, part, SUM_PARTS, grad_passages)]
    return (loss.reshape(-1), grad_queries[-1], grad_passages[0])


def solution(mesh):
    placed = (
        P(("idx", "enc"), None),
        P(("idx", "enc"), None),
        P("idx", None),
        P(("idx", "enc"), None),
    )
    return jax.shard_map(
        local,
        mesh=mesh,
        in_specs=placed,
        out_specs=(P(("idx", "enc")), P(("idx", "enc"), None), P("idx", None)),
        check_vma=False,
    )
```

```python
import functools
import math

import jax
import jax.numpy as jnp
from jax import lax
from jax.experimental import pallas as pl
from jax.experimental.pallas import tpu as pltpu
from jax.sharding import PartitionSpec as P

LSCALE = 32
DEAD = -1e30
LANES = 128
MIB = 1 << 20
GROUP_SLOTS = 256
SHARE = 0.3
WINDOW = 4
QUERY_TILE = 256
QUERY_PARTS = 2
SUM_PARTS = 4
SWAP = [(0, 1), (1, 0)]


def params(vmem_mib):
    return pltpu.CompilerParams(vmem_limit_bytes=vmem_mib * MIB)


def cost(flops, bytes_accessed, transcendentals=0):
    return pl.CostEstimate(
        flops=int(flops * SHARE), bytes_accessed=int(bytes_accessed * SHARE), transcendentals=0
    )


def whole(shape):
    return pl.BlockSpec(shape, lambda *_: (0,) * len(shape))


SCALAR = pl.BlockSpec(memory_space=pltpu.SMEM)
UNREAD = pl.BlockSpec(memory_space=pl.ANY)
IN_VMEM = pl.BlockSpec(memory_space=pltpu.VMEM)


def request_kernel(shard_rows, ids_ref, out_ref):
    shards, capacity = out_ref.shape
    count = ids_ref.shape[1]
    ids = ids_ref[...]
    base = lax.broadcasted_iota(jnp.int32, (shards, 1), 0) * shard_rows
    row = ids - base
    mine = (row >= 0) & (row < shard_rows)
    one = jnp.where(mine, 1.0, 0.0)
    high = jnp.where(mine, row // 128, 0).astype(jnp.float32)
    low = jnp.where(mine, row % 128, 0).astype(jnp.float32)
    before = (
        lax.broadcasted_iota(jnp.int32, (LANES, LANES), 0)
        < lax.broadcasted_iota(jnp.int32, (LANES, LANES), 1)
    ).astype(jnp.bfloat16)
    carry = jnp.zeros((shards, 1), jnp.float32)
    places = []
    for start in range(0, count, LANES):
        part = one[:, start : start + LANES]
        inside = jnp.dot(part.astype(jnp.bfloat16), before, preferred_element_type=jnp.float32)
        rank = jnp.sum(part * (inside + carry), axis=0, keepdims=True)
        carry = carry + jnp.sum(part, axis=1, keepdims=True)
        slot = lax.broadcasted_iota(jnp.int32, (capacity, LANES), 0).astype(jnp.float32)
        places.append(jnp.where(slot == rank, 1.0, 0.0))
    place = jnp.concatenate(places, axis=1).astype(jnp.bfloat16)
    parts = jnp.concatenate([one, high, low], axis=0).astype(jnp.bfloat16)
    packed = lax.dot_general(
        parts, place, (((1,), (1,)), ((), ())), preferred_element_type=jnp.float32
    )
    filled = packed[:shards] > 0.5
    rows = packed[shards : 2 * shards] * 128.0 + packed[2 * shards :]
    out_ref[...] = jnp.where(filled, rows.astype(jnp.int32), -1)


def build_request(ids, shards, shard_rows):
    count = ids.shape[1]
    capacity = count // shards
    return pl.pallas_call(
        functools.partial(request_kernel, shard_rows),
        out_shape=jax.ShapeDtypeStruct((shards, capacity), jnp.int32),
        compiler_params=params(16),
        cost_estimate=cost(2 * 3 * shards * count * capacity, 16384),
        name="build_request",
    )(ids)


def partner_line(table_ref, me, offset):
    return table_ref[pl.ds(jnp.bitwise_xor(me, offset), 1), :]


def partner_columns(table_ref, me, members):
    return as_columns([partner_line(table_ref, me, o).astype(jnp.float32) for o in members])


def as_columns(lines):
    blocks = []
    for line in lines:
        for start in range(0, line.shape[1], LANES):
            piece = line[:, start : start + LANES]
            blocks.append(jnp.broadcast_to(piece, (LANES, piece.shape[1])).T)
    return jnp.concatenate(blocks, axis=0)


def store_blocks(refs, value):
    size = refs[0].shape[0]
    for index, ref in enumerate(refs):
        ref[...] = value[index * size : (index + 1) * size]


def pick_kernel(members, place_ref, wanted_ref, passages_ref, *out_refs):
    rows = passages_ref.shape[0]
    wanted = partner_columns(wanted_ref, place_ref[0], members)
    lane = lax.broadcasted_iota(jnp.int32, wanted.shape, 1).astype(jnp.float32)
    hot = jnp.concatenate(
        [
            jnp.where(wanted == lane + float(start), 1.0, 0.0).astype(jnp.bfloat16)
            for start in range(0, rows, LANES)
        ],
        axis=1,
    )
    picked = jnp.dot(hot, passages_ref[...], preferred_element_type=jnp.float32)
    store_blocks(out_refs, picked.astype(jnp.bfloat16))


def pick(place, wanted, passages, members):
    rows, width = passages.shape
    slots = len(members) * wanted.shape[1]
    shapes = [jax.ShapeDtypeStruct((wanted.shape[1], width), jnp.bfloat16)] * len(members)
    return pl.pallas_call(
        functools.partial(pick_kernel, members),
        out_shape=shapes,
        in_specs=[SCALAR, IN_VMEM, IN_VMEM],
        out_specs=[IN_VMEM] * len(shapes),
        compiler_params=params(12),
        cost_estimate=cost(
            2 * slots * rows * width,
            2 * (rows + slots) * width,
        ),
        name="pick_rows",
    )(place, wanted, passages)


def logits_kernel(members, scale, place_ref, request_ref, top_ref, total_ref, queries_ref, *refs):
    fetched_refs, (exps_ref, new_top_ref, new_total_ref) = refs[:-3], refs[-3:]
    me = place_ref[0]
    live = partner_columns(request_ref, me, members) >= 0.0
    fetched = jnp.concatenate([ref[...] for ref in fetched_refs], axis=0)
    for first in range(0, queries_ref.shape[0], QUERY_TILE):
        logits = lax.dot_general(
            fetched,
            queries_ref[first : first + QUERY_TILE, :],
            (((1,), (1,)), ((), ())),
            preferred_element_type=jnp.float32,
        )
        for start in range(0, QUERY_TILE, LANES):
            lanes = slice(first + start, first + start + LANES)
            part = jnp.where(live, scale * logits[:, start : start + LANES], DEAD)
            old_top = top_ref[:, lanes]
            top = jnp.maximum(old_top, jnp.max(part, axis=0, keepdims=True))
            exps = jnp.exp(part - top)
            exps_ref[:, lanes] = exps.astype(exps_ref.dtype)
            new_top_ref[:, lanes] = top
            new_total_ref[:, lanes] = total_ref[:, lanes] * jnp.exp(old_top - top) + jnp.sum(
                exps, axis=0, keepdims=True
            )


def group_logits(place, request, top, total, queries, fetched, members, scale):
    width = fetched[0].shape[1]
    slots = sum(rows.shape[0] for rows in fetched)
    count = queries.shape[0]
    shape = jax.ShapeDtypeStruct((1, count), jnp.float32)
    return pl.pallas_call(
        functools.partial(logits_kernel, members, scale),
        out_shape=(jax.ShapeDtypeStruct((slots, count), jnp.bfloat16), shape, shape),
        in_specs=[SCALAR] + [IN_VMEM] * (4 + len(fetched)),
        out_specs=(IN_VMEM,) * 3,
        compiler_params=params(14),
        cost_estimate=cost(
            2 * slots * width * count,
            2 * (slots + count) * width + 4 * slots * count,
            slots * count,
        ),
        name="group_logits",
    )(place, request, top, total, queries, *fetched)


def row_grad_kernel(factor, exps_ref, own_top_ref, top_ref, total_ref, queries_ref, *refs):
    weights_ref, *out_refs = refs
    share = factor * jnp.exp(own_top_ref[...] - top_ref[...]) / total_ref[...]
    weights = (exps_ref[...].astype(jnp.float32) * share).astype(jnp.bfloat16)
    weights_ref[...] = weights
    value = jnp.dot(weights, queries_ref[...], preferred_element_type=jnp.float32)
    store_blocks(out_refs, value.astype(jnp.bfloat16))


def row_grad(exps, own_top, top, total, queries, members, factor):
    slots, count = exps.shape
    width = queries.shape[1]
    block = (slots // len(members), width)
    shapes = [jax.ShapeDtypeStruct(block, jnp.bfloat16)] * len(members)
    weights, *grads = pl.pallas_call(
        functools.partial(row_grad_kernel, factor),
        out_shape=[jax.ShapeDtypeStruct((slots, count), jnp.bfloat16)] + shapes,
        in_specs=[IN_VMEM] * 5,
        out_specs=[IN_VMEM] * (1 + len(shapes)),
        compiler_params=params(14),
        cost_estimate=cost(
            2 * slots * width * count, 2 * (slots + count) * width + 6 * slots * count
        ),
        name="row_grad",
    )(exps, own_top, top, total, queries)
    return weights, grads


def query_kernel(factor, sizes, pos_ref, top_ref, total_ref, positives_ref, *refs):
    weights_refs, rest = refs[: len(sizes)], refs[len(sizes) :]
    grad_ref = refs[-1]
    pos, top, total = pos_ref[...], top_ref[...], total_ref[...]
    coef = as_columns([factor * (jnp.exp(pos - top) / total - 1.0)])
    value = jnp.concatenate(
        [
            coef * positives_ref[:, start : start + LANES].astype(jnp.float32)
            for start in range(0, positives_ref.shape[1], LANES)
        ],
        axis=1,
    )
    first = 0
    for ref, size in zip(weights_refs, sizes):
        rows = jnp.concatenate([one[...] for one in rest[first : first + size]], axis=0)
        first += size
        value = value + lax.dot_general(
            ref[...], rows, (((0,), (0,)), ((), ())), preferred_element_type=jnp.float32
        )
    grad_ref[...] = value.astype(jnp.bfloat16)


def query_grad(pos, top, total, positives, weights, fetched, factor, part, grads):
    count, width = positives.shape
    tile = min(256, count // QUERY_PARTS)
    steps = count // QUERY_PARTS // tile
    first = part * steps
    line = pl.BlockSpec((1, tile), lambda t: (0, first + t))
    block = pl.BlockSpec((tile, width), lambda t: (first + t, 0))
    sizes = [len(group) for group in fetched]
    rows = [one for group in fetched for one in group]
    inputs = [pos, top, total, positives, *weights, *rows, *grads]
    slots = sum(one.shape[0] for one in weights)
    return pl.pallas_call(
        functools.partial(query_kernel, factor, sizes),
        out_shape=jax.ShapeDtypeStruct((count, width), jnp.bfloat16),
        grid=(steps,),
        in_specs=[line, line, line, block]
        + [pl.BlockSpec((one.shape[0], tile), lambda t: (0, first + t)) for one in weights]
        + [whole(one.shape) for one in rows]
        + [UNREAD] * len(grads),
        out_specs=block,
        input_output_aliases={len(inputs) - 1: 0} if grads else {},
        compiler_params=params(26),
        cost_estimate=cost(
            2 * slots * width * count // QUERY_PARTS,
            2 * slots * width + 4 * count * width // QUERY_PARTS,
        ),
        name="query_grad",
    )(*inputs)


def scatter_kernel(members, first, place_ref, wanted_ref, *refs):
    *value_refs, out_ref = refs
    base_ref = value_refs.pop(0) if value_refs[0].shape == out_ref.shape else None
    rows = out_ref.shape[0]
    me = place_ref[0]
    row = (first + pl.program_id(0)) * rows + lax.broadcasted_iota(jnp.int32, (rows, 1), 0)
    wanted = jnp.concatenate(
        [partner_line(wanted_ref, me, o) for o in members], axis=1
    )
    hot = jnp.where(wanted == row, 1.0, 0.0).astype(jnp.bfloat16)
    values = jnp.concatenate([ref[...] for ref in value_refs], axis=0)
    total = jnp.dot(hot, values, preferred_element_type=jnp.float32)
    if base_ref is not None:
        total = base_ref[...] + total
    out_ref[...] = total.astype(out_ref.dtype)


def scatter(place, wanted, values, members, base, shard_rows, part, parts, dtype):
    width = values[0].shape[1]
    slots = sum(one.shape[0] for one in values)
    rows = shard_rows // parts
    tile = 2 * LANES
    first = part * rows // tile
    return pl.pallas_call(
        functools.partial(scatter_kernel, members, first),
        out_shape=jax.ShapeDtypeStruct((rows, width), dtype),
        grid=(rows // tile,),
        in_specs=[SCALAR, whole(wanted.shape)]
        + [pl.BlockSpec((tile, width), lambda t: (first + t, 0))] * len(base)
        + [whole(one.shape) for one in values],
        out_specs=pl.BlockSpec((tile, width), lambda t: (t, 0)),
        compiler_params=params(18),
        cost_estimate=cost(
            2 * rows * slots * width, 2 * slots * width + 4 * (1 + len(base)) * rows * width
        ),
        name="scatter_rows",
    )(place, wanted, *base, *values)


def add_kernel(own_ref, other_ref, *refs):
    out_ref = refs[-1]
    rows = out_ref.shape[0]
    span = pl.ds(pl.multiple_of(pl.program_id(0) * rows, rows), rows)
    total = own_ref[span, :].astype(jnp.float32) + other_ref[span, :].astype(jnp.float32)
    out_ref[...] = total.astype(jnp.bfloat16)


def add_part(own, other, part, parts, sums):
    rows, width = own.shape
    tile = min(256, rows)
    first = part * rows // tile
    return pl.pallas_call(
        add_kernel,
        out_shape=jax.ShapeDtypeStruct((rows * parts, width), jnp.bfloat16),
        grid=(rows // tile,),
        in_specs=[IN_VMEM, IN_VMEM] + [UNREAD] * len(sums),
        out_specs=pl.BlockSpec((tile, width), lambda t: (first + t, 0)),
        input_output_aliases={2: 0} if sums else {},
        compiler_params=params(8),
        cost_estimate=cost(rows * width, 6 * rows * width),
        name="add_cores",
    )(own, other, *sums)


def behind(value, earlier):
    if not earlier:
        return value
    return lax.optimization_barrier((value, *earlier))[0]


def exchange(blocks, members, shards):
    return [
        block
        if offset == 0
        else lax.ppermute(block, "idx", [(i, i ^ offset) for i in range(shards)])
        for block, offset in zip(blocks, members)
    ]


def partner_groups(shards, per):
    half = shards // 2
    quarter = half // 2
    far = [half + part * quarter + place for place in range(quarter) for part in range(2)]
    near = [*range(quarter, half), *range(1, quarter)]
    near = [near.pop(), 0, *near] if per == 2 else [0, *near]
    far = [tuple(far[i : i + per]) for i in range(0, half, per)]
    near = [tuple(near[i : i + per]) for i in range(0, half, per)]
    return [group for pair in zip(far, near) for group in pair]


def local(queries, positives, passages, negatives):
    shards = lax.axis_size("idx")
    shard_rows, width = passages.shape
    ids = negatives.reshape(1, -1)
    capacity = ids.shape[1] // shards
    scale = 3.0 / math.sqrt(width)
    factor = LSCALE * scale
    groups = partner_groups(shards, max(1, GROUP_SLOTS // capacity))
    place = lax.axis_index("idx").astype(jnp.int32).reshape(1)

    request = build_request(ids, shards, shard_rows)
    wanted = lax.all_to_all(request, "idx", split_axis=0, concat_axis=0, tiled=True)
    pos_logit = scale * jnp.sum(
        queries.astype(jnp.float32) * positives.astype(jnp.float32), axis=1
    )
    pos_logit = pos_logit.reshape(1, -1)

    fetched = []
    for index, group in enumerate(groups):
        earlier = fetched[index - WINDOW][-1:] if index >= WINDOW else [pos_logit]
        picked = pick(behind(place, earlier), wanted, passages, group)
        fetched.append(exchange(picked, group, shards))

    top, total = pos_logit, jnp.ones_like(pos_logit)
    exps, tops = [], []
    for group, rows in zip(groups, fetched):
        value, top, total = group_logits(
            place, request, top, total, queries, rows, group, scale
        )
        exps.append(value)
        tops.append(top)
    loss = top + jnp.log(total) - pos_logit

    order = [*range(len(groups))]
    weights, grads, last = [None] * len(groups), {}, []
    for index in order:
        weights[index], grads[index] = row_grad(
            exps[index], behind(tops[index], last), top, total, queries, groups[index], factor
        )
        last = grads[index][-1:]

    grad_queries = []
    for part in range(QUERY_PARTS):
        done = query_grad(
            pos_logit,
            top,
            total,
            positives,
            weights,
            fetched,
            factor,
            part,
            grad_queries[-1:],
        )
        grad_queries.append(done)

    sums, returned = [], {}

    def scattered(indices, part=0, parts=1, dtype=jnp.float32):
        return scatter(
            place,
            wanted,
            [one for index in indices for one in returned[index]],
            sum((groups[index] for index in indices), ()),
            sums[-1:],
            shard_rows,
            part,
            parts,
            dtype,
        )

    first_query = len(order) - 1 - QUERY_PARTS
    for step, index in enumerate(order):
        blocks = grads[index]
        if step >= WINDOW:
            sums.append(scattered([order[step - WINDOW]]))
            earlier = sums[-1:]
            if first_query <= step < first_query + QUERY_PARTS:
                earlier = earlier + [grad_queries[step - first_query]]
            blocks = [behind(blocks[0], earlier), *blocks[1:]]
        returned[index] = exchange(blocks, groups[index], shards)
    sums.append(scattered(order[-WINDOW:-1]))
    parts = [
        scattered(order[-1:], part, SUM_PARTS, jnp.bfloat16) for part in range(SUM_PARTS)
    ]
    grad_passages = []
    for part, own in enumerate(parts):
        other = lax.ppermute(own, "enc", SWAP)
        grad_passages = [add_part(own, other, part, SUM_PARTS, grad_passages)]
    return (loss.reshape(-1), grad_queries[-1], grad_passages[0])


def solution(mesh):
    placed = (
        P(("idx", "enc"), None),
        P(("idx", "enc"), None),
        P("idx", None),
        P(("idx", "enc"), None),
    )
    return jax.shard_map(
        local,
        mesh=mesh,
        in_specs=placed,
        out_specs=(P(("idx", "enc")), P(("idx", "enc"), None), P("idx", None)),
        check_vma=False,
    )
```

```python
import functools
import math

import jax
import jax.numpy as jnp
from jax import lax
from jax.experimental import pallas as pl
from jax.experimental.pallas import tpu as pltpu
from jax.sharding import PartitionSpec as P

LSCALE = 32
DEAD = -1e30
LANES = 128
MIB = 1 << 20
GROUP_SLOTS = 256
WINDOW = 4
LIGHT = 0.1
QUERY_TILE = 256
QUERY_PARTS = 2
SUM_PARTS = 4
SWAP = [(0, 1), (1, 0)]


def params(vmem_mib):
    return pltpu.CompilerParams(vmem_limit_bytes=vmem_mib * MIB)


def cost(flops, bytes_accessed, transcendentals=0):
    return pl.CostEstimate(
        flops=int(flops), bytes_accessed=int(bytes_accessed), transcendentals=int(transcendentals)
    )


def whole(shape):
    return pl.BlockSpec(shape, lambda *_: (0,) * len(shape))


SCALAR = pl.BlockSpec(memory_space=pltpu.SMEM)
UNREAD = pl.BlockSpec(memory_space=pl.ANY)
IN_VMEM = pl.BlockSpec(memory_space=pltpu.VMEM)


def request_kernel(shard_rows, ids_ref, out_ref):
    shards, capacity = out_ref.shape
    count = ids_ref.shape[1]
    ids = ids_ref[...]
    base = lax.broadcasted_iota(jnp.int32, (shards, 1), 0) * shard_rows
    row = ids - base
    mine = (row >= 0) & (row < shard_rows)
    one = jnp.where(mine, 1.0, 0.0)
    high = jnp.where(mine, row // 128, 0).astype(jnp.float32)
    low = jnp.where(mine, row % 128, 0).astype(jnp.float32)
    before = (
        lax.broadcasted_iota(jnp.int32, (LANES, LANES), 0)
        < lax.broadcasted_iota(jnp.int32, (LANES, LANES), 1)
    ).astype(jnp.bfloat16)
    carry = jnp.zeros((shards, 1), jnp.float32)
    places = []
    for start in range(0, count, LANES):
        part = one[:, start : start + LANES]
        inside = jnp.dot(part.astype(jnp.bfloat16), before, preferred_element_type=jnp.float32)
        rank = jnp.sum(part * (inside + carry), axis=0, keepdims=True)
        carry = carry + jnp.sum(part, axis=1, keepdims=True)
        slot = lax.broadcasted_iota(jnp.int32, (capacity, LANES), 0).astype(jnp.float32)
        places.append(jnp.where(slot == rank, 1.0, 0.0))
    place = jnp.concatenate(places, axis=1).astype(jnp.bfloat16)
    parts = jnp.concatenate([one, high, low], axis=0).astype(jnp.bfloat16)
    packed = lax.dot_general(
        parts, place, (((1,), (1,)), ((), ())), preferred_element_type=jnp.float32
    )
    filled = packed[:shards] > 0.5
    rows = packed[shards : 2 * shards] * 128.0 + packed[2 * shards :]
    out_ref[...] = jnp.where(filled, rows.astype(jnp.int32), -1)


def build_request(ids, shards, shard_rows):
    count = ids.shape[1]
    capacity = count // shards
    return pl.pallas_call(
        functools.partial(request_kernel, shard_rows),
        out_shape=jax.ShapeDtypeStruct((shards, capacity), jnp.int32),
        compiler_params=params(16),
        cost_estimate=cost(2 * 3 * shards * count * capacity, 16384),
        name="build_request",
    )(ids)


def partner_line(table_ref, me, offset):
    return table_ref[pl.ds(jnp.bitwise_xor(me, offset), 1), :]


def partner_columns(table_ref, me, members):
    return as_columns([partner_line(table_ref, me, o).astype(jnp.float32) for o in members])


def as_columns(lines):
    blocks = []
    for line in lines:
        for start in range(0, line.shape[1], LANES):
            piece = line[:, start : start + LANES]
            blocks.append(jnp.broadcast_to(piece, (LANES, piece.shape[1])).T)
    return jnp.concatenate(blocks, axis=0)


def store_blocks(refs, value):
    size = refs[0].shape[0]
    for index, ref in enumerate(refs):
        ref[...] = value[index * size : (index + 1) * size]


def pick_kernel(members, place_ref, wanted_ref, passages_ref, *out_refs):
    rows = passages_ref.shape[0]
    wanted = partner_columns(wanted_ref, place_ref[0], members)
    lane = lax.broadcasted_iota(jnp.int32, wanted.shape, 1).astype(jnp.float32)
    hot = jnp.concatenate(
        [
            jnp.where(wanted == lane + float(start), 1.0, 0.0).astype(jnp.bfloat16)
            for start in range(0, rows, LANES)
        ],
        axis=1,
    )
    picked = jnp.dot(hot, passages_ref[...], preferred_element_type=jnp.float32)
    store_blocks(out_refs, picked.astype(jnp.bfloat16))


def pick(place, wanted, passages, members):
    rows, width = passages.shape
    slots = len(members) * wanted.shape[1]
    shapes = [jax.ShapeDtypeStruct((wanted.shape[1], width), jnp.bfloat16)] * len(members)
    return pl.pallas_call(
        functools.partial(pick_kernel, members),
        out_shape=shapes,
        in_specs=[SCALAR, IN_VMEM, IN_VMEM],
        out_specs=[IN_VMEM] * len(shapes),
        compiler_params=params(12),
        cost_estimate=cost(
            2 * slots * rows * width * LIGHT,
            2 * (rows + slots) * width * LIGHT,
        ),
        name="pick_rows",
    )(place, wanted, passages)


def logits_kernel(members, scale, place_ref, request_ref, top_ref, total_ref, queries_ref, *refs):
    fetched_refs, (exps_ref, new_top_ref, new_total_ref) = refs[:-3], refs[-3:]
    me = place_ref[0]
    live = partner_columns(request_ref, me, members) >= 0.0
    fetched = jnp.concatenate([ref[...] for ref in fetched_refs], axis=0)
    for first in range(0, queries_ref.shape[0], QUERY_TILE):
        logits = lax.dot_general(
            fetched,
            queries_ref[first : first + QUERY_TILE, :],
            (((1,), (1,)), ((), ())),
            preferred_element_type=jnp.float32,
        )
        for start in range(0, QUERY_TILE, LANES):
            lanes = slice(first + start, first + start + LANES)
            part = jnp.where(live, scale * logits[:, start : start + LANES], DEAD)
            old_top = top_ref[:, lanes]
            top = jnp.maximum(old_top, jnp.max(part, axis=0, keepdims=True))
            exps = jnp.exp(part - top)
            exps_ref[:, lanes] = exps.astype(exps_ref.dtype)
            new_top_ref[:, lanes] = top
            new_total_ref[:, lanes] = total_ref[:, lanes] * jnp.exp(old_top - top) + jnp.sum(
                exps, axis=0, keepdims=True
            )


def group_logits(place, request, top, total, queries, fetched, members, scale):
    width = fetched[0].shape[1]
    slots = sum(rows.shape[0] for rows in fetched)
    count = queries.shape[0]
    shape = jax.ShapeDtypeStruct((1, count), jnp.float32)
    return pl.pallas_call(
        functools.partial(logits_kernel, members, scale),
        out_shape=(jax.ShapeDtypeStruct((slots, count), jnp.bfloat16), shape, shape),
        in_specs=[SCALAR] + [IN_VMEM] * (4 + len(fetched)),
        out_specs=(IN_VMEM,) * 3,
        compiler_params=params(14),
        cost_estimate=cost(
            2 * slots * width * count,
            2 * (slots + count) * width + 4 * slots * count,
            slots * count,
        ),
        name="group_logits",
    )(place, request, top, total, queries, *fetched)


def row_grad_kernel(factor, exps_ref, own_top_ref, top_ref, total_ref, queries_ref, *refs):
    weights_ref, *out_refs = refs
    share = factor * jnp.exp(own_top_ref[...] - top_ref[...]) / total_ref[...]
    weights = (exps_ref[...].astype(jnp.float32) * share).astype(jnp.bfloat16)
    weights_ref[...] = weights
    value = jnp.dot(weights, queries_ref[...], preferred_element_type=jnp.float32)
    store_blocks(out_refs, value.astype(jnp.bfloat16))


def row_grad(exps, own_top, top, total, queries, members, factor):
    slots, count = exps.shape
    width = queries.shape[1]
    block = (slots // len(members), width)
    shapes = [jax.ShapeDtypeStruct(block, jnp.bfloat16)] * len(members)
    weights, *grads = pl.pallas_call(
        functools.partial(row_grad_kernel, factor),
        out_shape=[jax.ShapeDtypeStruct((slots, count), jnp.bfloat16)] + shapes,
        in_specs=[IN_VMEM] * 5,
        out_specs=[IN_VMEM] * (1 + len(shapes)),
        compiler_params=params(14),
        cost_estimate=cost(
            2 * slots * width * count * LIGHT, 2 * slots * (width + count) * LIGHT
        ),
        name="row_grad",
    )(exps, own_top, top, total, queries)
    return weights, grads


def query_kernel(factor, sizes, pos_ref, top_ref, total_ref, positives_ref, *refs):
    weights_refs, rest = refs[: len(sizes)], refs[len(sizes) :]
    grad_ref = refs[-1]
    pos, top, total = pos_ref[...], top_ref[...], total_ref[...]
    coef = as_columns([factor * (jnp.exp(pos - top) / total - 1.0)])
    value = jnp.concatenate(
        [
            coef * positives_ref[:, start : start + LANES].astype(jnp.float32)
            for start in range(0, positives_ref.shape[1], LANES)
        ],
        axis=1,
    )
    first = 0
    for ref, size in zip(weights_refs, sizes):
        rows = jnp.concatenate([one[...] for one in rest[first : first + size]], axis=0)
        first += size
        value = value + lax.dot_general(
            ref[...], rows, (((0,), (0,)), ((), ())), preferred_element_type=jnp.float32
        )
    grad_ref[...] = value.astype(jnp.bfloat16)


def query_grad(pos, top, total, positives, weights, fetched, factor, part, grads):
    count, width = positives.shape
    tile = min(256, count // QUERY_PARTS)
    steps = count // QUERY_PARTS // tile
    first = part * steps
    line = pl.BlockSpec((1, tile), lambda t: (0, first + t))
    block = pl.BlockSpec((tile, width), lambda t: (first + t, 0))
    sizes = [len(group) for group in fetched]
    rows = [one for group in fetched for one in group]
    inputs = [pos, top, total, positives, *weights, *rows, *grads]
    slots = sum(one.shape[0] for one in weights)
    return pl.pallas_call(
        functools.partial(query_kernel, factor, sizes),
        out_shape=jax.ShapeDtypeStruct((count, width), jnp.bfloat16),
        grid=(steps,),
        in_specs=[line, line, line, block]
        + [pl.BlockSpec((one.shape[0], tile), lambda t: (0, first + t)) for one in weights]
        + [whole(one.shape) for one in rows]
        + [UNREAD] * len(grads),
        out_specs=block,
        input_output_aliases={len(inputs) - 1: 0} if grads else {},
        compiler_params=params(26),
        cost_estimate=cost(
            2 * slots * width * count // QUERY_PARTS,
            2 * slots * width + 4 * count * width // QUERY_PARTS,
        ),
        name="query_grad",
    )(*inputs)


def scatter_kernel(members, first, place_ref, wanted_ref, *refs):
    *value_refs, out_ref = refs
    base_ref = value_refs.pop(0) if value_refs[0].shape == out_ref.shape else None
    rows = out_ref.shape[0]
    me = place_ref[0]
    row = (first + pl.program_id(0)) * rows + lax.broadcasted_iota(jnp.int32, (rows, 1), 0)
    wanted = jnp.concatenate(
        [partner_line(wanted_ref, me, o) for o in members], axis=1
    )
    hot = jnp.where(wanted == row, 1.0, 0.0).astype(jnp.bfloat16)
    values = jnp.concatenate([ref[...] for ref in value_refs], axis=0)
    total = jnp.dot(hot, values, preferred_element_type=jnp.float32)
    if base_ref is not None:
        total = base_ref[...] + total
    out_ref[...] = total.astype(out_ref.dtype)


def scatter(place, wanted, values, members, base, shard_rows, part, parts, dtype):
    width = values[0].shape[1]
    slots = sum(one.shape[0] for one in values)
    rows = shard_rows // parts
    tile = 2 * LANES
    first = part * rows // tile
    return pl.pallas_call(
        functools.partial(scatter_kernel, members, first),
        out_shape=jax.ShapeDtypeStruct((rows, width), dtype),
        grid=(rows // tile,),
        in_specs=[SCALAR, whole(wanted.shape)]
        + [pl.BlockSpec((tile, width), lambda t: (first + t, 0))] * len(base)
        + [whole(one.shape) for one in values],
        out_specs=pl.BlockSpec((tile, width), lambda t: (t, 0)),
        compiler_params=params(18),
        cost_estimate=cost(
            2 * rows * slots * width, 2 * slots * width + 4 * (1 + len(base)) * rows * width
        ),
        name="scatter_rows",
    )(place, wanted, *base, *values)


def add_kernel(own_refs, other_refs, out_ref):
    rows = out_ref.shape[0]
    steps = own_refs[0].shape[0] // rows
    for part, (own_ref, other_ref) in enumerate(zip(own_refs, other_refs)):

        @pl.when(pl.program_id(0) // steps == part)
        def _():
            first = pl.multiple_of(pl.program_id(0) % steps * rows, rows)
            span = pl.ds(first, rows)
            total = own_ref[span, :].astype(jnp.float32) + other_ref[span, :].astype(jnp.float32)
            out_ref[...] = total.astype(jnp.bfloat16)


def add_cores(own, other):
    rows, width = own[0].shape
    parts = len(own)
    tile = min(256, rows)
    return pl.pallas_call(
        lambda *refs: add_kernel(refs[:parts], refs[parts:-1], refs[-1]),
        out_shape=jax.ShapeDtypeStruct((rows * parts, width), jnp.bfloat16),
        grid=(rows * parts // tile,),
        in_specs=[IN_VMEM] * (2 * parts),
        out_specs=pl.BlockSpec((tile, width), lambda t: (t, 0)),
        compiler_params=params(8),
        cost_estimate=cost(rows * parts * width, 6 * rows * parts * width),
        name="add_cores",
    )(*own, *other)


def behind(value, earlier):
    if not earlier:
        return value
    return lax.optimization_barrier((value, *earlier))[0]


def exchange(blocks, members, shards):
    return [
        block
        if offset == 0
        else lax.ppermute(block, "idx", [(i, i ^ offset) for i in range(shards)])
        for block, offset in zip(blocks, members)
    ]


def partner_groups(shards, per):
    half = shards // 2
    quarter = half // 2
    far = [half + part * quarter + place for place in range(quarter) for part in range(2)]
    near = [*range(quarter, half), *range(1, quarter)]
    near = [near.pop(), 0, *near] if per == 2 else [0, *near]
    far = [tuple(far[i : i + per]) for i in range(0, half, per)]
    near = [tuple(near[i : i + per]) for i in range(0, half, per)]
    return [group for pair in zip(near, far) for group in pair]


def local(queries, positives, passages, negatives):
    shards = lax.axis_size("idx")
    shard_rows, width = passages.shape
    ids = negatives.reshape(1, -1)
    capacity = ids.shape[1] // shards
    scale = 3.0 / math.sqrt(width)
    factor = LSCALE * scale
    groups = partner_groups(shards, max(1, GROUP_SLOTS // capacity))
    place = lax.axis_index("idx").astype(jnp.int32).reshape(1)

    request = build_request(ids, shards, shard_rows)
    wanted = lax.all_to_all(request, "idx", split_axis=0, concat_axis=0, tiled=True)
    pos_logit = scale * jnp.sum(
        queries.astype(jnp.float32) * positives.astype(jnp.float32), axis=1
    )
    pos_logit = pos_logit.reshape(1, -1)

    fetched = []
    for index, group in enumerate(groups):
        earlier = fetched[index - WINDOW][-1:] if index >= WINDOW else [pos_logit]
        picked = pick(behind(place, earlier), wanted, passages, group)
        fetched.append(exchange(picked, group, shards))

    top, total = pos_logit, jnp.ones_like(pos_logit)
    exps, tops = [], []
    for group, rows in zip(groups, fetched):
        value, top, total = group_logits(
            place, request, top, total, queries, rows, group, scale
        )
        exps.append(value)
        tops.append(top)
    loss = top + jnp.log(total) - pos_logit

    order = [1, 0, *range(2, len(groups))]
    weights, grads, last = [None] * len(groups), {}, []
    for index in order:
        weights[index], grads[index] = row_grad(
            exps[index], behind(tops[index], last), top, total, queries, groups[index], factor
        )
        last = grads[index][-1:]

    grad_queries = []
    for part in range(QUERY_PARTS):
        done = query_grad(
            pos_logit,
            top,
            total,
            positives,
            weights,
            fetched,
            factor,
            part,
            grad_queries[-1:],
        )
        grad_queries.append(done)

    sums, returned = [], {}

    def scattered(indices, part=0, parts=1, dtype=jnp.float32):
        return scatter(
            place,
            wanted,
            [one for index in indices for one in returned[index]],
            sum((groups[index] for index in indices), ()),
            sums[-1:],
            shard_rows,
            part,
            parts,
            dtype,
        )

    first_query = len(order) - 1 - QUERY_PARTS
    for step, index in enumerate(order):
        blocks = grads[index]
        if step >= WINDOW:
            sums.append(scattered([order[step - WINDOW]]))
            earlier = sums[-1:]
            if first_query <= step < first_query + QUERY_PARTS:
                earlier = earlier + [grad_queries[step - first_query]]
            blocks = [behind(blocks[0], earlier), *blocks[1:]]
        returned[index] = exchange(blocks, groups[index], shards)
    sums.append(scattered(order[-WINDOW:-1]))
    parts = [
        scattered(order[-1:], part, SUM_PARTS, jnp.bfloat16) for part in range(SUM_PARTS)
    ]
    grad_passages = add_cores(parts, [lax.ppermute(own, "enc", SWAP) for own in parts])
    return (loss.reshape(-1), grad_queries[-1], grad_passages)


def solution(mesh):
    placed = (
        P(("idx", "enc"), None),
        P(("idx", "enc"), None),
        P("idx", None),
        P(("idx", "enc"), None),
    )
    return jax.shard_map(
        local,
        mesh=mesh,
        in_specs=placed,
        out_specs=(P(("idx", "enc")), P(("idx", "enc"), None), P("idx", None)),
        check_vma=False,
    )
```

```python
import functools
import math

import jax
import jax.numpy as jnp
from jax import lax
from jax.experimental import pallas as pl
from jax.experimental.pallas import tpu as pltpu
from jax.sharding import PartitionSpec as P

LSCALE = 32
DEAD = -1e30
LANES = 128
MIB = 1 << 20
GROUP_SLOTS = 256
WINDOW = 4
LIGHT = 0.1
QUERY_TILE = 256
QUERY_PARTS = 2
SUM_PARTS = 4
SWAP = [(0, 1), (1, 0)]


def params(vmem_mib):
    return pltpu.CompilerParams(vmem_limit_bytes=vmem_mib * MIB)


def cost(flops, bytes_accessed, transcendentals=0):
    return pl.CostEstimate(
        flops=int(flops), bytes_accessed=int(bytes_accessed), transcendentals=int(transcendentals)
    )


def whole(shape):
    return pl.BlockSpec(shape, lambda *_: (0,) * len(shape))


SCALAR = pl.BlockSpec(memory_space=pltpu.SMEM)
UNREAD = pl.BlockSpec(memory_space=pl.ANY)
IN_VMEM = pl.BlockSpec(memory_space=pltpu.VMEM)


def request_kernel(shard_rows, ids_ref, out_ref):
    shards, capacity = out_ref.shape
    count = ids_ref.shape[1]
    ids = ids_ref[...]
    base = lax.broadcasted_iota(jnp.int32, (shards, 1), 0) * shard_rows
    row = ids - base
    mine = (row >= 0) & (row < shard_rows)
    one = jnp.where(mine, 1.0, 0.0)
    high = jnp.where(mine, row // 128, 0).astype(jnp.float32)
    low = jnp.where(mine, row % 128, 0).astype(jnp.float32)
    before = (
        lax.broadcasted_iota(jnp.int32, (LANES, LANES), 0)
        < lax.broadcasted_iota(jnp.int32, (LANES, LANES), 1)
    ).astype(jnp.bfloat16)
    carry = jnp.zeros((shards, 1), jnp.float32)
    places = []
    for start in range(0, count, LANES):
        part = one[:, start : start + LANES]
        inside = jnp.dot(part.astype(jnp.bfloat16), before, preferred_element_type=jnp.float32)
        rank = jnp.sum(part * (inside + carry), axis=0, keepdims=True)
        carry = carry + jnp.sum(part, axis=1, keepdims=True)
        slot = lax.broadcasted_iota(jnp.int32, (capacity, LANES), 0).astype(jnp.float32)
        places.append(jnp.where(slot == rank, 1.0, 0.0))
    place = jnp.concatenate(places, axis=1).astype(jnp.bfloat16)
    parts = jnp.concatenate([one, high, low], axis=0).astype(jnp.bfloat16)
    packed = lax.dot_general(
        parts, place, (((1,), (1,)), ((), ())), preferred_element_type=jnp.float32
    )
    filled = packed[:shards] > 0.5
    rows = packed[shards : 2 * shards] * 128.0 + packed[2 * shards :]
    out_ref[...] = jnp.where(filled, rows.astype(jnp.int32), -1)


def build_request(ids, shards, shard_rows):
    count = ids.shape[1]
    capacity = count // shards
    return pl.pallas_call(
        functools.partial(request_kernel, shard_rows),
        out_shape=jax.ShapeDtypeStruct((shards, capacity), jnp.int32),
        compiler_params=params(16),
        cost_estimate=cost(2 * 3 * shards * count * capacity, 16384),
        name="build_request",
    )(ids)


def partner_line(table_ref, me, offset):
    return table_ref[pl.ds(jnp.bitwise_xor(me, offset), 1), :]


def partner_columns(table_ref, me, members):
    return as_columns([partner_line(table_ref, me, o).astype(jnp.float32) for o in members])


def as_columns(lines):
    blocks = []
    for line in lines:
        for start in range(0, line.shape[1], LANES):
            piece = line[:, start : start + LANES]
            blocks.append(jnp.broadcast_to(piece, (LANES, piece.shape[1])).T)
    return jnp.concatenate(blocks, axis=0)


def store_blocks(refs, value):
    size = refs[0].shape[0]
    for index, ref in enumerate(refs):
        ref[...] = value[index * size : (index + 1) * size]


def pick_kernel(members, place_ref, wanted_ref, passages_ref, *out_refs):
    rows = passages_ref.shape[0]
    wanted = partner_columns(wanted_ref, place_ref[0], members)
    lane = lax.broadcasted_iota(jnp.int32, wanted.shape, 1).astype(jnp.float32)
    hot = jnp.concatenate(
        [
            jnp.where(wanted == lane + float(start), 1.0, 0.0).astype(jnp.bfloat16)
            for start in range(0, rows, LANES)
        ],
        axis=1,
    )
    picked = jnp.dot(hot, passages_ref[...], preferred_element_type=jnp.float32)
    store_blocks(out_refs, picked.astype(jnp.bfloat16))


def pick(place, wanted, passages, members):
    rows, width = passages.shape
    slots = len(members) * wanted.shape[1]
    shapes = [jax.ShapeDtypeStruct((wanted.shape[1], width), jnp.bfloat16)] * len(members)
    return pl.pallas_call(
        functools.partial(pick_kernel, members),
        out_shape=shapes,
        in_specs=[SCALAR, IN_VMEM, IN_VMEM],
        out_specs=[IN_VMEM] * len(shapes),
        compiler_params=params(12),
        cost_estimate=cost(
            2 * slots * rows * width * LIGHT,
            2 * (rows + slots) * width * LIGHT,
        ),
        name="pick_rows",
    )(place, wanted, passages)


def logits_kernel(members, scale, place_ref, request_ref, top_ref, total_ref, queries_ref, *refs):
    fetched_refs, (exps_ref, new_top_ref, new_total_ref) = refs[:-3], refs[-3:]
    me = place_ref[0]
    live = partner_columns(request_ref, me, members) >= 0.0
    fetched = jnp.concatenate([ref[...] for ref in fetched_refs], axis=0)
    for first in range(0, queries_ref.shape[0], QUERY_TILE):
        logits = lax.dot_general(
            fetched,
            queries_ref[first : first + QUERY_TILE, :],
            (((1,), (1,)), ((), ())),
            preferred_element_type=jnp.float32,
        )
        for start in range(0, QUERY_TILE, LANES):
            lanes = slice(first + start, first + start + LANES)
            part = jnp.where(live, scale * logits[:, start : start + LANES], DEAD)
            old_top = top_ref[:, lanes]
            top = jnp.maximum(old_top, jnp.max(part, axis=0, keepdims=True))
            exps = jnp.exp(part - top)
            exps_ref[:, lanes] = exps.astype(exps_ref.dtype)
            new_top_ref[:, lanes] = top
            new_total_ref[:, lanes] = total_ref[:, lanes] * jnp.exp(old_top - top) + jnp.sum(
                exps, axis=0, keepdims=True
            )


def group_logits(place, request, top, total, queries, fetched, members, scale):
    width = fetched[0].shape[1]
    slots = sum(rows.shape[0] for rows in fetched)
    count = queries.shape[0]
    shape = jax.ShapeDtypeStruct((1, count), jnp.float32)
    return pl.pallas_call(
        functools.partial(logits_kernel, members, scale),
        out_shape=(jax.ShapeDtypeStruct((slots, count), jnp.bfloat16), shape, shape),
        in_specs=[SCALAR] + [IN_VMEM] * (4 + len(fetched)),
        out_specs=(IN_VMEM,) * 3,
        compiler_params=params(14),
        cost_estimate=cost(
            2 * slots * width * count,
            2 * (slots + count) * width + 4 * slots * count,
            slots * count,
        ),
        name="group_logits",
    )(place, request, top, total, queries, *fetched)


def row_grad_kernel(factor, exps_ref, own_top_ref, top_ref, total_ref, queries_ref, *refs):
    weights_ref, *out_refs = refs
    share = factor * jnp.exp(own_top_ref[...] - top_ref[...]) / total_ref[...]
    weights = (exps_ref[...].astype(jnp.float32) * share).astype(jnp.bfloat16)
    weights_ref[...] = weights
    value = jnp.dot(weights, queries_ref[...], preferred_element_type=jnp.float32)
    store_blocks(out_refs, value.astype(jnp.bfloat16))


def row_grad(exps, own_top, top, total, queries, members, factor):
    slots, count = exps.shape
    width = queries.shape[1]
    block = (slots // len(members), width)
    shapes = [jax.ShapeDtypeStruct(block, jnp.bfloat16)] * len(members)
    weights, *grads = pl.pallas_call(
        functools.partial(row_grad_kernel, factor),
        out_shape=[jax.ShapeDtypeStruct((slots, count), jnp.bfloat16)] + shapes,
        in_specs=[IN_VMEM] * 5,
        out_specs=[IN_VMEM] * (1 + len(shapes)),
        compiler_params=params(14),
        cost_estimate=cost(
            2 * slots * width * count * LIGHT, 2 * slots * (width + count) * LIGHT
        ),
        name="row_grad",
    )(exps, own_top, top, total, queries)
    return weights, grads


def query_kernel(factor, sizes, pos_ref, top_ref, total_ref, positives_ref, *refs):
    weights_refs, rest = refs[: len(sizes)], refs[len(sizes) :]
    grad_ref = refs[-1]
    pos, top, total = pos_ref[...], top_ref[...], total_ref[...]
    coef = as_columns([factor * (jnp.exp(pos - top) / total - 1.0)])
    value = jnp.concatenate(
        [
            coef * positives_ref[:, start : start + LANES].astype(jnp.float32)
            for start in range(0, positives_ref.shape[1], LANES)
        ],
        axis=1,
    )
    first = 0
    for ref, size in zip(weights_refs, sizes):
        rows = jnp.concatenate([one[...] for one in rest[first : first + size]], axis=0)
        first += size
        value = value + lax.dot_general(
            ref[...], rows, (((0,), (0,)), ((), ())), preferred_element_type=jnp.float32
        )
    grad_ref[...] = value.astype(jnp.bfloat16)


def query_grad(pos, top, total, positives, weights, fetched, factor, part, grads):
    count, width = positives.shape
    tile = min(256, count // QUERY_PARTS)
    steps = count // QUERY_PARTS // tile
    first = part * steps
    line = pl.BlockSpec((1, tile), lambda t: (0, first + t))
    block = pl.BlockSpec((tile, width), lambda t: (first + t, 0))
    sizes = [len(group) for group in fetched]
    rows = [one for group in fetched for one in group]
    inputs = [pos, top, total, positives, *weights, *rows, *grads]
    slots = sum(one.shape[0] for one in weights)
    return pl.pallas_call(
        functools.partial(query_kernel, factor, sizes),
        out_shape=jax.ShapeDtypeStruct((count, width), jnp.bfloat16),
        grid=(steps,),
        in_specs=[line, line, line, block]
        + [pl.BlockSpec((one.shape[0], tile), lambda t: (0, first + t)) for one in weights]
        + [whole(one.shape) for one in rows]
        + [UNREAD] * len(grads),
        out_specs=block,
        input_output_aliases={len(inputs) - 1: 0} if grads else {},
        compiler_params=params(26),
        cost_estimate=cost(
            2 * slots * width * count // QUERY_PARTS,
            2 * slots * width + 4 * count * width // QUERY_PARTS,
        ),
        name="query_grad",
    )(*inputs)


def scatter_kernel(members, first, place_ref, wanted_ref, *refs):
    *value_refs, out_ref = refs
    base_ref = value_refs.pop(0) if value_refs[0].shape == out_ref.shape else None
    rows = out_ref.shape[0]
    me = place_ref[0]
    row = (first + pl.program_id(0)) * rows + lax.broadcasted_iota(jnp.int32, (rows, 1), 0)
    wanted = jnp.concatenate(
        [partner_line(wanted_ref, me, o) for o in members], axis=1
    )
    hot = jnp.where(wanted == row, 1.0, 0.0).astype(jnp.bfloat16)
    values = jnp.concatenate([ref[...] for ref in value_refs], axis=0)
    total = jnp.dot(hot, values, preferred_element_type=jnp.float32)
    if base_ref is not None:
        total = base_ref[...] + total
    out_ref[...] = total.astype(out_ref.dtype)


def scatter(place, wanted, values, members, base, shard_rows, part, parts, dtype):
    width = values[0].shape[1]
    slots = sum(one.shape[0] for one in values)
    rows = shard_rows // parts
    tile = 2 * LANES
    first = part * rows // tile
    return pl.pallas_call(
        functools.partial(scatter_kernel, members, first),
        out_shape=jax.ShapeDtypeStruct((rows, width), dtype),
        grid=(rows // tile,),
        in_specs=[SCALAR, whole(wanted.shape)]
        + [pl.BlockSpec((tile, width), lambda t: (first + t, 0))] * len(base)
        + [whole(one.shape) for one in values],
        out_specs=pl.BlockSpec((tile, width), lambda t: (t, 0)),
        compiler_params=params(18),
        cost_estimate=cost(
            2 * rows * slots * width, 2 * slots * width + 4 * (1 + len(base)) * rows * width
        ),
        name="scatter_rows",
    )(place, wanted, *base, *values)


def add_kernel(own_refs, other_refs, out_ref):
    rows = out_ref.shape[0]
    steps = own_refs[0].shape[0] // rows
    for part, (own_ref, other_ref) in enumerate(zip(own_refs, other_refs)):

        @pl.when(pl.program_id(0) // steps == part)
        def _():
            first = pl.multiple_of(pl.program_id(0) % steps * rows, rows)
            span = pl.ds(first, rows)
            total = own_ref[span, :].astype(jnp.float32) + other_ref[span, :].astype(jnp.float32)
            out_ref[...] = total.astype(jnp.bfloat16)


def add_cores(own, other):
    rows, width = own[0].shape
    parts = len(own)
    tile = min(512, rows)
    return pl.pallas_call(
        lambda *refs: add_kernel(refs[:parts], refs[parts:-1], refs[-1]),
        out_shape=jax.ShapeDtypeStruct((rows * parts, width), jnp.bfloat16),
        grid=(rows * parts // tile,),
        in_specs=[IN_VMEM] * (2 * parts),
        out_specs=pl.BlockSpec((tile, width), lambda t: (t, 0)),
        compiler_params=params(8),
        cost_estimate=cost(rows * parts * width, 6 * rows * parts * width),
        name="add_cores",
    )(*own, *other)


def behind(value, earlier):
    if not earlier:
        return value
    return lax.optimization_barrier((value, *earlier))[0]


def exchange(blocks, members, shards):
    return [
        block
        if offset == 0
        else lax.ppermute(block, "idx", [(i, i ^ offset) for i in range(shards)])
        for block, offset in zip(blocks, members)
    ]


def partner_groups(shards, per):
    half = shards // 2
    quarter = half // 2
    far = [half + part * quarter + place for place in range(quarter) for part in range(2)]
    near = [*range(quarter, half), *range(1, quarter)]
    near = [near.pop(), 0, *near] if per == 2 else [0, *near]
    far = [tuple(far[i : i + per]) for i in range(0, half, per)]
    near = [tuple(near[i : i + per]) for i in range(0, half, per)]
    return [*far[:2], *near[:2], far[2], near[2], near[3], far[3]]


def local(queries, positives, passages, negatives):
    shards = lax.axis_size("idx")
    shard_rows, width = passages.shape
    ids = negatives.reshape(1, -1)
    capacity = ids.shape[1] // shards
    scale = 3.0 / math.sqrt(width)
    factor = LSCALE * scale
    groups = partner_groups(shards, max(1, GROUP_SLOTS // capacity))
    place = lax.axis_index("idx").astype(jnp.int32).reshape(1)

    request = build_request(ids, shards, shard_rows)
    wanted = lax.all_to_all(request, "idx", split_axis=0, concat_axis=0, tiled=True)
    pos_logit = scale * jnp.sum(
        queries.astype(jnp.float32) * positives.astype(jnp.float32), axis=1
    )
    pos_logit = pos_logit.reshape(1, -1)

    fetched, last = [None] * len(groups), [pos_logit]
    for step, index in enumerate(range(len(groups))):
        earlier = last
        picked = pick(behind(place, earlier), wanted, passages, groups[index])
        fetched[index] = exchange(picked, groups[index], shards)
        last = picked[-1:]

    top, total = pos_logit, jnp.ones_like(pos_logit)
    exps, tops = [], []
    for group, rows in zip(groups, fetched):
        value, top, total = group_logits(
            place, request, top, total, queries, rows, group, scale
        )
        exps.append(value)
        tops.append(top)
    loss = top + jnp.log(total) - pos_logit

    order = [*range(len(groups))]
    weights, grads, last = [None] * len(groups), {}, []
    for index in order:
        weights[index], grads[index] = row_grad(
            exps[index], behind(tops[index], last), top, total, queries, groups[index], factor
        )
        last = grads[index][-1:]

    grad_queries = []
    for part in range(QUERY_PARTS):
        done = query_grad(
            pos_logit,
            top,
            total,
            positives,
            weights,
            fetched,
            factor,
            part,
            grad_queries[-1:],
        )
        grad_queries.append(done)

    sums, returned = [], {}

    def scattered(indices, part=0, parts=1, dtype=jnp.float32):
        return scatter(
            place,
            wanted,
            [one for index in indices for one in returned[index]],
            sum((groups[index] for index in indices), ()),
            sums[-1:],
            shard_rows,
            part,
            parts,
            dtype,
        )

    first_query = len(order) - 1 - QUERY_PARTS
    for step, index in enumerate(order):
        blocks = grads[index]
        if step >= WINDOW:
            sums.append(scattered([order[step - WINDOW]]))
            earlier = sums[-1:]
            if first_query <= step < first_query + QUERY_PARTS:
                earlier = earlier + [grad_queries[step - first_query]]
            blocks = [behind(blocks[0], earlier), *blocks[1:]]
        returned[index] = exchange(blocks, groups[index], shards)
    sums.append(scattered(order[-WINDOW:-1]))
    parts = [
        scattered(order[-1:], part, SUM_PARTS, jnp.bfloat16) for part in range(SUM_PARTS)
    ]
    grad_passages = add_cores(parts, [lax.ppermute(own, "enc", SWAP) for own in parts])
    return (loss.reshape(-1), grad_queries[-1], grad_passages)


def solution(mesh):
    placed = (
        P(("idx", "enc"), None),
        P(("idx", "enc"), None),
        P("idx", None),
        P(("idx", "enc"), None),
    )
    return jax.shard_map(
        local,
        mesh=mesh,
        in_specs=placed,
        out_specs=(P(("idx", "enc")), P(("idx", "enc"), None), P("idx", None)),
        check_vma=False,
    )
```

```python
import functools
import math

import jax
import jax.numpy as jnp
from jax import lax
from jax.experimental import pallas as pl
from jax.experimental.pallas import tpu as pltpu
from jax.sharding import PartitionSpec as P

LSCALE = 32
DEAD = -1e30
LANES = 128
MIB = 1 << 20
GROUP_SLOTS = 256
WINDOW = 4
LIGHT = 0.1
QUERY_TILE = 256
QUERY_PARTS = 2
SUM_PARTS = 4
SWAP = [(0, 1), (1, 0)]


def params(vmem_mib):
    return pltpu.CompilerParams(vmem_limit_bytes=vmem_mib * MIB)


def cost(flops, bytes_accessed, transcendentals=0):
    return pl.CostEstimate(
        flops=int(flops), bytes_accessed=int(bytes_accessed), transcendentals=int(transcendentals)
    )


def whole(shape):
    return pl.BlockSpec(shape, lambda *_: (0,) * len(shape))


SCALAR = pl.BlockSpec(memory_space=pltpu.SMEM)
UNREAD = pl.BlockSpec(memory_space=pl.ANY)
IN_VMEM = pl.BlockSpec(memory_space=pltpu.VMEM)


def request_kernel(shard_rows, ids_ref, out_ref):
    shards, capacity = out_ref.shape
    count = ids_ref.shape[1]
    ids = ids_ref[...]
    base = lax.broadcasted_iota(jnp.int32, (shards, 1), 0) * shard_rows
    row = ids - base
    mine = (row >= 0) & (row < shard_rows)
    one = jnp.where(mine, 1.0, 0.0)
    high = jnp.where(mine, row // 128, 0).astype(jnp.float32)
    low = jnp.where(mine, row % 128, 0).astype(jnp.float32)
    before = (
        lax.broadcasted_iota(jnp.int32, (LANES, LANES), 0)
        < lax.broadcasted_iota(jnp.int32, (LANES, LANES), 1)
    ).astype(jnp.bfloat16)
    carry = jnp.zeros((shards, 1), jnp.float32)
    places = []
    for start in range(0, count, LANES):
        part = one[:, start : start + LANES]
        inside = jnp.dot(part.astype(jnp.bfloat16), before, preferred_element_type=jnp.float32)
        rank = jnp.sum(part * (inside + carry), axis=0, keepdims=True)
        carry = carry + jnp.sum(part, axis=1, keepdims=True)
        slot = lax.broadcasted_iota(jnp.int32, (capacity, LANES), 0).astype(jnp.float32)
        places.append(jnp.where(slot == rank, 1.0, 0.0))
    place = jnp.concatenate(places, axis=1).astype(jnp.bfloat16)
    parts = jnp.concatenate([one, high, low], axis=0).astype(jnp.bfloat16)
    packed = lax.dot_general(
        parts, place, (((1,), (1,)), ((), ())), preferred_element_type=jnp.float32
    )
    filled = packed[:shards] > 0.5
    rows = packed[shards : 2 * shards] * 128.0 + packed[2 * shards :]
    out_ref[...] = jnp.where(filled, rows.astype(jnp.int32), -1)


def build_request(ids, shards, shard_rows):
    count = ids.shape[1]
    capacity = count // shards
    return pl.pallas_call(
        functools.partial(request_kernel, shard_rows),
        out_shape=jax.ShapeDtypeStruct((shards, capacity), jnp.int32),
        compiler_params=params(16),
        cost_estimate=cost(2 * 3 * shards * count * capacity, 16384),
        name="build_request",
    )(ids)


def partner_line(table_ref, me, offset):
    return table_ref[pl.ds(jnp.bitwise_xor(me, offset), 1), :]


def partner_columns(table_ref, me, members):
    return as_columns([partner_line(table_ref, me, o).astype(jnp.float32) for o in members])


def as_columns(lines):
    blocks = []
    for line in lines:
        for start in range(0, line.shape[1], LANES):
            piece = line[:, start : start + LANES]
            blocks.append(jnp.broadcast_to(piece, (LANES, piece.shape[1])).T)
    return jnp.concatenate(blocks, axis=0)


def store_blocks(refs, value):
    size = refs[0].shape[0]
    for index, ref in enumerate(refs):
        ref[...] = value[index * size : (index + 1) * size]


def pick_kernel(members, place_ref, wanted_ref, passages_ref, *out_refs):
    rows = passages_ref.shape[0]
    wanted = partner_columns(wanted_ref, place_ref[0], members)
    lane = lax.broadcasted_iota(jnp.int32, wanted.shape, 1).astype(jnp.float32)
    hot = jnp.concatenate(
        [
            jnp.where(wanted == lane + float(start), 1.0, 0.0).astype(jnp.bfloat16)
            for start in range(0, rows, LANES)
        ],
        axis=1,
    )
    picked = jnp.dot(hot, passages_ref[...], preferred_element_type=jnp.float32)
    store_blocks(out_refs, picked.astype(jnp.bfloat16))


def pick(place, wanted, passages, members):
    rows, width = passages.shape
    slots = len(members) * wanted.shape[1]
    shapes = [jax.ShapeDtypeStruct((wanted.shape[1], width), jnp.bfloat16)] * len(members)
    return pl.pallas_call(
        functools.partial(pick_kernel, members),
        out_shape=shapes,
        in_specs=[SCALAR, IN_VMEM, IN_VMEM],
        out_specs=[IN_VMEM] * len(shapes),
        compiler_params=params(12),
        cost_estimate=cost(
            2 * slots * rows * width * LIGHT,
            2 * (rows + slots) * width * LIGHT,
        ),
        name="pick_rows",
    )(place, wanted, passages)


def logits_kernel(members, scale, place_ref, request_ref, top_ref, total_ref, queries_ref, *refs):
    fetched_refs, (exps_ref, new_top_ref, new_total_ref) = refs[:-3], refs[-3:]
    me = place_ref[0]
    live = partner_columns(request_ref, me, members) >= 0.0
    fetched = jnp.concatenate([ref[...] for ref in fetched_refs], axis=0)
    for first in range(0, queries_ref.shape[0], QUERY_TILE):
        logits = lax.dot_general(
            fetched,
            queries_ref[first : first + QUERY_TILE, :],
            (((1,), (1,)), ((), ())),
            preferred_element_type=jnp.float32,
        )
        for start in range(0, QUERY_TILE, LANES):
            lanes = slice(first + start, first + start + LANES)
            part = jnp.where(live, scale * logits[:, start : start + LANES], DEAD)
            old_top = top_ref[:, lanes]
            top = jnp.maximum(old_top, jnp.max(part, axis=0, keepdims=True))
            exps = jnp.exp(part - top)
            exps_ref[:, lanes] = exps.astype(exps_ref.dtype)
            new_top_ref[:, lanes] = top
            new_total_ref[:, lanes] = total_ref[:, lanes] * jnp.exp(old_top - top) + jnp.sum(
                exps, axis=0, keepdims=True
            )


def group_logits(place, request, top, total, queries, fetched, members, scale):
    width = fetched[0].shape[1]
    slots = sum(rows.shape[0] for rows in fetched)
    count = queries.shape[0]
    shape = jax.ShapeDtypeStruct((1, count), jnp.float32)
    return pl.pallas_call(
        functools.partial(logits_kernel, members, scale),
        out_shape=(jax.ShapeDtypeStruct((slots, count), jnp.bfloat16), shape, shape),
        in_specs=[SCALAR] + [IN_VMEM] * (4 + len(fetched)),
        out_specs=(IN_VMEM,) * 3,
        compiler_params=params(14),
        cost_estimate=cost(
            2 * slots * width * count,
            2 * (slots + count) * width + 4 * slots * count,
            slots * count,
        ),
        name="group_logits",
    )(place, request, top, total, queries, *fetched)


def row_grad_kernel(factor, exps_ref, own_top_ref, top_ref, total_ref, queries_ref, *refs):
    weights_ref, *out_refs = refs
    share = factor * jnp.exp(own_top_ref[...] - top_ref[...]) / total_ref[...]
    weights = (exps_ref[...].astype(jnp.float32) * share).astype(jnp.bfloat16)
    weights_ref[...] = weights
    value = jnp.dot(weights, queries_ref[...], preferred_element_type=jnp.float32)
    store_blocks(out_refs, value.astype(jnp.bfloat16))


def row_grad(exps, own_top, top, total, queries, members, factor):
    slots, count = exps.shape
    width = queries.shape[1]
    block = (slots // len(members), width)
    shapes = [jax.ShapeDtypeStruct(block, jnp.bfloat16)] * len(members)
    weights, *grads = pl.pallas_call(
        functools.partial(row_grad_kernel, factor),
        out_shape=[jax.ShapeDtypeStruct((slots, count), jnp.bfloat16)] + shapes,
        in_specs=[IN_VMEM] * 5,
        out_specs=[IN_VMEM] * (1 + len(shapes)),
        compiler_params=params(14),
        cost_estimate=cost(
            2 * slots * width * count * LIGHT, 2 * slots * (width + count) * LIGHT
        ),
        name="row_grad",
    )(exps, own_top, top, total, queries)
    return weights, grads


def query_kernel(factor, sizes, pos_ref, top_ref, total_ref, positives_ref, *refs):
    weights_refs, rest = refs[: len(sizes)], refs[len(sizes) :]
    grad_ref = refs[-1]
    pos, top, total = pos_ref[...], top_ref[...], total_ref[...]
    coef = as_columns([factor * (jnp.exp(pos - top) / total - 1.0)])
    value = jnp.concatenate(
        [
            coef * positives_ref[:, start : start + LANES].astype(jnp.float32)
            for start in range(0, positives_ref.shape[1], LANES)
        ],
        axis=1,
    )
    first = 0
    for ref, size in zip(weights_refs, sizes):
        rows = jnp.concatenate([one[...] for one in rest[first : first + size]], axis=0)
        first += size
        value = value + lax.dot_general(
            ref[...], rows, (((0,), (0,)), ((), ())), preferred_element_type=jnp.float32
        )
    grad_ref[...] = value.astype(jnp.bfloat16)


def query_grad(pos, top, total, positives, weights, fetched, factor, part, grads):
    count, width = positives.shape
    tile = min(256, count // QUERY_PARTS)
    steps = count // QUERY_PARTS // tile
    first = part * steps
    line = pl.BlockSpec((1, tile), lambda t: (0, first + t))
    block = pl.BlockSpec((tile, width), lambda t: (first + t, 0))
    sizes = [len(group) for group in fetched]
    rows = [one for group in fetched for one in group]
    inputs = [pos, top, total, positives, *weights, *rows, *grads]
    slots = sum(one.shape[0] for one in weights)
    return pl.pallas_call(
        functools.partial(query_kernel, factor, sizes),
        out_shape=jax.ShapeDtypeStruct((count, width), jnp.bfloat16),
        grid=(steps,),
        in_specs=[line, line, line, block]
        + [pl.BlockSpec((one.shape[0], tile), lambda t: (0, first + t)) for one in weights]
        + [whole(one.shape) for one in rows]
        + [UNREAD] * len(grads),
        out_specs=block,
        input_output_aliases={len(inputs) - 1: 0} if grads else {},
        compiler_params=params(26),
        cost_estimate=cost(
            2 * slots * width * count // QUERY_PARTS,
            2 * slots * width + 4 * count * width // QUERY_PARTS,
        ),
        name="query_grad",
    )(*inputs)


def scatter_kernel(members, first, place_ref, wanted_ref, *refs):
    *value_refs, out_ref = refs
    base_ref = value_refs.pop(0) if value_refs[0].shape == out_ref.shape else None
    rows = out_ref.shape[0]
    me = place_ref[0]
    row = (first + pl.program_id(0)) * rows + lax.broadcasted_iota(jnp.int32, (rows, 1), 0)
    wanted = jnp.concatenate(
        [partner_line(wanted_ref, me, o) for o in members], axis=1
    )
    hot = jnp.where(wanted == row, 1.0, 0.0).astype(jnp.bfloat16)
    values = jnp.concatenate([ref[...] for ref in value_refs], axis=0)
    total = jnp.dot(hot, values, preferred_element_type=jnp.float32)
    if base_ref is not None:
        total = base_ref[...] + total
    out_ref[...] = total.astype(out_ref.dtype)


def scatter(place, wanted, values, members, base, shard_rows, part, parts, dtype):
    width = values[0].shape[1]
    slots = sum(one.shape[0] for one in values)
    rows = shard_rows // parts
    tile = 2 * LANES
    first = part * rows // tile
    return pl.pallas_call(
        functools.partial(scatter_kernel, members, first),
        out_shape=jax.ShapeDtypeStruct((rows, width), dtype),
        grid=(rows // tile,),
        in_specs=[SCALAR, whole(wanted.shape)]
        + [pl.BlockSpec((tile, width), lambda t: (first + t, 0))] * len(base)
        + [whole(one.shape) for one in values],
        out_specs=pl.BlockSpec((tile, width), lambda t: (t, 0)),
        compiler_params=params(18),
        cost_estimate=cost(
            2 * rows * slots * width, 2 * slots * width + 4 * (1 + len(base)) * rows * width
        ),
        name="scatter_rows",
    )(place, wanted, *base, *values)


def add_kernel(own_refs, other_refs, out_ref):
    rows = out_ref.shape[0]
    steps = own_refs[0].shape[0] // rows
    for part, (own_ref, other_ref) in enumerate(zip(own_refs, other_refs)):

        @pl.when(pl.program_id(0) // steps == part)
        def _():
            first = pl.multiple_of(pl.program_id(0) % steps * rows, rows)
            span = pl.ds(first, rows)
            total = own_ref[span, :].astype(jnp.float32) + other_ref[span, :].astype(jnp.float32)
            out_ref[...] = total.astype(jnp.bfloat16)


def add_cores(own, other):
    rows, width = own[0].shape
    parts = len(own)
    tile = min(512, rows)
    return pl.pallas_call(
        lambda *refs: add_kernel(refs[:parts], refs[parts:-1], refs[-1]),
        out_shape=jax.ShapeDtypeStruct((rows * parts, width), jnp.bfloat16),
        grid=(rows * parts // tile,),
        in_specs=[IN_VMEM] * (2 * parts),
        out_specs=pl.BlockSpec((tile, width), lambda t: (t, 0)),
        compiler_params=params(8),
        cost_estimate=cost(rows * parts * width, 6 * rows * parts * width),
        name="add_cores",
    )(*own, *other)


def behind(value, earlier):
    if not earlier:
        return value
    return lax.optimization_barrier((value, *earlier))[0]


def exchange(blocks, members, shards):
    return [
        block
        if offset == 0
        else lax.ppermute(block, "idx", [(i, i ^ offset) for i in range(shards)])
        for block, offset in zip(blocks, members)
    ]


def partner_groups(shards, per):
    half = shards // 2
    quarter = half // 2
    far = [*range(half, shards)]
    near = [*range(quarter, half), *range(1, quarter)]
    near = [near.pop(), 0, *near] if per == 2 else [0, *near]
    far = [tuple(far[i : i + per]) for i in range(0, half, per)]
    near = [tuple(near[i : i + per]) for i in range(0, half, per)]
    return [group for pair in zip(near, far) for group in pair]


def local(queries, positives, passages, negatives):
    shards = lax.axis_size("idx")
    shard_rows, width = passages.shape
    ids = negatives.reshape(1, -1)
    capacity = ids.shape[1] // shards
    scale = 3.0 / math.sqrt(width)
    factor = LSCALE * scale
    groups = partner_groups(shards, max(1, GROUP_SLOTS // capacity))
    place = lax.axis_index("idx").astype(jnp.int32).reshape(1)

    request = build_request(ids, shards, shard_rows)
    wanted = lax.all_to_all(request, "idx", split_axis=0, concat_axis=0, tiled=True)
    pos_logit = scale * jnp.sum(
        queries.astype(jnp.float32) * positives.astype(jnp.float32), axis=1
    )
    pos_logit = pos_logit.reshape(1, -1)

    fetched = []
    for index, group in enumerate(groups):
        earlier = fetched[index - WINDOW][-1:] if index >= WINDOW else [pos_logit]
        picked = pick(behind(place, earlier), wanted, passages, group)
        fetched.append(exchange(picked, group, shards))

    top, total = pos_logit, jnp.ones_like(pos_logit)
    exps, tops = [], []
    for group, rows in zip(groups, fetched):
        value, top, total = group_logits(
            place, request, top, total, queries, rows, group, scale
        )
        exps.append(value)
        tops.append(top)
    loss = top + jnp.log(total) - pos_logit

    order = [1, 0, *range(2, len(groups))]
    weights, grads, last = [None] * len(groups), {}, []
    for index in order:
        weights[index], grads[index] = row_grad(
            exps[index], behind(tops[index], last), top, total, queries, groups[index], factor
        )
        last = grads[index][-1:]

    grad_queries = []
    for part in range(QUERY_PARTS):
        done = query_grad(
            pos_logit,
            top,
            total,
            positives,
            weights,
            fetched,
            factor,
            part,
            grad_queries[-1:],
        )
        grad_queries.append(done)

    sums, returned = [], {}

    def scattered(indices, part=0, parts=1, dtype=jnp.float32, after=()):
        return scatter(
            behind(place, after),
            wanted,
            [one for index in indices for one in returned[index]],
            sum((groups[index] for index in indices), ()),
            sums[-1:],
            shard_rows,
            part,
            parts,
            dtype,
        )

    first_query = len(order) - 1 - QUERY_PARTS
    for step, index in enumerate(order):
        blocks = grads[index]
        if step > WINDOW:
            after = [one for near in order[2:3] for one in returned[near]]
            sums.append(scattered([order[step - WINDOW - 1]], after=after))
            earlier = sums[-1:]
            if first_query <= step < first_query + QUERY_PARTS:
                earlier = earlier + [grad_queries[step - first_query]]
            blocks = [behind(blocks[0], earlier), *blocks[1:]]
        returned[index] = exchange(blocks, groups[index], shards)
    sums.append(scattered(order[-WINDOW - 1 : -1]))
    parts = [
        scattered(order[-1:], part, SUM_PARTS, jnp.bfloat16) for part in range(SUM_PARTS)
    ]
    grad_passages = add_cores(parts, [lax.ppermute(own, "enc", SWAP) for own in parts])
    return (loss.reshape(-1), grad_queries[-1], grad_passages)


def solution(mesh):
    placed = (
        P(("idx", "enc"), None),
        P(("idx", "enc"), None),
        P("idx", None),
        P(("idx", "enc"), None),
    )
    return jax.shard_map(
        local,
        mesh=mesh,
        in_specs=placed,
        out_specs=(P(("idx", "enc")), P(("idx", "enc"), None), P("idx", None)),
        check_vma=False,
    )
```

```python
import functools
import math

import jax
import jax.numpy as jnp
from jax import lax
from jax.experimental import pallas as pl
from jax.experimental.pallas import tpu as pltpu
from jax.sharding import PartitionSpec as P

LSCALE = 32
DEAD = -1e30
LANES = 128
MIB = 1 << 20
GROUP_SLOTS = 256
WINDOW = 4
LIGHT = 0.1
QUERY_TILE = 256
QUERY_PARTS = 2
SUM_PARTS = 4
SWAP = [(0, 1), (1, 0)]


def params(vmem_mib):
    return pltpu.CompilerParams(vmem_limit_bytes=vmem_mib * MIB)


def cost(flops, bytes_accessed, transcendentals=0):
    return pl.CostEstimate(
        flops=int(flops), bytes_accessed=int(bytes_accessed), transcendentals=int(transcendentals)
    )


def whole(shape):
    return pl.BlockSpec(shape, lambda *_: (0,) * len(shape))


SCALAR = pl.BlockSpec(memory_space=pltpu.SMEM)
UNREAD = pl.BlockSpec(memory_space=pl.ANY)
IN_VMEM = pl.BlockSpec(memory_space=pltpu.VMEM)


def request_kernel(shard_rows, ids_ref, out_ref):
    shards, capacity = out_ref.shape
    count = ids_ref.shape[1]
    ids = ids_ref[...]
    base = lax.broadcasted_iota(jnp.int32, (shards, 1), 0) * shard_rows
    row = ids - base
    mine = (row >= 0) & (row < shard_rows)
    one = jnp.where(mine, 1.0, 0.0)
    high = jnp.where(mine, row // 128, 0).astype(jnp.float32)
    low = jnp.where(mine, row % 128, 0).astype(jnp.float32)
    before = (
        lax.broadcasted_iota(jnp.int32, (LANES, LANES), 0)
        < lax.broadcasted_iota(jnp.int32, (LANES, LANES), 1)
    ).astype(jnp.bfloat16)
    carry = jnp.zeros((shards, 1), jnp.float32)
    places = []
    for start in range(0, count, LANES):
        part = one[:, start : start + LANES]
        inside = jnp.dot(part.astype(jnp.bfloat16), before, preferred_element_type=jnp.float32)
        rank = jnp.sum(part * (inside + carry), axis=0, keepdims=True)
        carry = carry + jnp.sum(part, axis=1, keepdims=True)
        slot = lax.broadcasted_iota(jnp.int32, (capacity, LANES), 0).astype(jnp.float32)
        places.append(jnp.where(slot == rank, 1.0, 0.0))
    place = jnp.concatenate(places, axis=1).astype(jnp.bfloat16)
    parts = jnp.concatenate([one, high, low], axis=0).astype(jnp.bfloat16)
    packed = lax.dot_general(
        parts, place, (((1,), (1,)), ((), ())), preferred_element_type=jnp.float32
    )
    filled = packed[:shards] > 0.5
    rows = packed[shards : 2 * shards] * 128.0 + packed[2 * shards :]
    out_ref[...] = jnp.where(filled, rows.astype(jnp.int32), -1)


def build_request(ids, shards, shard_rows):
    count = ids.shape[1]
    capacity = count // shards
    return pl.pallas_call(
        functools.partial(request_kernel, shard_rows),
        out_shape=jax.ShapeDtypeStruct((shards, capacity), jnp.int32),
        compiler_params=params(16),
        cost_estimate=cost(2 * 3 * shards * count * capacity, 16384),
        name="build_request",
    )(ids)


def partner_line(table_ref, me, offset):
    return table_ref[pl.ds(jnp.bitwise_xor(me, offset), 1), :]


def partner_columns(table_ref, me, members):
    return as_columns([partner_line(table_ref, me, o).astype(jnp.float32) for o in members])


def as_columns(lines):
    blocks = []
    for line in lines:
        for start in range(0, line.shape[1], LANES):
            piece = line[:, start : start + LANES]
            blocks.append(jnp.broadcast_to(piece, (LANES, piece.shape[1])).T)
    return jnp.concatenate(blocks, axis=0)


def store_blocks(refs, value):
    size = refs[0].shape[0]
    for index, ref in enumerate(refs):
        ref[...] = value[index * size : (index + 1) * size]


def pick_kernel(members, place_ref, wanted_ref, passages_ref, *out_refs):
    rows = passages_ref.shape[0]
    wanted = partner_columns(wanted_ref, place_ref[0], members)
    lane = lax.broadcasted_iota(jnp.int32, wanted.shape, 1).astype(jnp.float32)
    hot = jnp.concatenate(
        [
            jnp.where(wanted == lane + float(start), 1.0, 0.0).astype(jnp.bfloat16)
            for start in range(0, rows, LANES)
        ],
        axis=1,
    )
    picked = jnp.dot(hot, passages_ref[...], preferred_element_type=jnp.float32)
    store_blocks(out_refs, picked.astype(jnp.bfloat16))


def pick(place, wanted, passages, members):
    rows, width = passages.shape
    slots = len(members) * wanted.shape[1]
    shapes = [jax.ShapeDtypeStruct((wanted.shape[1], width), jnp.bfloat16)] * len(members)
    return pl.pallas_call(
        functools.partial(pick_kernel, members),
        out_shape=shapes,
        in_specs=[SCALAR, IN_VMEM, IN_VMEM],
        out_specs=[IN_VMEM] * len(shapes),
        compiler_params=params(12),
        cost_estimate=cost(
            2 * slots * rows * width * LIGHT,
            2 * (rows + slots) * width * LIGHT,
        ),
        name="pick_rows",
    )(place, wanted, passages)


def logits_kernel(members, scale, place_ref, request_ref, top_ref, total_ref, queries_ref, *refs):
    fetched_refs, (exps_ref, new_top_ref, new_total_ref) = refs[:-3], refs[-3:]
    me = place_ref[0]
    live = partner_columns(request_ref, me, members) >= 0.0
    fetched = jnp.concatenate([ref[...] for ref in fetched_refs], axis=0)
    for first in range(0, queries_ref.shape[0], QUERY_TILE):
        logits = lax.dot_general(
            fetched,
            queries_ref[first : first + QUERY_TILE, :],
            (((1,), (1,)), ((), ())),
            preferred_element_type=jnp.float32,
        )
        for start in range(0, QUERY_TILE, LANES):
            lanes = slice(first + start, first + start + LANES)
            part = jnp.where(live, scale * logits[:, start : start + LANES], DEAD)
            old_top = top_ref[:, lanes]
            top = jnp.maximum(old_top, jnp.max(part, axis=0, keepdims=True))
            exps = jnp.exp(part - top)
            exps_ref[:, lanes] = exps.astype(exps_ref.dtype)
            new_top_ref[:, lanes] = top
            new_total_ref[:, lanes] = total_ref[:, lanes] * jnp.exp(old_top - top) + jnp.sum(
                exps, axis=0, keepdims=True
            )


def group_logits(place, request, top, total, queries, fetched, members, scale):
    width = fetched[0].shape[1]
    slots = sum(rows.shape[0] for rows in fetched)
    count = queries.shape[0]
    shape = jax.ShapeDtypeStruct((1, count), jnp.float32)
    return pl.pallas_call(
        functools.partial(logits_kernel, members, scale),
        out_shape=(jax.ShapeDtypeStruct((slots, count), jnp.bfloat16), shape, shape),
        in_specs=[SCALAR] + [IN_VMEM] * (4 + len(fetched)),
        out_specs=(IN_VMEM,) * 3,
        compiler_params=params(14),
        cost_estimate=cost(
            2 * slots * width * count,
            2 * (slots + count) * width + 4 * slots * count,
            slots * count,
        ),
        name="group_logits",
    )(place, request, top, total, queries, *fetched)


def row_grad_kernel(factor, exps_ref, own_top_ref, top_ref, total_ref, queries_ref, *refs):
    weights_ref, *out_refs = refs
    share = factor * jnp.exp(own_top_ref[...] - top_ref[...]) / total_ref[...]
    weights = (exps_ref[...].astype(jnp.float32) * share).astype(jnp.bfloat16)
    weights_ref[...] = weights
    value = jnp.dot(weights, queries_ref[...], preferred_element_type=jnp.float32)
    store_blocks(out_refs, value.astype(jnp.bfloat16))


def row_grad(exps, own_top, top, total, queries, members, factor):
    slots, count = exps.shape
    width = queries.shape[1]
    block = (slots // len(members), width)
    shapes = [jax.ShapeDtypeStruct(block, jnp.bfloat16)] * len(members)
    weights, *grads = pl.pallas_call(
        functools.partial(row_grad_kernel, factor),
        out_shape=[jax.ShapeDtypeStruct((slots, count), jnp.bfloat16)] + shapes,
        in_specs=[IN_VMEM] * 5,
        out_specs=[IN_VMEM] * (1 + len(shapes)),
        compiler_params=params(14),
        cost_estimate=cost(
            2 * slots * width * count * LIGHT, 2 * slots * (width + count) * LIGHT
        ),
        name="row_grad",
    )(exps, own_top, top, total, queries)
    return weights, grads


def query_kernel(factor, sizes, pos_ref, top_ref, total_ref, positives_ref, *refs):
    weights_refs, rest = refs[: len(sizes)], refs[len(sizes) :]
    grad_ref = refs[-1]
    pos, top, total = pos_ref[...], top_ref[...], total_ref[...]
    coef = as_columns([factor * (jnp.exp(pos - top) / total - 1.0)])
    value = jnp.concatenate(
        [
            coef * positives_ref[:, start : start + LANES].astype(jnp.float32)
            for start in range(0, positives_ref.shape[1], LANES)
        ],
        axis=1,
    )
    first = 0
    for ref, size in zip(weights_refs, sizes):
        rows = jnp.concatenate([one[...] for one in rest[first : first + size]], axis=0)
        first += size
        value = value + lax.dot_general(
            ref[...], rows, (((0,), (0,)), ((), ())), preferred_element_type=jnp.float32
        )
    grad_ref[...] = value.astype(jnp.bfloat16)


def query_grad(pos, top, total, positives, weights, fetched, factor, part, grads):
    count, width = positives.shape
    tile = min(256, count // QUERY_PARTS)
    steps = count // QUERY_PARTS // tile
    first = part * steps
    line = pl.BlockSpec((1, tile), lambda t: (0, first + t))
    block = pl.BlockSpec((tile, width), lambda t: (first + t, 0))
    sizes = [len(group) for group in fetched]
    rows = [one for group in fetched for one in group]
    inputs = [pos, top, total, positives, *weights, *rows, *grads]
    slots = sum(one.shape[0] for one in weights)
    return pl.pallas_call(
        functools.partial(query_kernel, factor, sizes),
        out_shape=jax.ShapeDtypeStruct((count, width), jnp.bfloat16),
        grid=(steps,),
        in_specs=[line, line, line, block]
        + [pl.BlockSpec((one.shape[0], tile), lambda t: (0, first + t)) for one in weights]
        + [whole(one.shape) for one in rows]
        + [UNREAD] * len(grads),
        out_specs=block,
        input_output_aliases={len(inputs) - 1: 0} if grads else {},
        compiler_params=params(26),
        cost_estimate=cost(
            2 * slots * width * count * 0.5 / QUERY_PARTS,
            2 * slots * width + 4 * count * width // QUERY_PARTS,
        ),
        name="query_grad",
    )(*inputs)


def scatter_kernel(members, first, place_ref, wanted_ref, *refs):
    *value_refs, out_ref = refs
    base_ref = value_refs.pop(0) if value_refs[0].shape == out_ref.shape else None
    rows = out_ref.shape[0]
    me = place_ref[0]
    row = (first + pl.program_id(0)) * rows + lax.broadcasted_iota(jnp.int32, (rows, 1), 0)
    wanted = jnp.concatenate(
        [partner_line(wanted_ref, me, o) for o in members], axis=1
    )
    hot = jnp.where(wanted == row, 1.0, 0.0).astype(jnp.bfloat16)
    values = jnp.concatenate([ref[...] for ref in value_refs], axis=0)
    total = jnp.dot(hot, values, preferred_element_type=jnp.float32)
    if base_ref is not None:
        total = base_ref[...] + total
    out_ref[...] = total.astype(out_ref.dtype)


def scatter(place, wanted, values, members, base, shard_rows, part, parts, dtype):
    width = values[0].shape[1]
    slots = sum(one.shape[0] for one in values)
    rows = shard_rows // parts
    tile = 2 * LANES
    first = part * rows // tile
    return pl.pallas_call(
        functools.partial(scatter_kernel, members, first),
        out_shape=jax.ShapeDtypeStruct((rows, width), dtype),
        grid=(rows // tile,),
        in_specs=[SCALAR, whole(wanted.shape)]
        + [pl.BlockSpec((tile, width), lambda t: (first + t, 0))] * len(base)
        + [whole(one.shape) for one in values],
        out_specs=pl.BlockSpec((tile, width), lambda t: (t, 0)),
        compiler_params=params(18),
        cost_estimate=cost(
            2 * rows * slots * width, 2 * slots * width + 4 * (1 + len(base)) * rows * width
        ),
        name="scatter_rows",
    )(place, wanted, *base, *values)


def add_kernel(own_refs, other_refs, out_ref):
    rows = out_ref.shape[0]
    steps = own_refs[0].shape[0] // rows
    for part, (own_ref, other_ref) in enumerate(zip(own_refs, other_refs)):

        @pl.when(pl.program_id(0) // steps == part)
        def _():
            first = pl.multiple_of(pl.program_id(0) % steps * rows, rows)
            span = pl.ds(first, rows)
            total = own_ref[span, :].astype(jnp.float32) + other_ref[span, :].astype(jnp.float32)
            out_ref[...] = total.astype(jnp.bfloat16)


def add_cores(own, other):
    rows, width = own[0].shape
    parts = len(own)
    tile = min(512, rows)
    return pl.pallas_call(
        lambda *refs: add_kernel(refs[:parts], refs[parts:-1], refs[-1]),
        out_shape=jax.ShapeDtypeStruct((rows * parts, width), jnp.bfloat16),
        grid=(rows * parts // tile,),
        in_specs=[IN_VMEM] * (2 * parts),
        out_specs=pl.BlockSpec((tile, width), lambda t: (t, 0)),
        compiler_params=params(8),
        cost_estimate=cost(rows * parts * width, 6 * rows * parts * width),
        name="add_cores",
    )(*own, *other)


def behind(value, earlier):
    if not earlier:
        return value
    return lax.optimization_barrier((value, *earlier))[0]


def exchange(blocks, members, shards):
    return [
        block
        if offset == 0
        else lax.ppermute(block, "idx", [(i, i ^ offset) for i in range(shards)])
        for block, offset in zip(blocks, members)
    ]


def partner_groups(shards, per):
    half = shards // 2
    quarter = half // 2
    far = [half + part * quarter + place for place in range(quarter) for part in range(2)]
    near = [*range(quarter, half), *range(1, quarter)]
    near = [near.pop(), 0, *near] if per == 2 else [0, *near]
    far = [tuple(far[i : i + per]) for i in range(0, half, per)]
    near = [tuple(near[i : i + per]) for i in range(0, half, per)]
    return [group for pair in zip(near, far) for group in pair]


def local(queries, positives, passages, negatives):
    shards = lax.axis_size("idx")
    shard_rows, width = passages.shape
    ids = negatives.reshape(1, -1)
    capacity = ids.shape[1] // shards
    scale = 3.0 / math.sqrt(width)
    factor = LSCALE * scale
    groups = partner_groups(shards, max(1, GROUP_SLOTS // capacity))
    place = lax.axis_index("idx").astype(jnp.int32).reshape(1)

    request = build_request(ids, shards, shard_rows)
    wanted = lax.all_to_all(request, "idx", split_axis=0, concat_axis=0, tiled=True)
    pos_logit = scale * jnp.sum(
        queries.astype(jnp.float32) * positives.astype(jnp.float32), axis=1
    )
    pos_logit = pos_logit.reshape(1, -1)

    fetched = []
    for index, group in enumerate(groups):
        earlier = fetched[index - WINDOW][-1:] if index >= WINDOW else [pos_logit]
        picked = pick(behind(place, earlier), wanted, passages, group)
        fetched.append(exchange(picked, group, shards))

    top, total = pos_logit, jnp.ones_like(pos_logit)
    exps, tops = [], []
    for group, rows in zip(groups, fetched):
        value, top, total = group_logits(
            place, request, top, total, queries, rows, group, scale
        )
        exps.append(value)
        tops.append(top)
    loss = top + jnp.log(total) - pos_logit

    order = [1, 0, *range(2, len(groups))]
    weights, grads, last = [None] * len(groups), {}, []
    for index in order:
        weights[index], grads[index] = row_grad(
            exps[index], behind(tops[index], last), top, total, queries, groups[index], factor
        )
        last = grads[index][-1:]

    grad_queries = []
    for part in range(QUERY_PARTS):
        done = query_grad(
            pos_logit,
            top,
            total,
            positives,
            weights,
            fetched,
            factor,
            part,
            grad_queries[-1:],
        )
        grad_queries.append(done)

    sums, returned = [], {}

    def scattered(indices, part=0, parts=1, dtype=jnp.float32):
        return scatter(
            place,
            wanted,
            [one for index in indices for one in returned[index]],
            sum((groups[index] for index in indices), ()),
            sums[-1:],
            shard_rows,
            part,
            parts,
            dtype,
        )

    first_query = len(order) - 1 - QUERY_PARTS
    for step, index in enumerate(order):
        blocks = grads[index]
        if step >= WINDOW:
            sums.append(scattered([order[step - WINDOW]]))
            earlier = sums[-1:]
            if first_query <= step < first_query + QUERY_PARTS:
                earlier = earlier + [grad_queries[step - first_query]]
            blocks = [behind(blocks[0], earlier), *blocks[1:]]
        returned[index] = exchange(blocks, groups[index], shards)
    sums.append(scattered(order[-WINDOW:-1]))
    parts = [
        scattered(order[-1:], part, SUM_PARTS, jnp.bfloat16) for part in range(SUM_PARTS)
    ]
    grad_passages = add_cores(parts, [lax.ppermute(own, "enc", SWAP) for own in parts])
    return (loss.reshape(-1), grad_queries[-1], grad_passages)


def solution(mesh):
    placed = (
        P(("idx", "enc"), None),
        P(("idx", "enc"), None),
        P("idx", None),
        P(("idx", "enc"), None),
    )
    return jax.shard_map(
        local,
        mesh=mesh,
        in_specs=placed,
        out_specs=(P(("idx", "enc")), P(("idx", "enc"), None), P("idx", None)),
        check_vma=False,
    )
```

```python
import functools
import math

import jax
import jax.numpy as jnp
from jax import lax
from jax.experimental import pallas as pl
from jax.experimental.pallas import tpu as pltpu
from jax.sharding import PartitionSpec as P

LSCALE = 32
DEAD = -1e30
LANES = 128
MIB = 1 << 20
GROUP_SLOTS = 256
WINDOW = 4
LIGHT = 0.1
QUERY_TILE = 256
QUERY_PARTS = 2
SUM_PARTS = 4
SWAP = [(0, 1), (1, 0)]


def params(vmem_mib):
    return pltpu.CompilerParams(vmem_limit_bytes=vmem_mib * MIB)


def cost(flops, bytes_accessed, transcendentals=0):
    return pl.CostEstimate(
        flops=int(flops), bytes_accessed=int(bytes_accessed), transcendentals=int(transcendentals)
    )


def whole(shape):
    return pl.BlockSpec(shape, lambda *_: (0,) * len(shape))


SCALAR = pl.BlockSpec(memory_space=pltpu.SMEM)
UNREAD = pl.BlockSpec(memory_space=pl.ANY)
IN_VMEM = pl.BlockSpec(memory_space=pltpu.VMEM)


def request_kernel(shard_rows, ids_ref, out_ref):
    shards, capacity = out_ref.shape
    count = ids_ref.shape[1]
    ids = ids_ref[...]
    base = lax.broadcasted_iota(jnp.int32, (shards, 1), 0) * shard_rows
    row = ids - base
    mine = (row >= 0) & (row < shard_rows)
    one = jnp.where(mine, 1.0, 0.0)
    high = jnp.where(mine, row // 128, 0).astype(jnp.float32)
    low = jnp.where(mine, row % 128, 0).astype(jnp.float32)
    before = (
        lax.broadcasted_iota(jnp.int32, (LANES, LANES), 0)
        < lax.broadcasted_iota(jnp.int32, (LANES, LANES), 1)
    ).astype(jnp.bfloat16)
    carry = jnp.zeros((shards, 1), jnp.float32)
    places = []
    for start in range(0, count, LANES):
        part = one[:, start : start + LANES]
        inside = jnp.dot(part.astype(jnp.bfloat16), before, preferred_element_type=jnp.float32)
        rank = jnp.sum(part * (inside + carry), axis=0, keepdims=True)
        carry = carry + jnp.sum(part, axis=1, keepdims=True)
        slot = lax.broadcasted_iota(jnp.int32, (capacity, LANES), 0).astype(jnp.float32)
        places.append(jnp.where(slot == rank, 1.0, 0.0))
    place = jnp.concatenate(places, axis=1).astype(jnp.bfloat16)
    parts = jnp.concatenate([one, high, low], axis=0).astype(jnp.bfloat16)
    packed = lax.dot_general(
        parts, place, (((1,), (1,)), ((), ())), preferred_element_type=jnp.float32
    )
    filled = packed[:shards] > 0.5
    rows = packed[shards : 2 * shards] * 128.0 + packed[2 * shards :]
    out_ref[...] = jnp.where(filled, rows.astype(jnp.int32), -1)


def build_request(ids, shards, shard_rows):
    count = ids.shape[1]
    capacity = count // shards
    return pl.pallas_call(
        functools.partial(request_kernel, shard_rows),
        out_shape=jax.ShapeDtypeStruct((shards, capacity), jnp.int32),
        compiler_params=params(16),
        cost_estimate=cost(2 * 3 * shards * count * capacity, 16384),
        name="build_request",
    )(ids)


def partner_line(table_ref, me, offset):
    return table_ref[pl.ds(jnp.bitwise_xor(me, offset), 1), :]


def partner_columns(table_ref, me, members):
    return as_columns([partner_line(table_ref, me, o).astype(jnp.float32) for o in members])


def as_columns(lines):
    blocks = []
    for line in lines:
        for start in range(0, line.shape[1], LANES):
            piece = line[:, start : start + LANES]
            blocks.append(jnp.broadcast_to(piece, (LANES, piece.shape[1])).T)
    return jnp.concatenate(blocks, axis=0)


def store_blocks(refs, value):
    size = refs[0].shape[0]
    for index, ref in enumerate(refs):
        ref[...] = value[index * size : (index + 1) * size]


def pick_kernel(members, place_ref, wanted_ref, passages_ref, *out_refs):
    rows = passages_ref.shape[0]
    wanted = partner_columns(wanted_ref, place_ref[0], members)
    lane = lax.broadcasted_iota(jnp.int32, wanted.shape, 1).astype(jnp.float32)
    hot = jnp.concatenate(
        [
            jnp.where(wanted == lane + float(start), 1.0, 0.0).astype(jnp.bfloat16)
            for start in range(0, rows, LANES)
        ],
        axis=1,
    )
    picked = jnp.dot(hot, passages_ref[...], preferred_element_type=jnp.float32)
    store_blocks(out_refs, picked.astype(jnp.bfloat16))


def pick(place, wanted, passages, members):
    rows, width = passages.shape
    slots = len(members) * wanted.shape[1]
    shapes = [jax.ShapeDtypeStruct((wanted.shape[1], width), jnp.bfloat16)] * len(members)
    return pl.pallas_call(
        functools.partial(pick_kernel, members),
        out_shape=shapes,
        in_specs=[SCALAR, IN_VMEM, IN_VMEM],
        out_specs=[IN_VMEM] * len(shapes),
        compiler_params=params(12),
        cost_estimate=cost(
            2 * slots * rows * width * LIGHT,
            2 * (rows + slots) * width * LIGHT,
        ),
        name="pick_rows",
    )(place, wanted, passages)


def logits_kernel(members, scale, place_ref, request_ref, top_ref, total_ref, queries_ref, *refs):
    fetched_refs, (exps_ref, new_top_ref, new_total_ref) = refs[:-3], refs[-3:]
    me = place_ref[0]
    live = partner_columns(request_ref, me, members) >= 0.0
    fetched = jnp.concatenate([ref[...] for ref in fetched_refs], axis=0)
    for first in range(0, queries_ref.shape[0], QUERY_TILE):
        logits = lax.dot_general(
            fetched,
            queries_ref[first : first + QUERY_TILE, :],
            (((1,), (1,)), ((), ())),
            preferred_element_type=jnp.float32,
        )
        for start in range(0, QUERY_TILE, LANES):
            lanes = slice(first + start, first + start + LANES)
            part = jnp.where(live, scale * logits[:, start : start + LANES], DEAD)
            old_top = top_ref[:, lanes]
            top = jnp.maximum(old_top, jnp.max(part, axis=0, keepdims=True))
            exps = jnp.exp(part - top)
            exps_ref[:, lanes] = exps.astype(exps_ref.dtype)
            new_top_ref[:, lanes] = top
            new_total_ref[:, lanes] = total_ref[:, lanes] * jnp.exp(old_top - top) + jnp.sum(
                exps, axis=0, keepdims=True
            )


def group_logits(place, request, top, total, queries, fetched, members, scale):
    width = fetched[0].shape[1]
    slots = sum(rows.shape[0] for rows in fetched)
    count = queries.shape[0]
    shape = jax.ShapeDtypeStruct((1, count), jnp.float32)
    return pl.pallas_call(
        functools.partial(logits_kernel, members, scale),
        out_shape=(jax.ShapeDtypeStruct((slots, count), jnp.bfloat16), shape, shape),
        in_specs=[SCALAR] + [IN_VMEM] * (4 + len(fetched)),
        out_specs=(IN_VMEM,) * 3,
        compiler_params=params(14),
        cost_estimate=cost(
            2 * slots * width * count,
            2 * (slots + count) * width + 4 * slots * count,
            slots * count,
        ),
        name="group_logits",
    )(place, request, top, total, queries, *fetched)


def row_grad_kernel(factor, exps_ref, own_top_ref, top_ref, total_ref, queries_ref, *refs):
    weights_ref, *out_refs = refs
    share = factor * jnp.exp(own_top_ref[...] - top_ref[...]) / total_ref[...]
    weights = (exps_ref[...].astype(jnp.float32) * share).astype(jnp.bfloat16)
    weights_ref[...] = weights
    value = jnp.dot(weights, queries_ref[...], preferred_element_type=jnp.float32)
    store_blocks(out_refs, value.astype(jnp.bfloat16))


def row_grad(exps, own_top, top, total, queries, members, factor):
    slots, count = exps.shape
    width = queries.shape[1]
    block = (slots // len(members), width)
    shapes = [jax.ShapeDtypeStruct(block, jnp.bfloat16)] * len(members)
    weights, *grads = pl.pallas_call(
        functools.partial(row_grad_kernel, factor),
        out_shape=[jax.ShapeDtypeStruct((slots, count), jnp.bfloat16)] + shapes,
        in_specs=[IN_VMEM] * 5,
        out_specs=[IN_VMEM] * (1 + len(shapes)),
        compiler_params=params(14),
        cost_estimate=cost(
            2 * slots * width * count * LIGHT, 2 * slots * (width + count) * LIGHT
        ),
        name="row_grad",
    )(exps, own_top, top, total, queries)
    return weights, grads


def query_kernel(factor, sizes, pos_ref, top_ref, total_ref, positives_ref, *refs):
    weights_refs, rest = refs[: len(sizes)], refs[len(sizes) :]
    grad_ref = refs[-1]
    pos, top, total = pos_ref[...], top_ref[...], total_ref[...]
    coef = as_columns([factor * (jnp.exp(pos - top) / total - 1.0)])
    value = jnp.concatenate(
        [
            coef * positives_ref[:, start : start + LANES].astype(jnp.float32)
            for start in range(0, positives_ref.shape[1], LANES)
        ],
        axis=1,
    )
    first = 0
    for ref, size in zip(weights_refs, sizes):
        rows = jnp.concatenate([one[...] for one in rest[first : first + size]], axis=0)
        first += size
        value = value + lax.dot_general(
            ref[...], rows, (((0,), (0,)), ((), ())), preferred_element_type=jnp.float32
        )
    grad_ref[...] = value.astype(jnp.bfloat16)


def query_grad(pos, top, total, positives, weights, fetched, factor, part, grads):
    count, width = positives.shape
    tile = min(256, count // QUERY_PARTS)
    steps = count // QUERY_PARTS // tile
    first = part * steps
    line = pl.BlockSpec((1, tile), lambda t: (0, first + t))
    block = pl.BlockSpec((tile, width), lambda t: (first + t, 0))
    sizes = [len(group) for group in fetched]
    rows = [one for group in fetched for one in group]
    inputs = [pos, top, total, positives, *weights, *rows, *grads]
    slots = sum(one.shape[0] for one in weights)
    return pl.pallas_call(
        functools.partial(query_kernel, factor, sizes),
        out_shape=jax.ShapeDtypeStruct((count, width), jnp.bfloat16),
        grid=(steps,),
        in_specs=[line, line, line, block]
        + [pl.BlockSpec((one.shape[0], tile), lambda t: (0, first + t)) for one in weights]
        + [whole(one.shape) for one in rows]
        + [UNREAD] * len(grads),
        out_specs=block,
        input_output_aliases={len(inputs) - 1: 0} if grads else {},
        compiler_params=params(26),
        cost_estimate=cost(
            2 * slots * width * count * 0.5 / QUERY_PARTS,
            2 * slots * width + 4 * count * width // QUERY_PARTS,
        ),
        name="query_grad",
    )(*inputs)


def scatter_kernel(members, first, place_ref, wanted_ref, *refs):
    *value_refs, out_ref = refs
    base_ref = value_refs.pop(0) if value_refs[0].shape == out_ref.shape else None
    rows = out_ref.shape[0]
    me = place_ref[0]
    row = (first + pl.program_id(0)) * rows + lax.broadcasted_iota(jnp.int32, (rows, 1), 0)
    wanted = jnp.concatenate(
        [partner_line(wanted_ref, me, o) for o in members], axis=1
    )
    hot = jnp.where(wanted == row, 1.0, 0.0).astype(jnp.bfloat16)
    values = jnp.concatenate([ref[...] for ref in value_refs], axis=0)
    total = jnp.dot(hot, values, preferred_element_type=jnp.float32)
    if base_ref is not None:
        total = base_ref[...] + total
    out_ref[...] = total.astype(out_ref.dtype)


def scatter(place, wanted, values, members, base, shard_rows, part, parts, dtype):
    width = values[0].shape[1]
    slots = sum(one.shape[0] for one in values)
    rows = shard_rows // parts
    tile = 2 * LANES
    first = part * rows // tile
    return pl.pallas_call(
        functools.partial(scatter_kernel, members, first),
        out_shape=jax.ShapeDtypeStruct((rows, width), dtype),
        grid=(rows // tile,),
        in_specs=[SCALAR, whole(wanted.shape)]
        + [pl.BlockSpec((tile, width), lambda t: (first + t, 0))] * len(base)
        + [whole(one.shape) for one in values],
        out_specs=pl.BlockSpec((tile, width), lambda t: (t, 0)),
        compiler_params=params(18),
        cost_estimate=cost(
            2 * rows * slots * width, 2 * slots * width + 4 * (1 + len(base)) * rows * width
        ),
        name="scatter_rows",
    )(place, wanted, *base, *values)


def add_kernel(own_refs, other_refs, out_ref):
    rows = out_ref.shape[0]
    steps = own_refs[0].shape[0] // rows
    for part, (own_ref, other_ref) in enumerate(zip(own_refs, other_refs)):

        @pl.when(pl.program_id(0) // steps == part)
        def _():
            first = pl.multiple_of(pl.program_id(0) % steps * rows, rows)
            span = pl.ds(first, rows)
            total = own_ref[span, :].astype(jnp.float32) + other_ref[span, :].astype(jnp.float32)
            out_ref[...] = total.astype(jnp.bfloat16)


def add_cores(own, other):
    rows, width = own[0].shape
    parts = len(own)
    tile = min(512, rows)
    return pl.pallas_call(
        lambda *refs: add_kernel(refs[:parts], refs[parts:-1], refs[-1]),
        out_shape=jax.ShapeDtypeStruct((rows * parts, width), jnp.bfloat16),
        grid=(rows * parts // tile,),
        in_specs=[IN_VMEM] * (2 * parts),
        out_specs=pl.BlockSpec((tile, width), lambda t: (t, 0)),
        compiler_params=params(8),
        cost_estimate=cost(rows * parts * width, 6 * rows * parts * width),
        name="add_cores",
    )(*own, *other)


def behind(value, earlier):
    if not earlier:
        return value
    return lax.optimization_barrier((value, *earlier))[0]


def exchange(blocks, members, shards):
    return [
        block
        if offset == 0
        else lax.ppermute(block, "idx", [(i, i ^ offset) for i in range(shards)])
        for block, offset in zip(blocks, members)
    ]


def partner_groups(shards, per):
    half = shards // 2
    quarter = half // 2
    far = [half + part * quarter + place for place in range(quarter) for part in range(2)]
    near = [*range(quarter, half), *range(1, quarter)]
    near = [near.pop(), 0, *near] if per == 2 else [0, *near]
    far = [tuple(far[i : i + per]) for i in range(0, half, per)]
    near = [tuple(near[i : i + per]) for i in range(0, half, per)]
    return [group for pair in zip(near, far) for group in pair]


def local(queries, positives, passages, negatives):
    shards = lax.axis_size("idx")
    shard_rows, width = passages.shape
    ids = negatives.reshape(1, -1)
    capacity = ids.shape[1] // shards
    scale = 3.0 / math.sqrt(width)
    factor = LSCALE * scale
    groups = partner_groups(shards, max(1, GROUP_SLOTS // capacity))
    place = lax.axis_index("idx").astype(jnp.int32).reshape(1)

    request = build_request(ids, shards, shard_rows)
    wanted = lax.all_to_all(request, "idx", split_axis=0, concat_axis=0, tiled=True)
    pos_logit = scale * jnp.sum(
        queries.astype(jnp.float32) * positives.astype(jnp.float32), axis=1
    )
    pos_logit = pos_logit.reshape(1, -1)

    fetched = []
    for index, group in enumerate(groups):
        earlier = fetched[index - WINDOW][-1:] if index >= WINDOW else [pos_logit]
        picked = pick(behind(place, earlier), wanted, passages, group)
        fetched.append(exchange(picked, group, shards))

    top, total = pos_logit, jnp.ones_like(pos_logit)
    exps, tops = [], []
    for group, rows in zip(groups, fetched):
        value, top, total = group_logits(
            place, request, top, total, queries, rows, group, scale
        )
        exps.append(value)
        tops.append(top)
    loss = top + jnp.log(total) - pos_logit

    order = [1, 0, *range(2, len(groups) - 2), len(groups) - 1, len(groups) - 2]
    weights, grads, last = [None] * len(groups), {}, []
    for index in order:
        weights[index], grads[index] = row_grad(
            exps[index], behind(tops[index], last), top, total, queries, groups[index], factor
        )
        last = grads[index][-1:]

    grad_queries = []
    for part in range(QUERY_PARTS):
        done = query_grad(
            pos_logit,
            top,
            total,
            positives,
            weights,
            fetched,
            factor,
            part,
            grad_queries[-1:],
        )
        grad_queries.append(done)

    sums, returned = [], {}

    def scattered(indices, part=0, parts=1, dtype=jnp.float32):
        return scatter(
            place,
            wanted,
            [one for index in indices for one in returned[index]],
            sum((groups[index] for index in indices), ()),
            sums[-1:],
            shard_rows,
            part,
            parts,
            dtype,
        )

    first_query = len(order) - 1 - QUERY_PARTS
    for step, index in enumerate(order):
        blocks = grads[index]
        if step >= WINDOW:
            sums.append(scattered([order[step - WINDOW]]))
            earlier = sums[-1:]
            if first_query <= step < first_query + QUERY_PARTS:
                earlier = earlier + [grad_queries[step - first_query]]
            blocks = [behind(blocks[0], earlier), *blocks[1:]]
        returned[index] = exchange(blocks, groups[index], shards)
    sums.append(scattered(order[-WINDOW:-1]))
    parts = [
        scattered(order[-1:], part, SUM_PARTS, jnp.bfloat16) for part in range(SUM_PARTS)
    ]
    grad_passages = add_cores(parts, [lax.ppermute(own, "enc", SWAP) for own in parts])
    return (loss.reshape(-1), grad_queries[-1], grad_passages)


def solution(mesh):
    placed = (
        P(("idx", "enc"), None),
        P(("idx", "enc"), None),
        P("idx", None),
        P(("idx", "enc"), None),
    )
    return jax.shard_map(
        local,
        mesh=mesh,
        in_specs=placed,
        out_specs=(P(("idx", "enc")), P(("idx", "enc"), None), P("idx", None)),
        check_vma=False,
    )
```

```python
import functools
import math

import jax
import jax.numpy as jnp
from jax import lax
from jax.experimental import pallas as pl
from jax.experimental.pallas import tpu as pltpu
from jax.sharding import PartitionSpec as P

LSCALE = 32
DEAD = -1e30
LANES = 128
MIB = 1 << 20
GROUP_SLOTS = 256
WINDOW = 4
LIGHT = 0.1
QUERY_TILE = 256
QUERY_PARTS = 2
SUM_PARTS = 4
SWAP = [(0, 1), (1, 0)]


def params(vmem_mib):
    return pltpu.CompilerParams(vmem_limit_bytes=vmem_mib * MIB)


def cost(flops, bytes_accessed, transcendentals=0):
    return pl.CostEstimate(
        flops=int(flops), bytes_accessed=int(bytes_accessed), transcendentals=int(transcendentals)
    )


def whole(shape):
    return pl.BlockSpec(shape, lambda *_: (0,) * len(shape))


SCALAR = pl.BlockSpec(memory_space=pltpu.SMEM)
UNREAD = pl.BlockSpec(memory_space=pl.ANY)
IN_VMEM = pl.BlockSpec(memory_space=pltpu.VMEM)


def request_kernel(shard_rows, ids_ref, out_ref):
    shards, capacity = out_ref.shape
    count = ids_ref.shape[1]
    ids = ids_ref[...]
    base = lax.broadcasted_iota(jnp.int32, (shards, 1), 0) * shard_rows
    row = ids - base
    mine = (row >= 0) & (row < shard_rows)
    one = jnp.where(mine, 1.0, 0.0)
    high = jnp.where(mine, row // 128, 0).astype(jnp.float32)
    low = jnp.where(mine, row % 128, 0).astype(jnp.float32)
    before = (
        lax.broadcasted_iota(jnp.int32, (LANES, LANES), 0)
        < lax.broadcasted_iota(jnp.int32, (LANES, LANES), 1)
    ).astype(jnp.bfloat16)
    carry = jnp.zeros((shards, 1), jnp.float32)
    places = []
    for start in range(0, count, LANES):
        part = one[:, start : start + LANES]
        inside = jnp.dot(part.astype(jnp.bfloat16), before, preferred_element_type=jnp.float32)
        rank = jnp.sum(part * (inside + carry), axis=0, keepdims=True)
        carry = carry + jnp.sum(part, axis=1, keepdims=True)
        slot = lax.broadcasted_iota(jnp.int32, (capacity, LANES), 0).astype(jnp.float32)
        places.append(jnp.where(slot == rank, 1.0, 0.0))
    place = jnp.concatenate(places, axis=1).astype(jnp.bfloat16)
    parts = jnp.concatenate([one, high, low], axis=0).astype(jnp.bfloat16)
    packed = lax.dot_general(
        parts, place, (((1,), (1,)), ((), ())), preferred_element_type=jnp.float32
    )
    filled = packed[:shards] > 0.5
    rows = packed[shards : 2 * shards] * 128.0 + packed[2 * shards :]
    out_ref[...] = jnp.where(filled, rows.astype(jnp.int32), -1)


def build_request(ids, shards, shard_rows):
    count = ids.shape[1]
    capacity = count // shards
    return pl.pallas_call(
        functools.partial(request_kernel, shard_rows),
        out_shape=jax.ShapeDtypeStruct((shards, capacity), jnp.int32),
        compiler_params=params(16),
        cost_estimate=cost(2 * 3 * shards * count * capacity, 16384),
        name="build_request",
    )(ids)


def partner_line(table_ref, me, offset):
    return table_ref[pl.ds(jnp.bitwise_xor(me, offset), 1), :]


def partner_columns(table_ref, me, members):
    return as_columns([partner_line(table_ref, me, o).astype(jnp.float32) for o in members])


def as_columns(lines):
    blocks = []
    for line in lines:
        for start in range(0, line.shape[1], LANES):
            piece = line[:, start : start + LANES]
            blocks.append(jnp.broadcast_to(piece, (LANES, piece.shape[1])).T)
    return jnp.concatenate(blocks, axis=0)


def store_blocks(refs, value):
    size = refs[0].shape[0]
    for index, ref in enumerate(refs):
        ref[...] = value[index * size : (index + 1) * size]


def pick_kernel(members, place_ref, wanted_ref, passages_ref, *out_refs):
    rows = passages_ref.shape[0]
    wanted = partner_columns(wanted_ref, place_ref[0], members)
    lane = lax.broadcasted_iota(jnp.int32, wanted.shape, 1).astype(jnp.float32)
    hot = jnp.concatenate(
        [
            jnp.where(wanted == lane + float(start), 1.0, 0.0).astype(jnp.bfloat16)
            for start in range(0, rows, LANES)
        ],
        axis=1,
    )
    picked = jnp.dot(hot, passages_ref[...], preferred_element_type=jnp.float32)
    store_blocks(out_refs, picked.astype(jnp.bfloat16))


def pick(place, wanted, passages, members):
    rows, width = passages.shape
    slots = len(members) * wanted.shape[1]
    shapes = [jax.ShapeDtypeStruct((wanted.shape[1], width), jnp.bfloat16)] * len(members)
    return pl.pallas_call(
        functools.partial(pick_kernel, members),
        out_shape=shapes,
        in_specs=[SCALAR, IN_VMEM, IN_VMEM],
        out_specs=[IN_VMEM] * len(shapes),
        compiler_params=params(12),
        cost_estimate=cost(
            2 * slots * rows * width * LIGHT,
            2 * (rows + slots) * width * LIGHT,
        ),
        name="pick_rows",
    )(place, wanted, passages)


def logits_kernel(members, scale, place_ref, request_ref, top_ref, total_ref, queries_ref, *refs):
    fetched_refs, (exps_ref, new_top_ref, new_total_ref) = refs[:-3], refs[-3:]
    me = place_ref[0]
    live = partner_columns(request_ref, me, members) >= 0.0
    fetched = jnp.concatenate([ref[...] for ref in fetched_refs], axis=0)
    for first in range(0, queries_ref.shape[0], QUERY_TILE):
        logits = lax.dot_general(
            fetched,
            queries_ref[first : first + QUERY_TILE, :],
            (((1,), (1,)), ((), ())),
            preferred_element_type=jnp.float32,
        )
        for start in range(0, QUERY_TILE, LANES):
            lanes = slice(first + start, first + start + LANES)
            part = jnp.where(live, scale * logits[:, start : start + LANES], DEAD)
            old_top = top_ref[:, lanes]
            top = jnp.maximum(old_top, jnp.max(part, axis=0, keepdims=True))
            exps = jnp.exp(part - top)
            exps_ref[:, lanes] = exps.astype(exps_ref.dtype)
            new_top_ref[:, lanes] = top
            new_total_ref[:, lanes] = total_ref[:, lanes] * jnp.exp(old_top - top) + jnp.sum(
                exps, axis=0, keepdims=True
            )


def group_logits(place, request, top, total, queries, fetched, members, scale):
    width = fetched[0].shape[1]
    slots = sum(rows.shape[0] for rows in fetched)
    count = queries.shape[0]
    shape = jax.ShapeDtypeStruct((1, count), jnp.float32)
    return pl.pallas_call(
        functools.partial(logits_kernel, members, scale),
        out_shape=(jax.ShapeDtypeStruct((slots, count), jnp.bfloat16), shape, shape),
        in_specs=[SCALAR] + [IN_VMEM] * (4 + len(fetched)),
        out_specs=(IN_VMEM,) * 3,
        compiler_params=params(14),
        cost_estimate=cost(
            slots * width * count,
            (slots + count) * width + 2 * slots * count,
            slots * count,
        ),
        name="group_logits",
    )(place, request, top, total, queries, *fetched)


def row_grad_kernel(factor, exps_ref, own_top_ref, top_ref, total_ref, queries_ref, *refs):
    weights_ref, *out_refs = refs
    share = factor * jnp.exp(own_top_ref[...] - top_ref[...]) / total_ref[...]
    weights = (exps_ref[...].astype(jnp.float32) * share).astype(jnp.bfloat16)
    weights_ref[...] = weights
    value = jnp.dot(weights, queries_ref[...], preferred_element_type=jnp.float32)
    store_blocks(out_refs, value.astype(jnp.bfloat16))


def row_grad(exps, own_top, top, total, queries, members, factor):
    slots, count = exps.shape
    width = queries.shape[1]
    block = (slots // len(members), width)
    shapes = [jax.ShapeDtypeStruct(block, jnp.bfloat16)] * len(members)
    weights, *grads = pl.pallas_call(
        functools.partial(row_grad_kernel, factor),
        out_shape=[jax.ShapeDtypeStruct((slots, count), jnp.bfloat16)] + shapes,
        in_specs=[IN_VMEM] * 5,
        out_specs=[IN_VMEM] * (1 + len(shapes)),
        compiler_params=params(14),
        cost_estimate=cost(
            2 * slots * width * count * LIGHT, 2 * slots * (width + count) * LIGHT
        ),
        name="row_grad",
    )(exps, own_top, top, total, queries)
    return weights, grads


def query_kernel(factor, sizes, pos_ref, top_ref, total_ref, positives_ref, *refs):
    weights_refs, rest = refs[: len(sizes)], refs[len(sizes) :]
    grad_ref = refs[-1]
    pos, top, total = pos_ref[...], top_ref[...], total_ref[...]
    coef = as_columns([factor * (jnp.exp(pos - top) / total - 1.0)])
    value = jnp.concatenate(
        [
            coef * positives_ref[:, start : start + LANES].astype(jnp.float32)
            for start in range(0, positives_ref.shape[1], LANES)
        ],
        axis=1,
    )
    first = 0
    for ref, size in zip(weights_refs, sizes):
        rows = jnp.concatenate([one[...] for one in rest[first : first + size]], axis=0)
        first += size
        value = value + lax.dot_general(
            ref[...], rows, (((0,), (0,)), ((), ())), preferred_element_type=jnp.float32
        )
    grad_ref[...] = value.astype(jnp.bfloat16)


def query_grad(pos, top, total, positives, weights, fetched, factor, part, grads):
    count, width = positives.shape
    tile = min(256, count // QUERY_PARTS)
    steps = count // QUERY_PARTS // tile
    first = part * steps
    line = pl.BlockSpec((1, tile), lambda t: (0, first + t))
    block = pl.BlockSpec((tile, width), lambda t: (first + t, 0))
    sizes = [len(group) for group in fetched]
    rows = [one for group in fetched for one in group]
    inputs = [pos, top, total, positives, *weights, *rows, *grads]
    slots = sum(one.shape[0] for one in weights)
    return pl.pallas_call(
        functools.partial(query_kernel, factor, sizes),
        out_shape=jax.ShapeDtypeStruct((count, width), jnp.bfloat16),
        grid=(steps,),
        in_specs=[line, line, line, block]
        + [pl.BlockSpec((one.shape[0], tile), lambda t: (0, first + t)) for one in weights]
        + [whole(one.shape) for one in rows]
        + [UNREAD] * len(grads),
        out_specs=block,
        input_output_aliases={len(inputs) - 1: 0} if grads else {},
        compiler_params=params(26),
        cost_estimate=cost(
            2 * slots * width * count * 0.5 / QUERY_PARTS,
            2 * slots * width + 4 * count * width // QUERY_PARTS,
        ),
        name="query_grad",
    )(*inputs)


def scatter_kernel(members, first, place_ref, wanted_ref, *refs):
    *value_refs, out_ref = refs
    base_ref = value_refs.pop(0) if value_refs[0].shape == out_ref.shape else None
    rows = out_ref.shape[0]
    me = place_ref[0]
    row = (first + pl.program_id(0)) * rows + lax.broadcasted_iota(jnp.int32, (rows, 1), 0)
    wanted = jnp.concatenate(
        [partner_line(wanted_ref, me, o) for o in members], axis=1
    )
    hot = jnp.where(wanted == row, 1.0, 0.0).astype(jnp.bfloat16)
    values = jnp.concatenate([ref[...] for ref in value_refs], axis=0)
    total = jnp.dot(hot, values, preferred_element_type=jnp.float32)
    if base_ref is not None:
        total = base_ref[...] + total
    out_ref[...] = total.astype(out_ref.dtype)


def scatter(place, wanted, values, members, base, shard_rows, part, parts, dtype):
    width = values[0].shape[1]
    slots = sum(one.shape[0] for one in values)
    rows = shard_rows // parts
    tile = 2 * LANES
    first = part * rows // tile
    return pl.pallas_call(
        functools.partial(scatter_kernel, members, first),
        out_shape=jax.ShapeDtypeStruct((rows, width), dtype),
        grid=(rows // tile,),
        in_specs=[SCALAR, whole(wanted.shape)]
        + [pl.BlockSpec((tile, width), lambda t: (first + t, 0))] * len(base)
        + [whole(one.shape) for one in values],
        out_specs=pl.BlockSpec((tile, width), lambda t: (t, 0)),
        compiler_params=params(18),
        cost_estimate=cost(
            2 * rows * slots * width, 2 * slots * width + 4 * (1 + len(base)) * rows * width
        ),
        name="scatter_rows",
    )(place, wanted, *base, *values)


def add_kernel(own_refs, other_refs, out_ref):
    rows = out_ref.shape[0]
    steps = own_refs[0].shape[0] // rows
    for part, (own_ref, other_ref) in enumerate(zip(own_refs, other_refs)):

        @pl.when(pl.program_id(0) // steps == part)
        def _():
            first = pl.multiple_of(pl.program_id(0) % steps * rows, rows)
            span = pl.ds(first, rows)
            total = own_ref[span, :].astype(jnp.float32) + other_ref[span, :].astype(jnp.float32)
            out_ref[...] = total.astype(jnp.bfloat16)


def add_cores(own, other):
    rows, width = own[0].shape
    parts = len(own)
    tile = min(512, rows)
    return pl.pallas_call(
        lambda *refs: add_kernel(refs[:parts], refs[parts:-1], refs[-1]),
        out_shape=jax.ShapeDtypeStruct((rows * parts, width), jnp.bfloat16),
        grid=(rows * parts // tile,),
        in_specs=[IN_VMEM] * (2 * parts),
        out_specs=pl.BlockSpec((tile, width), lambda t: (t, 0)),
        compiler_params=params(8),
        cost_estimate=cost(rows * parts * width, 6 * rows * parts * width),
        name="add_cores",
    )(*own, *other)


def behind(value, earlier):
    if not earlier:
        return value
    return lax.optimization_barrier((value, *earlier))[0]


def exchange(blocks, members, shards):
    return [
        block
        if offset == 0
        else lax.ppermute(block, "idx", [(i, i ^ offset) for i in range(shards)])
        for block, offset in zip(blocks, members)
    ]


def partner_groups(shards, per):
    half = shards // 2
    quarter = half // 2
    far = [half + part * quarter + place for place in range(quarter) for part in range(2)]
    near = [*range(quarter, half), *range(1, quarter)]
    near = [near.pop(), 0, *near] if per == 2 else [0, *near]
    far = [tuple(far[i : i + per]) for i in range(0, half, per)]
    near = [tuple(near[i : i + per]) for i in range(0, half, per)]
    return [group for pair in zip(near, far) for group in pair]


def local(queries, positives, passages, negatives):
    shards = lax.axis_size("idx")
    shard_rows, width = passages.shape
    ids = negatives.reshape(1, -1)
    capacity = ids.shape[1] // shards
    scale = 3.0 / math.sqrt(width)
    factor = LSCALE * scale
    groups = partner_groups(shards, max(1, GROUP_SLOTS // capacity))
    place = lax.axis_index("idx").astype(jnp.int32).reshape(1)

    request = build_request(ids, shards, shard_rows)
    wanted = lax.all_to_all(request, "idx", split_axis=0, concat_axis=0, tiled=True)
    pos_logit = scale * jnp.sum(
        queries.astype(jnp.float32) * positives.astype(jnp.float32), axis=1
    )
    pos_logit = pos_logit.reshape(1, -1)

    fetched = []
    for index, group in enumerate(groups):
        earlier = fetched[index - WINDOW][-1:] if index >= WINDOW else [pos_logit]
        picked = pick(behind(place, earlier), wanted, passages, group)
        fetched.append(exchange(picked, group, shards))

    top, total = pos_logit, jnp.ones_like(pos_logit)
    exps, tops = [], []
    for group, rows in zip(groups, fetched):
        value, top, total = group_logits(
            place, request, top, total, queries, rows, group, scale
        )
        exps.append(value)
        tops.append(top)
    loss = top + jnp.log(total) - pos_logit

    order = [1, 0, *range(2, len(groups))]
    weights, grads, last = [None] * len(groups), {}, []
    for index in order:
        weights[index], grads[index] = row_grad(
            exps[index], behind(tops[index], last), top, total, queries, groups[index], factor
        )
        last = grads[index][-1:]

    grad_queries = []
    for part in range(QUERY_PARTS):
        done = query_grad(
            pos_logit,
            top,
            total,
            positives,
            weights,
            fetched,
            factor,
            part,
            grad_queries[-1:],
        )
        grad_queries.append(done)

    sums, returned = [], {}

    def scattered(indices, part=0, parts=1, dtype=jnp.float32):
        return scatter(
            place,
            wanted,
            [one for index in indices for one in returned[index]],
            sum((groups[index] for index in indices), ()),
            sums[-1:],
            shard_rows,
            part,
            parts,
            dtype,
        )

    first_query = len(order) - 1 - QUERY_PARTS
    for step, index in enumerate(order):
        blocks = grads[index]
        if step >= WINDOW:
            sums.append(scattered([order[step - WINDOW]]))
            earlier = sums[-1:]
            if first_query <= step < first_query + QUERY_PARTS:
                earlier = earlier + [grad_queries[step - first_query]]
            blocks = [behind(blocks[0], earlier), *blocks[1:]]
        returned[index] = exchange(blocks, groups[index], shards)
    sums.append(scattered(order[-WINDOW:-1]))
    parts = [
        scattered(order[-1:], part, SUM_PARTS, jnp.bfloat16) for part in range(SUM_PARTS)
    ]
    grad_passages = add_cores(parts, [lax.ppermute(own, "enc", SWAP) for own in parts])
    return (loss.reshape(-1), grad_queries[-1], grad_passages)


def solution(mesh):
    placed = (
        P(("idx", "enc"), None),
        P(("idx", "enc"), None),
        P("idx", None),
        P(("idx", "enc"), None),
    )
    return jax.shard_map(
        local,
        mesh=mesh,
        in_specs=placed,
        out_specs=(P(("idx", "enc")), P(("idx", "enc"), None), P("idx", None)),
        check_vma=False,
    )
```
